256 devices in a mesh: ctx: 32 (over y, z_lo, core), mp: 8 (over x, z_hi).
Axes of the slice: x: 4, y: 4, z: 8 (z_hi: 2, z_lo: 4; z = z_hi * 4 + z_lo), core: 2. Of those that a mesh axis runs over, the one named last changes fastest.
Arguments:
- query_mr: bfloat16 [8192, 4096], P('ctx', 'mp'), may hold values from -6 to 6
- key_mr: bfloat16 [8192, 4096], P('ctx', 'mp'), may hold values from -6 to 6
- value_mr: bfloat16 [8192, 4096], P('ctx', 'mp'), may hold values from -6 to 6
- featurizer_mr: float32 [3, 3, 4096], P(None, None, 'mp'), may hold values from -3 to 3
- mr_taps: float32 [128, 256], P(None, 'mp'), may hold values from -0.5 to 0.5
- out_mr: bfloat16 [4096, 4096], P('mp'), may hold values from -0.09375 to 0.09375
- residual: bfloat16 [8192, 4096], P('ctx', 'mp'), may hold values from -6 to 6
- in_weight: bfloat16 [3, 4096, 4096], P(None, 'mp', 'ctx'), may hold values from -0.09375 to 0.09375
- featurizer_li: float32 [3, 3, 4096], P(None, None, 'mp'), may hold values from -3 to 3
- li_rates: float32 [256, 16], P('mp'), may hold values from 0.0001 to 0.1
- li_residues: float32 [256, 16], P('mp'), may hold values from -0.06 to 0.06
- out_li: bfloat16 [4096, 4096], P('mp'), may hold values from -0.09375 to 0.09375
Outputs:
- block_output: bfloat16 [8192, 4096], P('ctx', 'mp')
The draws below stay inside these ranges and needn't reach their ends.
All inputs are finite; a program needn't handle non-finite values.
Results may differ from the reference program's by a relative error of at most 0.03.
Values may be sent and summed in bfloat16 or wider, within the bound.
No kernel may reach another device: no remote copies, remote signals or barrier semaphores. Data moves between devices by JAX's collectives and lax.ppermute only.
A program may use at most 128 MiB of HBM per device.

```python
import math
import jax
import jax.numpy as jnp
from jax import lax

D = 4096
GS = 16
FEAT = 3
MRK = 128
NM = 16
G = 256
LENGTH = 8192
N_MP = 8


def levels(rng, dims, pieces, low, largest):
    level, own = 1.0, jax.random.fold_in(rng, 6)
    for position, shards_of in pieces:
        heights = jnp.exp(jax.random.uniform(jax.random.fold_in(own, position), (shards_of,), jnp.float32, low / len(pieces), largest / len(pieces)))
        level = level * jnp.repeat(heights, dims[position] // shards_of).reshape([-1 if axis == position else 1 for axis in range(len(dims))])
    return level


def centred(own_key, extent, deviation, most, pieces=(), kind=jnp.bfloat16):
    entries = jax.random.normal(own_key, extent, jnp.float32) * deviation
    if len(pieces) > 0:
        entries = levels(own_key, extent, pieces, -0.22, 0.18) * entries
    return jnp.clip(entries, min=-most, max=most).astype(kind)


def setup_inputs(seed: int = 0) -> dict:
    keys = jax.random.split(jax.random.key(seed), 13)
    return {
        "query_mr": centred(keys[0], (LENGTH, D), 1.0, 6.0, ((0, 32), (1, 8))),
        "key_mr": centred(keys[1], (LENGTH, D), 1.0, 6.0, ((0, 32), (1, 8))),
        "value_mr": centred(keys[2], (LENGTH, D), 1.0, 6.0, ((0, 32), (1, 8))),
        "featurizer_mr": centred(keys[3], (3, FEAT, D), 0.4, 3.0, ((2, 8),), jnp.float32),
        "mr_taps": centred(keys[4], (MRK, G), MRK ** -0.5, 0.5, ((1, 8),), jnp.float32),
        "out_mr": centred(keys[5], (D, D), D ** -0.5, 0.09375, ((0, 8),)),
        "residual": centred(keys[6], (LENGTH, D), 1.0, 6.0, ((0, 32), (1, 8))),
        "in_weight": centred(keys[7], (3, D, D), D ** -0.5, 0.09375, ((1, 8), (2, 32))),
        "featurizer_li": centred(keys[8], (3, FEAT, D), 0.4, 3.0, ((2, 8),), jnp.float32),
        "li_rates": jnp.clip(jnp.exp(math.log(0.1) - 6.9077553 * jax.random.uniform(keys[9], (G, NM), jnp.float32) ** levels(keys[9], (G, NM), ((0, 8),), -0.2, 0.2)), 0.0001, 0.1),
        "li_residues": centred(keys[10], (G, NM), 0.01, 0.06, ((0, 8),), jnp.float32),
        "out_li": centred(keys[11], (D, D), D ** -0.5, 0.09375, ((0, 8),)),
    }


def causal_taps(signal, filter_taps):
    count_taps = filter_taps.shape[0]
    length = signal.shape[0]
    padded = jnp.pad(signal, ((count_taps - 1, 0), (0, 0)))

    def accumulate(offset, summed):
        window = lax.dynamic_slice_in_dim(padded, count_taps - 1 - offset, length, 0)
        return summed + filter_taps[offset] * window

    return lax.fori_loop(0, count_taps, accumulate, jnp.zeros(signal.shape, jnp.float32))


def sharded_product(activations, weight):
    width_each = activations.shape[1] // N_MP
    summed = jnp.zeros((activations.shape[0], weight.shape[1]), jnp.float32)
    for member in range(N_MP):
        lower = member * width_each
        partial_sum = jnp.dot(activations[:, lower:lower + width_each], weight[lower:lower + width_each], preferred_element_type=jnp.float32)
        rounded = lax.optimization_barrier(partial_sum.astype(jnp.bfloat16))
        summed = summed + rounded.astype(jnp.float32)
    return summed


def featurized(members, taps_set):
    return [causal_taps(members[slot].astype(jnp.float32), taps_set[slot]) for slot in range(3)]


def reference(query_mr, key_mr, value_mr, featurizer_mr, mr_taps, out_mr, residual, in_weight, featurizer_li, li_rates, li_residues, out_li):
    q_one, k_one, v_one = featurized((query_mr, key_mr, value_mr), featurizer_mr)
    z_one = (k_one * v_one).astype(jnp.bfloat16)
    taps_full = jnp.repeat(mr_taps, GS, axis=1)
    conv_one = causal_taps(z_one.astype(jnp.float32), taps_full)
    conv_one = lax.optimization_barrier(conv_one.astype(jnp.bfloat16))
    gated_one = (q_one * conv_one.astype(jnp.float32)).astype(jnp.bfloat16)
    hidden = (residual.astype(jnp.float32) + sharded_product(gated_one, out_mr)).astype(jnp.bfloat16)
    fresh = [sharded_product(hidden, in_weight[slot]).astype(jnp.bfloat16) for slot in range(3)]
    q_two, k_two, v_two = featurized(fresh, featurizer_li)
    z_two = (k_two * v_two).astype(jnp.bfloat16)
    moments = jnp.arange(LENGTH).astype(jnp.float32)
    impulse = jnp.einsum("tgn,gn->tg", jnp.exp(-moments[:, None, None] * li_rates[None]), li_residues)
    impulse_full = jnp.repeat(impulse, GS, axis=1)
    spectrum = jnp.fft.rfft(z_two.astype(jnp.float32), n=2 * LENGTH, axis=0) * jnp.fft.rfft(impulse_full, n=2 * LENGTH, axis=0)
    conv_two = jnp.fft.irfft(spectrum, n=2 * LENGTH, axis=0)[:LENGTH]
    conv_two = lax.optimization_barrier(conv_two.astype(jnp.bfloat16))
    gated_two = (q_two * conv_two.astype(jnp.float32)).astype(jnp.bfloat16)
    return (hidden.astype(jnp.float32) + sharded_product(gated_two, out_li)).astype(jnp.bfloat16)
```

```python
import functools
import jax
import jax.numpy as jnp
from jax import lax
from jax.experimental import pallas as pl
from jax.experimental.pallas import tpu as pltpu
from jax.sharding import PartitionSpec as P

F32 = jnp.float32
BF16 = jnp.bfloat16
GS = 16
LANES = 128
NG = LANES // GS
ROWS = 256
WIDTH = 512
HALO = 144
VMEM_BYTES = 48 * 1024 * 1024


def params():
    return pltpu.CompilerParams(vmem_limit_bytes=VMEM_BYTES)


def vspecs(n):
    return [pl.BlockSpec(memory_space=pltpu.VMEM)] * n


def aspecs(n):
    return [pl.BlockSpec(memory_space=pl.ANY)] * n


SMEM_SPEC = pl.BlockSpec(memory_space=pltpu.SMEM)


def own_lanes(group):
    lane = lax.broadcasted_iota(jnp.int32, (1, LANES), 1)
    return (lane // GS) == group


def toeplitz_kernel(near_ref, far_ref, out_ref):
    row = lax.broadcasted_iota(jnp.int32, (LANES, LANES), 0)
    col = lax.broadcasted_iota(jnp.int32, (LANES, LANES), 1)
    groups = near_ref.shape[0]

    def one(g, carry):
        near = jnp.broadcast_to(near_ref[pl.ds(g, 1), :], (LANES, LANES))
        far = jnp.broadcast_to(far_ref[pl.ds(g, 1), :], (LANES, LANES))
        near = pltpu.roll(near, 0, 1, stride=1, stride_axis=0)
        far = pltpu.roll(far, 0, 1, stride=1, stride_axis=0)
        start = pl.multiple_of(g * LANES, LANES)
        out_ref[pl.ds(start, LANES), 0:LANES] = jnp.where(col > row, near, far).astype(BF16)
        out_ref[pl.ds(start, LANES), LANES:] = jnp.where(col <= row, near, 0.0).astype(BF16)
        return carry

    lax.fori_loop(0, groups, one, 0)


def toeplitz(near, far):
    groups = near.shape[0]
    return pl.pallas_call(
        toeplitz_kernel,
        out_shape=jax.ShapeDtypeStruct((groups * LANES, 2 * LANES), BF16),
        in_specs=vspecs(2),
        out_specs=pl.BlockSpec(memory_space=pltpu.VMEM),
        compiler_params=params(),
        name="toeplitz",
    )(near, far)


def feature(ext_ref, base, rows, taps):
    total = taps[0:1] * ext_ref[pl.ds(base, rows), :]
    for k in range(1, 3):
        total = total + taps[k : k + 1] * ext_ref[pl.ds(base - k, rows), :]
    return total


def filtered(toep_ref, block, early, middle, late):
    rhs = jnp.concatenate(
        [
            jnp.concatenate([early, middle], axis=0),
            jnp.concatenate([middle, late], axis=0),
        ],
        axis=1,
    )
    top = jnp.zeros((LANES, LANES), F32)
    low = jnp.zeros((LANES, LANES), F32)
    for g in range(NG):
        start = (block * NG + g) * LANES
        prod = jnp.dot(toep_ref[start : start + LANES, :], rhs, preferred_element_type=F32)
        mine = own_lanes(g)
        top = jnp.where(mine, prod[:, :LANES], top)
        low = jnp.where(mine, prod[:, LANES:], low)
    return top, low


def mr_kernel(q_ref, k_ref, v_ref, halo_ref, feat_ref, toep_ref, y_ref, kx, vx, qx):
    for block in range(WIDTH // LANES):
        cols = slice(block * LANES, (block + 1) * LANES)
        kx[0:HALO, :] = halo_ref[0:HALO, cols].astype(F32)
        kx[HALO:, :] = k_ref[:, cols].astype(F32)
        vx[0:HALO, :] = halo_ref[HALO : 2 * HALO, cols].astype(F32)
        vx[HALO:, :] = v_ref[:, cols].astype(F32)
        qx[0:16, :] = halo_ref[2 * HALO : 2 * HALO + 16, cols].astype(F32)
        qx[16:, :] = q_ref[:, cols].astype(F32)
        zs = []
        for part in range(3):
            base = HALO - LANES + part * LANES
            kf = feature(kx, base, LANES, feat_ref[1, :, cols])
            vf = feature(vx, base, LANES, feat_ref[2, :, cols])
            zs.append((kf * vf).astype(BF16))
        top, low = filtered(toep_ref, block, *zs)
        for part, conv in ((0, top), (1, low)):
            qf = feature(qx, 16 + part * LANES, LANES, feat_ref[0, :, cols])
            y_ref[part * LANES : (part + 1) * LANES, cols] = (qf * conv).astype(BF16)


def mr_op(q, k, v, halo, feat, toep):
    return pl.pallas_call(
        mr_kernel,
        out_shape=jax.ShapeDtypeStruct((ROWS, WIDTH), BF16),
        in_specs=vspecs(6),
        out_specs=pl.BlockSpec(memory_space=pltpu.VMEM),
        scratch_shapes=[
            pltpu.VMEM((HALO + ROWS, LANES), F32),
            pltpu.VMEM((HALO + ROWS, LANES), F32),
            pltpu.VMEM((16 + ROWS, LANES), F32),
        ],
        compiler_params=params(),
        name="mr_op",
    )(q, k, v, halo, feat, toep)


def share_kernel(flip, where_ref, y_ref, w_ref, o0, o1, o2, o3, wbuf, sems):
    x = where_ref[0]
    zh = where_ref[1]
    half = zh if flip == 0 else 1 - zh
    outs = (o0, o1, o2, o3)
    copies = []
    for d in range(4):
        block = lax.rem(x + d, 4) * 2 + half
        copy = pltpu.make_async_copy(
            w_ref.at[:, pl.ds(pl.multiple_of(block * WIDTH, WIDTH), WIDTH)], wbuf.at[d], sems.at[d]
        )
        copy.start()
        copies.append(copy)
    y = y_ref[...]
    for d in (1, 2, 3, 0):
        copies[d].wait()
        outs[d][...] = jnp.dot(y, wbuf[d], preferred_element_type=F32).astype(BF16)


def shares(where, y, weight, flip):
    piece = jax.ShapeDtypeStruct((ROWS, WIDTH), BF16)
    return pl.pallas_call(
        functools.partial(share_kernel, flip),
        out_shape=[piece] * 4,
        in_specs=[SMEM_SPEC] + vspecs(1) + aspecs(1),
        out_specs=vspecs(4),
        scratch_shapes=[
            pltpu.VMEM((4, WIDTH, WIDTH), BF16),
            pltpu.SemaphoreType.DMA((4,)),
        ],
        compiler_params=params(),
        name="shares",
    )(where, y, weight)


def project_kernel(count, where_ref, *refs):
    hidden_refs = refs[:8]
    weight_refs = refs[8:16]
    out_refs = refs[16 : 16 + count]
    hbuf, wbuf, hsem, wsem = refs[16 + count :]
    x, zh, y, zl, k = [where_ref[i] for i in range(5)]
    hcopies = []
    for e in range(2):
        for d in range(4):
            block = lax.rem(x + 4 - d, 4) * 2 + (zh if e == 0 else 1 - zh)
            copy = pltpu.make_async_copy(
                hidden_refs[e * 4 + d],
                hbuf.at[:, pl.ds(pl.multiple_of(block * WIDTH, WIDTH), WIDTH)],
                hsem.at[e * 4 + d],
            )
            copy.start()
            hcopies.append(copy)
    wcopies = []
    for j in range(count):
        for flip in range(2):
            for sy in range(4):
                for sz in range(4):
                    src_y = lax.rem(y + 4 - sy, 4)
                    src_z = lax.rem(zl + 4 - sz, 4)
                    src_k = k if flip == 0 else 1 - k
                    odd = lax.rem(src_z, 2)
                    high = lax.div(src_z, 2)
                    outer = jnp.where(odd == high, 1, 0)
                    row = src_y * 2 + jnp.where(outer == 1, 1 - zh, zh)
                    col = (1 - odd) * 2 + src_k
                    copy = pltpu.make_async_copy(
                        weight_refs[flip * 4 + sy].at[sz, j],
                        wbuf.at[
                            j,
                            pl.ds(pl.multiple_of(row * WIDTH, WIDTH), WIDTH),
                            pl.ds(pl.multiple_of(col * LANES, LANES), LANES),
                        ],
                        wsem.at[j, flip * 16 + sy * 4 + sz],
                    )
                    copy.start()
                    wcopies.append(copy)
    for copy in hcopies:
        copy.wait()
    for j in range(count):
        for copy in wcopies[j * 32 : (j + 1) * 32]:
            copy.wait()
        out_refs[j][...] = jnp.dot(hbuf[...], wbuf[j], preferred_element_type=F32).astype(BF16)


def project(where, pieces, weights, count):
    depth = 8 * WIDTH
    return pl.pallas_call(
        functools.partial(project_kernel, count),
        out_shape=[jax.ShapeDtypeStruct((ROWS, WIDTH), BF16)] * count,
        in_specs=[SMEM_SPEC] + aspecs(16),
        out_specs=vspecs(count),
        scratch_shapes=[
            pltpu.VMEM((ROWS, depth), BF16),
            pltpu.VMEM((count, depth, WIDTH), BF16),
            pltpu.SemaphoreType.DMA((8,)),
            pltpu.SemaphoreType.DMA((count, 32)),
        ],
        compiler_params=params(),
        name="project",
    )(where, *pieces, *weights)


def li_gate_kernel(k_ref, v_ref, halo_ref, feat_ref, enter_ref, z_ref, load_ref, kx, vx):
    for block in range(WIDTH // LANES):
        cols = slice(block * LANES, (block + 1) * LANES)
        kx[0:16, :] = halo_ref[0:16, cols].astype(F32)
        kx[16:, :] = k_ref[:, cols].astype(F32)
        vx[0:16, :] = halo_ref[16:32, cols].astype(F32)
        vx[16:, :] = v_ref[:, cols].astype(F32)
        kf = feature(kx, 16, ROWS, feat_ref[1, :, cols])
        vf = feature(vx, 16, ROWS, feat_ref[2, :, cols])
        z = (kf * vf).astype(BF16)
        z_ref[:, cols] = z
        enter = enter_ref[block * LANES : (block + 1) * LANES, :]
        high = enter.astype(BF16)
        rest = (enter - high.astype(F32)).astype(BF16)
        prod = jnp.dot(high, z, preferred_element_type=F32) + jnp.dot(rest, z, preferred_element_type=F32)
        load = jnp.zeros((GS, LANES), F32)
        for g in range(NG):
            load = jnp.where(own_lanes(g), prod[g * GS : (g + 1) * GS, :], load)
        load_ref[:, cols] = load


def li_gate(k, v, halo, feat, enter):
    return pl.pallas_call(
        li_gate_kernel,
        out_shape=[
            jax.ShapeDtypeStruct((ROWS, WIDTH), BF16),
            jax.ShapeDtypeStruct((GS, WIDTH), F32),
        ],
        in_specs=vspecs(5),
        out_specs=vspecs(2),
        scratch_shapes=[pltpu.VMEM((16 + ROWS, LANES), F32)] * 2,
        compiler_params=params(),
        name="li_gate",
    )(k, v, halo, feat, enter)


def li_inner_kernel(z_ref, toep_ref, q_ref, halo_ref, feat_ref, conv_ref, qf_ref, qx):
    for block in range(WIDTH // LANES):
        cols = slice(block * LANES, (block + 1) * LANES)
        qx[0:16, :] = halo_ref[:, cols].astype(F32)
        qx[16:, :] = q_ref[:, cols].astype(F32)
        qf_ref[:, cols] = feature(qx, 16, ROWS, feat_ref[0, :, cols])
        first = z_ref[0:LANES, cols]
        second = z_ref[LANES:ROWS, cols]
        top, low = filtered(toep_ref, block, jnp.zeros_like(first), first, second)
        conv_ref[0:LANES, cols] = top
        conv_ref[LANES:ROWS, cols] = low


def li_inner(z, toep, q, halo, feat):
    return pl.pallas_call(
        li_inner_kernel,
        out_shape=[jax.ShapeDtypeStruct((ROWS, WIDTH), F32)] * 2,
        in_specs=vspecs(5),
        out_specs=vspecs(2),
        scratch_shapes=[pltpu.VMEM((16 + ROWS, LANES), F32)],
        compiler_params=params(),
        name="li_inner",
    )(z, toep, q, halo, feat)


def li_outer_kernel(conv_ref, qf_ref, state_ref, leave_ref, y_ref):
    for block in range(WIDTH // LANES):
        cols = slice(block * LANES, (block + 1) * LANES)
        state = state_ref[:, cols]
        spread = jnp.concatenate(
            [jnp.where(own_lanes(g), state, 0.0) for g in range(NG)], axis=0
        )
        outer = jnp.dot(
            leave_ref[:, cols], spread, preferred_element_type=F32, precision=lax.Precision.HIGHEST
        )
        y_ref[:, cols] = (qf_ref[:, cols] * (conv_ref[:, cols] + outer)).astype(BF16)


def li_outer(conv, qf, state, leave):
    return pl.pallas_call(
        li_outer_kernel,
        out_shape=jax.ShapeDtypeStruct((ROWS, WIDTH), BF16),
        in_specs=vspecs(4),
        out_specs=pl.BlockSpec(memory_space=pltpu.VMEM),
        compiler_params=params(),
        name="li_outer",
    )(conv, qf, state, leave)


NY, NZ, NC, NX, NH = 4, 4, 2, 4, 2


def ctx_of(y, zl, k):
    return (y * NZ + zl) * NC + k


def mp_of(x, zh):
    return x * NH + zh


def x_shift(by):
    return [(mp_of(x, h), mp_of((x + by) % NX, h)) for x in range(NX) for h in range(NH)]


H_SWAP = [(mp_of(x, h), mp_of(x, 1 - h)) for x in range(NX) for h in range(NH)]
CORE_SWAP = [(i, i ^ 1) for i in range(NY * NZ * NC)]


def z_shift(by):
    return [
        (ctx_of(y, z, k), ctx_of(y, (z + by) % NZ, k))
        for y in range(NY) for z in range(NZ) for k in range(NC)
    ]


def y_shift(by):
    return [
        (ctx_of(y, z, k), ctx_of((y + by) % NY, z, k))
        for y in range(NY) for z in range(NZ) for k in range(NC)
    ]


def weight_moves():
    moves = []
    for y in range(NY):
        for zl in range(NZ):
            for k in range(NC):
                for x in range(NX):
                    for h in range(NH):
                        x2, h2, y2 = y, zl // 2, x
                        l0 = zl % 2
                        odd = 1 - l0
                        outer = h ^ h2
                        high = odd if outer else 1 - odd
                        z2 = high * 2 + odd
                        src = ctx_of(y, zl, k) * (NX * NH) + mp_of(x, h)
                        dst = ctx_of(y2, z2, k) * (NX * NH) + mp_of(x2, h2)
                        moves.append((src, dst))
    return moves


def gather_weight(piece):
    moved = lax.ppermute(piece, ("ctx", "mp"), weight_moves())
    line = jnp.stack([moved] + [lax.ppermute(moved, "ctx", z_shift(s)) for s in (1, 2, 3)])
    plane = [line] + [lax.ppermute(line, "ctx", y_shift(s)) for s in (1, 2, 3)]
    return plane + [lax.ppermute(p, "ctx", CORE_SWAP) for p in plane]


def sum_shares(where, y, weight, own_extra):
    other = shares(where, y, weight, 1)
    got_other = [lax.ppermute(other[d], "mp", x_shift(d)) for d in (1, 2, 3)]
    mine = shares(where, y, weight, 0)
    total_other = other[0].astype(F32)
    for piece in got_other:
        total_other = total_other + piece.astype(F32)
    crossed = lax.ppermute(total_other.astype(BF16), "mp", H_SWAP)
    got_mine = [lax.ppermute(mine[d], "mp", x_shift(d)) for d in (1, 2, 3)]
    total = own_extra.astype(F32) + mine[0].astype(F32)
    for piece in got_mine:
        total = total + piece.astype(F32)
    return (total + crossed.astype(F32)).astype(BF16)


def body(
    query_mr, key_mr, value_mr, featurizer_mr, mr_taps, out_mr,
    residual, in_weight, featurizer_li, li_rates, li_residues, out_li,
):
    ctx = lax.axis_index("ctx")
    mp = lax.axis_index("mp")
    x, zh = mp // NH, mp % NH
    y, zl, k = ctx // (NZ * NC), (ctx // NC) % NZ, ctx % NC
    where = jnp.stack([x, zh, y, zl, k]).astype(jnp.int32)

    forward = [(i, i + 1) for i in range(NY * NZ * NC - 1)]
    rim = jnp.concatenate(
        [key_mr[ROWS - HALO :], value_mr[ROWS - HALO :], query_mr[ROWS - 16 :]], axis=0
    )
    halo = lax.ppermute(rim, "ctx", forward)

    weights_kv = gather_weight(in_weight[1:3])
    weights_q = gather_weight(in_weight[0:1])

    def rolled(taps):
        return jnp.concatenate([taps[:1], taps[1:][::-1]], axis=0).T

    near_mr = rolled(mr_taps)
    toep_mr = toeplitz(near_mr, jnp.zeros_like(near_mr))

    steps = jnp.arange(ROWS).astype(F32)
    rates = li_rates.reshape(-1)
    decays = jnp.exp(-steps[:, None] * rates[None, :])
    leave = decays * li_residues.reshape(1, -1)
    impulse = leave.reshape(ROWS, -1, GS).sum(axis=2)
    toep_li = toeplitz(rolled(impulse[:LANES]), rolled(impulse[LANES:]))
    enter = jnp.exp(-rates[:, None] * (ROWS - steps)[None, :])
    lane_rates = jnp.repeat(li_rates.T, GS, axis=1)

    def fade(count):
        return jnp.exp(-lane_rates * count)

    gated_one = mr_op(query_mr, key_mr, value_mr, halo, featurizer_mr, toep_mr)
    hidden = sum_shares(where, gated_one, out_mr, residual)

    crossed = lax.ppermute(hidden, "mp", H_SWAP)
    pieces = [hidden] + [lax.ppermute(hidden, "mp", x_shift(d)) for d in (1, 2, 3)]
    pieces += [crossed] + [lax.ppermute(crossed, "mp", x_shift(d)) for d in (1, 2, 3)]
    fresh_k, fresh_v = project(where, pieces, weights_kv, 2)
    halo_kv = lax.ppermute(
        jnp.concatenate([fresh_k[ROWS - 16 :], fresh_v[ROWS - 16 :]], axis=0), "ctx", forward
    )
    (fresh_q,) = project(where, pieces, weights_q, 1)
    halo_q = lax.ppermute(fresh_q[ROWS - 16 :], "ctx", forward)

    product, load = li_gate(fresh_k, fresh_v, halo_kv, featurizer_li, enter)
    other_load = lax.ppermute(load, "ctx", CORE_SWAP)
    conv, qf = li_inner(product, toep_li, fresh_q, halo_q, featurizer_li)

    first = jnp.where(k == 0, load, other_load)
    second = jnp.where(k == 0, other_load, load)
    chip = first * fade(1.0 * ROWS) + second
    before = [lax.ppermute(chip, "ctx", z_shift(s)) for s in (1, 2, 3)]
    line_total = jnp.zeros_like(chip)
    line_carry = jnp.zeros_like(chip)
    for s, piece in enumerate([chip] + before):
        src = (zl - s) % NZ
        line_total = line_total + fade(2.0 * ROWS * (NZ - 1 - src).astype(F32)) * piece
        if s > 0:
            line_carry = line_carry + jnp.where(
                zl >= s, fade(2.0 * ROWS * (s - 1)) * piece, 0.0
            )
    y_carry = jnp.zeros_like(chip)
    for s in (1, 2, 3):
        pairs = [
            (ctx_of(a, b, c), ctx_of(a + s, b, c))
            for a in range(NY - s) for b in range(NZ) for c in range(NC)
        ]
        y_carry = y_carry + fade(2.0 * ROWS * NZ * (s - 1)) * lax.ppermute(line_total, "ctx", pairs)
    chip_state = line_carry + fade(2.0 * ROWS * zl.astype(F32)) * y_carry
    state = jnp.where(k == 0, chip_state, fade(1.0 * ROWS) * chip_state + other_load)

    gated_two = li_outer(conv, qf, state, leave)
    return sum_shares(where, gated_two, out_li, hidden)


def solution(mesh):
    return jax.shard_map(
        body,
        mesh=mesh,
        in_specs=(
            P("ctx", "mp"),
            P("ctx", "mp"),
            P("ctx", "mp"),
            P(None, None, "mp"),
            P(None, "mp"),
            P("mp", None),
            P("ctx", "mp"),
            P(None, "mp", "ctx"),
            P(None, None, "mp"),
            P("mp", None),
            P("mp", None),
            P("mp", None),
        ),
        out_specs=P("ctx", "mp"),
        check_vma=False,
    )
```

```python
import functools
import jax
import jax.numpy as jnp
from jax import lax
from jax.experimental import pallas as pl
from jax.experimental.pallas import tpu as pltpu
from jax.sharding import PartitionSpec as P

F32 = jnp.float32
BF16 = jnp.bfloat16
GS = 16
LANES = 128
NG = LANES // GS
ROWS = 256
WIDTH = 512
HALO = 144
VMEM_BYTES = 48 * 1024 * 1024


def params():
    return pltpu.CompilerParams(vmem_limit_bytes=VMEM_BYTES)


def vspecs(n):
    return [pl.BlockSpec(memory_space=pltpu.VMEM)] * n


def hspecs(n):
    return [pl.BlockSpec(memory_space=pltpu.HBM)] * n


SMEM_SPEC = pl.BlockSpec(memory_space=pltpu.SMEM)


def own_lanes(group):
    lane = lax.broadcasted_iota(jnp.int32, (1, LANES), 1)
    return (lane // GS) == group


NY, NZ, NC, NX, NH = 4, 4, 2, 4, 2

def toeplitz_rows(near, far):
    row = lax.broadcasted_iota(jnp.int32, (LANES, LANES), 0)
    col = lax.broadcasted_iota(jnp.int32, (LANES, LANES), 1)
    near = pltpu.roll(jnp.broadcast_to(near, (LANES, LANES)), 0, 1, stride=1, stride_axis=0)
    upper = near
    if far is not None:
        far = pltpu.roll(jnp.broadcast_to(far, (LANES, LANES)), 0, 1, stride=1, stride_axis=0)
    else:
        far = 0.0
    upper = jnp.where(col > row, near, far).astype(BF16)
    lower = jnp.where(col <= row, near, 0.0).astype(BF16)
    return upper, lower


def toeplitz_kernel(near_ref, out_ref):
    def one(g, carry):
        upper, lower = toeplitz_rows(near_ref[pl.ds(g, 1), :], None)
        start = pl.multiple_of(g * LANES, LANES)
        out_ref[pl.ds(start, LANES), 0:LANES] = upper
        out_ref[pl.ds(start, LANES), LANES:] = lower
        return carry

    lax.fori_loop(0, near_ref.shape[0], one, 0)


def toeplitz(near):
    groups = near.shape[0]
    return pl.pallas_call(
        toeplitz_kernel,
        out_shape=jax.ShapeDtypeStruct((groups * LANES, 2 * LANES), BF16),
        in_specs=vspecs(1),
        out_specs=pl.BlockSpec(memory_space=pltpu.VMEM),
        compiler_params=params(),
        name="toeplitz",
    )(near)


def prep_kernel(rates_ref, res_ref, rate_row_ref, res_row_ref, toep_ref, leave_ref, enter_ref, lane_ref, near, far):
    groups = rates_ref.shape[0]
    back = lax.broadcasted_iota(jnp.int32, (groups, LANES), 1)
    back = jnp.where(back == 0, 0, LANES - back).astype(F32)
    near_sum = jnp.zeros((groups, LANES), F32)
    far_sum = jnp.zeros((groups, LANES), F32)
    for n in range(GS):
        rate = rates_ref[:, n : n + 1]
        weight = res_ref[:, n : n + 1]
        near_sum = near_sum + weight * jnp.exp(-rate * back)
        far_sum = far_sum + weight * jnp.exp(-rate * (back + LANES))
    near[...] = near_sum
    far[...] = far_sum

    def one(g, carry):
        upper, lower = toeplitz_rows(near[pl.ds(g, 1), :], far[pl.ds(g, 1), :])
        start = pl.multiple_of(g * LANES, LANES)
        toep_ref[pl.ds(start, LANES), 0:LANES] = upper
        toep_ref[pl.ds(start, LANES), LANES:] = lower
        return carry

    lax.fori_loop(0, groups, one, 0)
    step = lax.broadcasted_iota(jnp.int32, (ROWS, LANES), 0).astype(F32)
    for block in range(WIDTH // LANES):
        cols = slice(block * LANES, (block + 1) * LANES)
        rate = rate_row_ref[:, cols]
        leave_ref[:, cols] = res_row_ref[:, cols] * jnp.exp(-rate * step)
        enter_ref[:, cols] = jnp.exp(-rate * (ROWS - step))
    lane = lax.broadcasted_iota(jnp.int32, (groups, WIDTH), 1)
    member = lax.broadcasted_iota(jnp.int32, (groups, WIDTH), 0)
    pick = jnp.where(lane // GS == member, 1.0, 0.0)
    lane_ref[...] = lax.dot_general(
        rates_ref[...], pick, (((0,), (0,)), ((), ())),
        preferred_element_type=F32, precision=lax.Precision.HIGHEST,
    )


def prep(rates, residues):
    groups = rates.shape[0]
    return pl.pallas_call(
        prep_kernel,
        out_shape=[
            jax.ShapeDtypeStruct((groups * LANES, 2 * LANES), BF16),
            jax.ShapeDtypeStruct((ROWS, WIDTH), F32),
            jax.ShapeDtypeStruct((ROWS, WIDTH), F32),
            jax.ShapeDtypeStruct((GS, WIDTH), F32),
        ],
        in_specs=vspecs(4),
        out_specs=vspecs(4),
        scratch_shapes=[pltpu.VMEM((groups, LANES), F32)] * 2,
        compiler_params=params(),
        name="prep",
    )(rates, residues, rates.reshape(1, WIDTH), residues.reshape(1, WIDTH))


def feature(ext_ref, base, rows, taps):
    total = taps[0:1] * ext_ref[pl.ds(base, rows), :]
    for k in range(1, 3):
        total = total + taps[k : k + 1] * ext_ref[pl.ds(base - k, rows), :]
    return total


def filtered(toep_ref, block, early, middle, late):
    rhs = jnp.concatenate(
        [
            jnp.concatenate([early, middle], axis=0),
            jnp.concatenate([middle, late], axis=0),
        ],
        axis=1,
    )
    top = jnp.zeros((LANES, LANES), F32)
    low = jnp.zeros((LANES, LANES), F32)
    for g in range(NG):
        start = (block * NG + g) * LANES
        prod = jnp.dot(toep_ref[start : start + LANES, :], rhs, preferred_element_type=F32)
        mine = own_lanes(g)
        top = jnp.where(mine, prod[:, :LANES], top)
        low = jnp.where(mine, prod[:, LANES:], low)
    return top, low


def share_loads(where_ref, w_ref, wbuf, sems, flip):
    x = where_ref[0]
    zh = where_ref[1]
    half = zh if flip == 0 else 1 - zh
    copies = []
    for d in range(4):
        block = lax.rem(x + d, 4) * 2 + half
        copy = pltpu.make_async_copy(
            w_ref.at[:, pl.ds(pl.multiple_of(block * WIDTH, WIDTH), WIDTH)], wbuf.at[d], sems.at[d]
        )
        copy.start()
        copies.append(copy)
    return copies


def share_products(copies, y_ref, wbuf, outs):
    for d in (1, 3, 2, 0):
        copies[d].wait()
        outs[d][...] = jnp.dot(y_ref[...], wbuf[d], preferred_element_type=F32).astype(BF16)


SHARE_SCRATCH = [pltpu.VMEM((4, WIDTH, WIDTH), BF16), pltpu.SemaphoreType.DMA((4,))]
PIECE = jax.ShapeDtypeStruct((ROWS, WIDTH), BF16)


def share_kernel(flip, where_ref, y_ref, w_ref, o0, o1, o2, o3, wbuf, sems):
    copies = share_loads(where_ref, w_ref, wbuf, sems, flip)
    share_products(copies, y_ref, wbuf, (o0, o1, o2, o3))


def shares(where, y, weight, flip):
    return pl.pallas_call(
        functools.partial(share_kernel, flip),
        out_shape=[PIECE] * 4,
        in_specs=[SMEM_SPEC] + vspecs(1) + hspecs(1),
        out_specs=vspecs(4),
        scratch_shapes=SHARE_SCRATCH,
        compiler_params=params(),
        name="shares",
    )(where, y, weight)


def mr_kernel(
    where_ref, q_ref, k_ref, v_ref, halo_ref, feat_ref, toep_ref, w_ref,
    y_ref, o0, o1, o2, o3, kx, vx, qx, wbuf, sems,
):
    copies = share_loads(where_ref, w_ref, wbuf, sems, 1)
    for block in range(WIDTH // LANES):
        cols = slice(block * LANES, (block + 1) * LANES)
        kx[0:HALO, :] = halo_ref[0:HALO, cols].astype(F32)
        kx[HALO:, :] = k_ref[:, cols].astype(F32)
        vx[0:HALO, :] = halo_ref[HALO : 2 * HALO, cols].astype(F32)
        vx[HALO:, :] = v_ref[:, cols].astype(F32)
        qx[0:16, :] = halo_ref[2 * HALO : 2 * HALO + 16, cols].astype(F32)
        qx[16:, :] = q_ref[:, cols].astype(F32)
        zs = []
        for part in range(3):
            base = HALO - LANES + part * LANES
            kf = feature(kx, base, LANES, feat_ref[1, :, cols])
            vf = feature(vx, base, LANES, feat_ref[2, :, cols])
            zs.append((kf * vf).astype(BF16))
        top, low = filtered(toep_ref, block, *zs)
        for part, conv in ((0, top), (1, low)):
            qf = feature(qx, 16 + part * LANES, LANES, feat_ref[0, :, cols])
            y_ref[part * LANES : (part + 1) * LANES, cols] = (qf * conv).astype(BF16)
    share_products(copies, y_ref, wbuf, (o0, o1, o2, o3))


def mr_op(where, q, k, v, halo, feat, toep, weight):
    return pl.pallas_call(
        mr_kernel,
        out_shape=[PIECE] * 5,
        in_specs=[SMEM_SPEC] + vspecs(6) + hspecs(1),
        out_specs=vspecs(5),
        scratch_shapes=[
            pltpu.VMEM((HALO + ROWS, LANES), F32),
            pltpu.VMEM((HALO + ROWS, LANES), F32),
            pltpu.VMEM((16 + ROWS, LANES), F32),
        ] + SHARE_SCRATCH,
        compiler_params=params(),
        name="mr_op",
    )(where, q, k, v, halo, feat, toep, weight)


def project_kernel(flips, count, first, last, where_ref, *refs):
    n = len(flips) * 4
    hidden_refs = refs[:n]
    w_ref = refs[n]
    pos = n + 1
    acc_refs = ()
    if not first:
        acc_refs = refs[pos : pos + count]
        pos += count
    out_refs = refs[pos : pos + count]
    hbuf, wbuf, hsem, wsem = refs[pos + count :]
    x = where_ref[0]
    hcopies, wcopies = [], []
    for i in range(n):
        e, d = flips[i // 4], i % 4
        copy = pltpu.make_async_copy(hidden_refs[i], hbuf.at[i], hsem.at[i])
        copy.start()
        hcopies.append(copy)
        src_y = lax.rem(x + 4 - d, 4)
        for b in range(4):
            odd = 1 - b // 2
            high = odd if e == 1 else 1 - odd
            member = (src_y * 4 + high * 2 + odd) * 2 + b % 2
            copy = pltpu.make_async_copy(
                w_ref.at[member],
                wbuf.at[i, :, :, pl.ds(b * LANES, LANES)],
                wsem.at[i, b],
            )
            copy.start()
            wcopies.append(copy)
    sums = [None] * count
    for i in range(n):
        hcopies[i].wait()
        for b in range(4):
            wcopies[i * 4 + b].wait()
        for j in range(count):
            prod = jnp.dot(hbuf[i], wbuf[i, j], preferred_element_type=F32)
            if i == 0:
                sums[j] = prod if first else prod + acc_refs[j][...]
            else:
                sums[j] = sums[j] + prod
    for j in range(count):
        out_refs[j][...] = sums[j].astype(BF16) if last else sums[j]


def project(where, pieces, weights, flips, count, acc=(), last=True):
    n = len(pieces)
    return pl.pallas_call(
        functools.partial(project_kernel, flips, count, not acc, last),
        out_shape=[jax.ShapeDtypeStruct((ROWS, WIDTH), BF16 if last else F32)] * count,
        in_specs=[SMEM_SPEC] + hspecs(n + 1) + vspecs(len(acc)),
        out_specs=vspecs(count),
        scratch_shapes=[
            pltpu.VMEM((n, ROWS, WIDTH), BF16),
            pltpu.VMEM((n, count, WIDTH, WIDTH), BF16),
            pltpu.SemaphoreType.DMA((n,)),
            pltpu.SemaphoreType.DMA((n, 4)),
        ],
        compiler_params=params(),
        name="project",
    )(where, *pieces, weights, *acc)


def li_gate_kernel(k_ref, v_ref, halo_ref, feat_ref, enter_ref, z_ref, load_ref, kx, vx):
    over_rows = (((0,), (0,)), ((), ()))
    for block in range(WIDTH // LANES):
        cols = slice(block * LANES, (block + 1) * LANES)
        kx[0:16, :] = halo_ref[0:16, cols].astype(F32)
        kx[16:, :] = k_ref[:, cols].astype(F32)
        vx[0:16, :] = halo_ref[16:32, cols].astype(F32)
        vx[16:, :] = v_ref[:, cols].astype(F32)
        kf = feature(kx, 16, ROWS, feat_ref[1, :, cols])
        vf = feature(vx, 16, ROWS, feat_ref[2, :, cols])
        z = (kf * vf).astype(BF16)
        z_ref[:, cols] = z
        enter = enter_ref[:, cols]
        high = enter.astype(BF16)
        rest = (enter - high.astype(F32)).astype(BF16)
        prod = lax.dot_general(high, z, over_rows, preferred_element_type=F32)
        prod = prod + lax.dot_general(rest, z, over_rows, preferred_element_type=F32)
        load = jnp.zeros((GS, LANES), F32)
        for g in range(NG):
            load = jnp.where(own_lanes(g), prod[g * GS : (g + 1) * GS, :], load)
        load_ref[:, cols] = load


def li_gate(k, v, halo, feat, enter):
    return pl.pallas_call(
        li_gate_kernel,
        out_shape=[PIECE, STATE],
        in_specs=vspecs(5),
        out_specs=vspecs(2),
        scratch_shapes=[pltpu.VMEM((16 + ROWS, LANES), F32)] * 2,
        compiler_params=params(),
        name="li_gate",
    )(k, v, halo, feat, enter)


STATE = jax.ShapeDtypeStruct((GS, WIDTH), F32)


def chip_kernel(where_ref, load_ref, other_ref, rates_ref, chip_ref):
    k = where_ref[4]
    load, other = load_ref[...], other_ref[...]
    fade = jnp.exp(-rates_ref[...] * (1.0 * ROWS))
    chip_ref[...] = jnp.where(k == 0, load * fade + other, other * fade + load)


def chip_state(where, load, other, rates):
    return pl.pallas_call(
        chip_kernel,
        out_shape=STATE,
        in_specs=[SMEM_SPEC] + vspecs(3),
        out_specs=pl.BlockSpec(memory_space=pltpu.VMEM),
        compiler_params=params(),
        name="chip_state",
    )(where, load, other, rates)


def line_kernel(where_ref, c0, c1, c2, c3, rates_ref, total_ref, carry_ref):
    zl = where_ref[3]
    rates = rates_ref[...]
    total = jnp.zeros(rates.shape, F32)
    carry = jnp.zeros(rates.shape, F32)
    for s, ref in enumerate((c0, c1, c2, c3)):
        piece = ref[...]
        src = lax.rem(zl + NZ - s, NZ)
        gap = ((NZ - 1 - src) * (2 * ROWS)).astype(F32)
        total = total + jnp.exp(-rates * gap) * piece
        if s > 0:
            part = jnp.exp(-rates * (2.0 * ROWS * (s - 1))) * piece
            carry = carry + jnp.where(zl >= s, part, 0.0)
    total_ref[...] = total
    carry_ref[...] = carry


def line_state(where, pieces, rates):
    return pl.pallas_call(
        line_kernel,
        out_shape=[STATE] * 2,
        in_specs=[SMEM_SPEC] + vspecs(5),
        out_specs=vspecs(2),
        compiler_params=params(),
        name="line_state",
    )(where, *pieces, rates)


def li_inner_kernel(z_ref, toep_ref, conv_ref):
    for block in range(WIDTH // LANES):
        cols = slice(block * LANES, (block + 1) * LANES)
        first = z_ref[0:LANES, cols]
        second = z_ref[LANES:ROWS, cols]
        top, low = filtered(toep_ref, block, jnp.zeros_like(first), first, second)
        conv_ref[0:LANES, cols] = top
        conv_ref[LANES:ROWS, cols] = low


def li_inner(z, toep):
    return pl.pallas_call(
        li_inner_kernel,
        out_shape=jax.ShapeDtypeStruct((ROWS, WIDTH), F32),
        in_specs=vspecs(2),
        out_specs=pl.BlockSpec(memory_space=pltpu.VMEM),
        compiler_params=params(),
        name="li_inner",
    )(z, toep)


def li_outer_kernel(
    where_ref, conv_ref, q_ref, halo_ref, feat_ref, leave_ref, rates_ref,
    carry_ref, other_ref, y1_ref, y2_ref, y3_ref, w_ref,
    y_ref, o0, o1, o2, o3, qx, wbuf, sems,
):
    copies = share_loads(where_ref, w_ref, wbuf, sems, 1)
    zl, k = where_ref[3], where_ref[4]
    rates = rates_ref[...]
    above = y1_ref[...]
    above = above + jnp.exp(-rates * (2.0 * ROWS * NZ)) * y2_ref[...]
    above = above + jnp.exp(-rates * (4.0 * ROWS * NZ)) * y3_ref[...]
    chip = carry_ref[...] + jnp.exp(-rates * (zl * (2 * ROWS)).astype(F32)) * above
    full = jnp.where(k == 0, chip, jnp.exp(-rates * (1.0 * ROWS)) * chip + other_ref[...])
    for block in range(WIDTH // LANES):
        cols = slice(block * LANES, (block + 1) * LANES)
        qx[0:16, :] = halo_ref[:, cols].astype(F32)
        qx[16:, :] = q_ref[:, cols].astype(F32)
        qf = feature(qx, 16, ROWS, feat_ref[0, :, cols])
        state = full[:, cols]
        spread = jnp.concatenate(
            [jnp.where(own_lanes(g), state, 0.0) for g in range(NG)], axis=0
        )
        outer = jnp.dot(
            leave_ref[:, cols], spread, preferred_element_type=F32, precision=lax.Precision.HIGHEST
        )
        y_ref[:, cols] = (qf * (conv_ref[:, cols] + outer)).astype(BF16)
    share_products(copies, y_ref, wbuf, (o0, o1, o2, o3))


def li_outer(where, conv, q, halo, feat, leave, rates, carry, other, above, weight):
    return pl.pallas_call(
        li_outer_kernel,
        out_shape=[PIECE] * 5,
        in_specs=[SMEM_SPEC] + vspecs(11) + hspecs(1),
        out_specs=vspecs(5),
        scratch_shapes=[pltpu.VMEM((16 + ROWS, LANES), F32)] + SHARE_SCRATCH,
        compiler_params=params(),
        name="li_outer",
    )(where, conv, q, halo, feat, leave, rates, carry, other, *above, weight)


def ctx_of(y, zl, k):
    return (y * NZ + zl) * NC + k


def mp_of(x, zh):
    return x * NH + zh


def x_shift(by):
    return [(mp_of(x, h), mp_of((x + by) % NX, h)) for x in range(NX) for h in range(NH)]


H_SWAP = [(mp_of(x, h), mp_of(x, 1 - h)) for x in range(NX) for h in range(NH)]
CORE_SWAP = [(i, i ^ 1) for i in range(NY * NZ * NC)]


def z_shift(by):
    return [
        (ctx_of(y, z, k), ctx_of(y, (z + by) % NZ, k))
        for y in range(NY) for z in range(NZ) for k in range(NC)
    ]


def y_shift(by):
    return [
        (ctx_of(y, z, k), ctx_of((y + by) % NY, z, k))
        for y in range(NY) for z in range(NZ) for k in range(NC)
    ]


def weight_moves():
    moves = []
    for y in range(NY):
        for zl in range(NZ):
            for k in range(NC):
                for x in range(NX):
                    for h in range(NH):
                        x2, h2, y2 = y, zl // 2, x
                        l0 = zl % 2
                        odd = 1 - l0
                        outer = h ^ h2
                        high = odd if outer else 1 - odd
                        z2 = high * 2 + odd
                        src = ctx_of(y, zl, k) * (NX * NH) + mp_of(x, h)
                        dst = ctx_of(y2, z2, k) * (NX * NH) + mp_of(x2, h2)
                        moves.append((src, dst))
    return moves


def tied(*values):
    return lax.optimization_barrier(values)


def sum_shares(where, y, other, weight, own_extra, fillers):
    got = [lax.ppermute(other[d], "mp", x_shift(d)) for d in (1, 3, 2)]
    if fillers:
        held = tied(*got, *fillers)
        got, fillers = held[:3], held[3:]
    total_other = other[0].astype(F32)
    for piece in got:
        total_other = total_other + piece.astype(F32)
    total_other, *mine = tied(total_other.astype(BF16), *shares(where, y, weight, 0))
    crossed = lax.ppermute(total_other, "mp", H_SWAP)
    got_mine = [lax.ppermute(mine[d], "mp", x_shift(d)) for d in (1, 3, 2)]
    total = own_extra.astype(F32) + mine[0].astype(F32)
    for piece in got_mine:
        total = total + piece.astype(F32)
    return (total + crossed.astype(F32)).astype(BF16), fillers


def body(
    query_mr, key_mr, value_mr, featurizer_mr, mr_taps, out_mr,
    residual, in_weight, featurizer_li, li_rates, li_residues, out_li,
):
    ctx = lax.axis_index("ctx")
    mp = lax.axis_index("mp")
    x, zh = mp // NH, mp % NH
    y, zl, k = ctx // (NZ * NC), (ctx // NC) % NZ, ctx % NC
    where = jnp.stack([x, zh, y, zl, k]).astype(jnp.int32)

    forward = [(i, i + 1) for i in range(NY * NZ * NC - 1)]
    rim = jnp.concatenate(
        [key_mr[ROWS - HALO :], value_mr[ROWS - HALO :], query_mr[ROWS - 16 :]], axis=0
    )
    rim, in_weight = tied(rim, in_weight)
    halo = lax.ppermute(rim, "ctx", forward)
    moved_kv = lax.ppermute(in_weight[1:3], ("ctx", "mp"), weight_moves())
    moved_q = lax.ppermute(in_weight[0:1], ("ctx", "mp"), weight_moves())

    toep_mr = toeplitz(jnp.concatenate([mr_taps[:1], mr_taps[1:][::-1]], axis=0).T)

    halo, moved_kv, toep_mr = tied(halo, moved_kv, toep_mr)
    gated_one, *other_one = mr_op(
        where, query_mr, key_mr, value_mr, halo, featurizer_mr, toep_mr, out_mr
    )
    weights_kv = lax.all_gather(moved_kv, "ctx")
    filters = prep(li_rates, li_residues)
    hidden, filters = sum_shares(
        where, gated_one, other_one, out_mr, residual, tuple(filters) + (moved_q,)
    )
    toep_li, leave, enter, lane_rates, moved_q = filters

    hidden, moved_q = tied(hidden, moved_q)
    crossed = lax.ppermute(hidden, "mp", H_SWAP)
    own_pieces = [hidden] + [lax.ppermute(hidden, "mp", x_shift(d)) for d in (1, 2, 3)]
    weights_q = lax.all_gather(moved_q, "ctx")
    far_pieces = [crossed] + [lax.ppermute(crossed, "mp", x_shift(d)) for d in (1, 2, 3)]
    partial = project(where, own_pieces, weights_kv, (0,), 2, last=False)
    fresh_k, fresh_v = project(where, far_pieces, weights_kv, (1,), 2, acc=tuple(partial))
    halo_kv = lax.ppermute(
        jnp.concatenate([fresh_k[ROWS - 16 :], fresh_v[ROWS - 16 :]], axis=0), "ctx", forward
    )
    product, load = li_gate(fresh_k, fresh_v, halo_kv, featurizer_li, enter)
    other_load = lax.ppermute(load, "ctx", CORE_SWAP)
    chip = chip_state(where, load, other_load, lane_rates)
    before = [lax.ppermute(chip, "ctx", z_shift(s)) for s in (1, 2, 3)]
    line_total, line_carry = line_state(where, [chip] + before, lane_rates)
    above = []
    for s in (1, 2, 3):
        pairs = [
            (ctx_of(a, b, c), ctx_of(a + s, b, c))
            for a in range(NY - s) for b in range(NZ) for c in range(NC)
        ]
        above.append(lax.ppermute(line_total, "ctx", pairs))

    (fresh_q,) = project(where, own_pieces + far_pieces, weights_q, (0, 1), 1)
    halo_q = lax.ppermute(fresh_q[ROWS - 16 :], "ctx", forward)
    conv = li_inner(product, toep_li)

    gated_two, *other_two = li_outer(
        where, conv, fresh_q, halo_q, featurizer_li, leave, lane_rates,
        line_carry, other_load, above, out_li,
    )
    return sum_shares(where, gated_two, other_two, out_li, hidden, ())[0]


def solution(mesh):
    return jax.shard_map(
        body,
        mesh=mesh,
        in_specs=(
            P("ctx", "mp"),
            P("ctx", "mp"),
            P("ctx", "mp"),
            P(None, None, "mp"),
            P(None, "mp"),
            P("mp", None),
            P("ctx", "mp"),
            P(None, "mp", "ctx"),
            P(None, None, "mp"),
            P("mp", None),
            P("mp", None),
            P("mp", None),
        ),
        out_specs=P("ctx", "mp"),
        check_vma=False,
    )
```

```python
import functools
import jax
import jax.numpy as jnp
from jax import lax
from jax.experimental import pallas as pl
from jax.experimental.pallas import tpu as pltpu
from jax.sharding import PartitionSpec as P

F32 = jnp.float32
BF16 = jnp.bfloat16
GS = 16
LANES = 128
NG = LANES // GS
ROWS = 256
WIDTH = 512
HALO = 144
VMEM_BYTES = 48 * 1024 * 1024


def params():
    return pltpu.CompilerParams(vmem_limit_bytes=VMEM_BYTES)


def vspecs(n):
    return [pl.BlockSpec(memory_space=pltpu.VMEM)] * n


def hspecs(n):
    return [pl.BlockSpec(memory_space=pltpu.HBM)] * n


SMEM_SPEC = pl.BlockSpec(memory_space=pltpu.SMEM)


def own_lanes(group):
    lane = lax.broadcasted_iota(jnp.int32, (1, LANES), 1)
    return (lane // GS) == group


NY, NZ, NC, NX, NH = 4, 4, 2, 4, 2

def rim_kernel(q_ref, k_ref, v_ref, out_ref, sems):
    parts = ((k_ref, HALO, 0), (v_ref, HALO, HALO), (q_ref, 16, 2 * HALO))
    copies = []
    for i, (ref, depth, at) in enumerate(parts):
        copy = pltpu.make_async_copy(
            ref.at[pl.ds(ROWS - depth, depth)], out_ref.at[pl.ds(at, depth)], sems.at[i]
        )
        copy.start()
        copies.append(copy)
    for copy in copies:
        copy.wait()


def rim_rows(q, k, v):
    return pl.pallas_call(
        rim_kernel,
        out_shape=jax.ShapeDtypeStruct((2 * HALO + 16, WIDTH), BF16),
        in_specs=hspecs(3),
        out_specs=pl.BlockSpec(memory_space=pltpu.VMEM),
        scratch_shapes=[pltpu.SemaphoreType.DMA((3,))],
        compiler_params=params(),
        name="rim_rows",
    )(q, k, v)


OVER_FIRST = (((0,), (0,)), ((), ()))


def exact(a, b):
    return lax.dot_general(a, b, OVER_FIRST, preferred_element_type=F32, precision=lax.Precision.HIGHEST)


def toeplitz_rows(near, far):
    row = lax.broadcasted_iota(jnp.int32, (LANES, LANES), 0)
    col = lax.broadcasted_iota(jnp.int32, (LANES, LANES), 1)
    near = pltpu.roll(jnp.broadcast_to(near, (LANES, LANES)), 0, 1, stride=1, stride_axis=0)
    upper = near
    if far is not None:
        far = pltpu.roll(jnp.broadcast_to(far, (LANES, LANES)), 0, 1, stride=1, stride_axis=0)
    else:
        far = 0.0
    upper = jnp.where(col > row, near, far).astype(BF16)
    lower = jnp.where(col <= row, near, 0.0).astype(BF16)
    return upper, lower


def toeplitz_kernel(taps_ref, out_ref, near):
    tap = lax.broadcasted_iota(jnp.int32, (LANES, LANES), 0)
    at = lax.broadcasted_iota(jnp.int32, (LANES, LANES), 1)
    near[...] = exact(taps_ref[...], jnp.where(tap == lax.rem(LANES - at, LANES), 1.0, 0.0))

    def one(g, carry):
        upper, lower = toeplitz_rows(near[pl.ds(g, 1), :], None)
        start = pl.multiple_of(g * LANES, LANES)
        out_ref[pl.ds(start, LANES), 0:LANES] = upper
        out_ref[pl.ds(start, LANES), LANES:] = lower
        return carry

    lax.fori_loop(0, near.shape[0], one, 0)


def toeplitz(taps):
    groups = taps.shape[1]
    return pl.pallas_call(
        toeplitz_kernel,
        out_shape=jax.ShapeDtypeStruct((groups * LANES, 2 * LANES), BF16),
        in_specs=vspecs(1),
        out_specs=pl.BlockSpec(memory_space=pltpu.VMEM),
        scratch_shapes=[pltpu.VMEM((groups, LANES), F32)],
        compiler_params=params(),
        name="toeplitz",
    )(taps)


def prep_kernel(rates_ref, res_ref, toep_ref, leave_ref, enter_ref, lane_ref, near, far):
    modes, groups = rates_ref.shape
    mode_r = lax.broadcasted_iota(jnp.int32, (modes, modes), 0)
    mode_c = lax.broadcasted_iota(jnp.int32, (modes, modes), 1)
    same = jnp.where(mode_r == mode_c, 1.0, 0.0)
    rates = exact(rates_ref[...], same)
    weights = exact(res_ref[...], same)
    back = lax.broadcasted_iota(jnp.int32, (groups, LANES), 1)
    back = jnp.where(back == 0, 0, LANES - back).astype(F32)
    near_sum = jnp.zeros((groups, LANES), F32)
    far_sum = jnp.zeros((groups, LANES), F32)
    for n in range(GS):
        rate = rates[:, n : n + 1]
        weight = weights[:, n : n + 1]
        near_sum = near_sum + weight * jnp.exp(-rate * back)
        far_sum = far_sum + weight * jnp.exp(-rate * (back + LANES))
    near[...] = near_sum
    far[...] = far_sum

    def one(g, carry):
        upper, lower = toeplitz_rows(near[pl.ds(g, 1), :], far[pl.ds(g, 1), :])
        start = pl.multiple_of(g * LANES, LANES)
        toep_ref[pl.ds(start, LANES), 0:LANES] = upper
        toep_ref[pl.ds(start, LANES), LANES:] = lower
        return carry

    lax.fori_loop(0, groups, one, 0)
    lane = lax.broadcasted_iota(jnp.int32, (groups, WIDTH), 1)
    member = lax.broadcasted_iota(jnp.int32, (groups, WIDTH), 0)
    pick = jnp.where(lane // GS == member, 1.0, 0.0)
    lane_rates = exact(rates, pick)
    lane_ref[...] = lane_rates
    lane = lax.broadcasted_iota(jnp.int32, (modes, WIDTH), 1)
    member = lax.broadcasted_iota(jnp.int32, (modes, WIDTH), 0)
    ours = lax.rem(lane, GS) == member
    rate_row = jnp.sum(jnp.where(ours, lane_rates, 0.0), axis=0, keepdims=True)
    weight_row = jnp.sum(jnp.where(ours, exact(weights, pick), 0.0), axis=0, keepdims=True)
    step = lax.broadcasted_iota(jnp.int32, (ROWS, LANES), 0).astype(F32)
    for block in range(WIDTH // LANES):
        cols = slice(block * LANES, (block + 1) * LANES)
        rate = rate_row[:, cols]
        leave_ref[:, cols] = weight_row[:, cols] * jnp.exp(-rate * step)
        enter_ref[:, cols] = jnp.exp(-rate * (ROWS - step))


def prep(rates, residues):
    groups = rates.shape[1]
    return pl.pallas_call(
        prep_kernel,
        out_shape=[
            jax.ShapeDtypeStruct((groups * LANES, 2 * LANES), BF16),
            jax.ShapeDtypeStruct((ROWS, WIDTH), F32),
            jax.ShapeDtypeStruct((ROWS, WIDTH), F32),
            jax.ShapeDtypeStruct((GS, WIDTH), F32),
        ],
        in_specs=vspecs(2),
        out_specs=vspecs(4),
        scratch_shapes=[pltpu.VMEM((groups, LANES), F32)] * 2,
        compiler_params=params(),
        name="prep",
    )(rates, residues)


def feature(ext_ref, base, rows, taps):
    total = taps[0:1] * ext_ref[pl.ds(base, rows), :]
    for k in range(1, 3):
        total = total + taps[k : k + 1] * ext_ref[pl.ds(base - k, rows), :]
    return total


def filtered(toep_ref, block, early, middle, late):
    rhs = jnp.concatenate(
        [
            jnp.concatenate([early, middle], axis=0),
            jnp.concatenate([middle, late], axis=0),
        ],
        axis=1,
    )
    top = jnp.zeros((LANES, LANES), F32)
    low = jnp.zeros((LANES, LANES), F32)
    for g in range(NG):
        start = (block * NG + g) * LANES
        prod = jnp.dot(toep_ref[start : start + LANES, :], rhs, preferred_element_type=F32)
        mine = own_lanes(g)
        top = jnp.where(mine, prod[:, :LANES], top)
        low = jnp.where(mine, prod[:, LANES:], low)
    return top, low


def share_loads(where_ref, w_ref, wbuf, sems, flip):
    x = where_ref[0]
    zh = where_ref[1]
    half = zh if flip == 0 else 1 - zh
    copies = []
    for d in range(4):
        block = lax.rem(x + d, 4) * 2 + half
        copy = pltpu.make_async_copy(
            w_ref.at[:, pl.ds(pl.multiple_of(block * WIDTH, WIDTH), WIDTH)], wbuf.at[d], sems.at[d]
        )
        copy.start()
        copies.append(copy)
    return copies


def share_products(copies, y_ref, wbuf, outs):
    for d in (1, 3, 2, 0):
        copies[d].wait()
        outs[d][...] = jnp.dot(y_ref[...], wbuf[d], preferred_element_type=F32).astype(BF16)


SHARE_SCRATCH = [pltpu.VMEM((4, WIDTH, WIDTH), BF16), pltpu.SemaphoreType.DMA((4,))]
PIECE = jax.ShapeDtypeStruct((ROWS, WIDTH), BF16)


def share_kernel(flip, where_ref, y_ref, w_ref, o0, o1, o2, o3, wbuf, sems):
    copies = share_loads(where_ref, w_ref, wbuf, sems, flip)
    share_products(copies, y_ref, wbuf, (o0, o1, o2, o3))


def shares(where, y, weight, flip):
    return pl.pallas_call(
        functools.partial(share_kernel, flip),
        out_shape=[PIECE] * 4,
        in_specs=[SMEM_SPEC] + vspecs(1) + hspecs(1),
        out_specs=vspecs(4),
        scratch_shapes=SHARE_SCRATCH,
        compiler_params=params(),
        name="shares",
    )(where, y, weight)


def mr_kernel(
    where_ref, q_ref, k_ref, v_ref, halo_ref, feat_ref, toep_ref, w_ref,
    y_ref, o0, o1, o2, o3, kx, vx, qx, wbuf, sems,
):
    copies = share_loads(where_ref, w_ref, wbuf, sems, 1)
    for block in range(WIDTH // LANES):
        cols = slice(block * LANES, (block + 1) * LANES)
        kx[0:HALO, :] = halo_ref[0:HALO, cols].astype(F32)
        kx[HALO:, :] = k_ref[:, cols].astype(F32)
        vx[0:HALO, :] = halo_ref[HALO : 2 * HALO, cols].astype(F32)
        vx[HALO:, :] = v_ref[:, cols].astype(F32)
        qx[0:16, :] = halo_ref[2 * HALO : 2 * HALO + 16, cols].astype(F32)
        qx[16:, :] = q_ref[:, cols].astype(F32)
        zs = []
        for part in range(3):
            base = HALO - LANES + part * LANES
            kf = feature(kx, base, LANES, feat_ref[1, :, cols])
            vf = feature(vx, base, LANES, feat_ref[2, :, cols])
            zs.append((kf * vf).astype(BF16))
        top, low = filtered(toep_ref, block, *zs)
        for part, conv in ((0, top), (1, low)):
            qf = feature(qx, 16 + part * LANES, LANES, feat_ref[0, :, cols])
            y_ref[part * LANES : (part + 1) * LANES, cols] = (qf * conv).astype(BF16)
    share_products(copies, y_ref, wbuf, (o0, o1, o2, o3))


def mr_op(where, q, k, v, halo, feat, toep, weight):
    return pl.pallas_call(
        mr_kernel,
        out_shape=[PIECE] * 5,
        in_specs=[SMEM_SPEC] + vspecs(6) + hspecs(1),
        out_specs=vspecs(5),
        scratch_shapes=[
            pltpu.VMEM((HALO + ROWS, LANES), F32),
            pltpu.VMEM((HALO + ROWS, LANES), F32),
            pltpu.VMEM((16 + ROWS, LANES), F32),
        ] + SHARE_SCRATCH,
        compiler_params=params(),
        name="mr_op",
    )(where, q, k, v, halo, feat, toep, weight)


def project_kernel(flips, slots, first, last, where_ref, *refs):
    n = len(flips) * 4
    count = len(slots)
    hidden_refs = refs[:n]
    w_ref = refs[n]
    pos = n + 1
    acc_refs = ()
    if not first:
        acc_refs = refs[pos : pos + count]
        pos += count
    out_refs = refs[pos : pos + count]
    hbuf, wbuf, hsem, wsem = refs[pos + count :]
    x = where_ref[0]
    hcopies, wcopies = [], []
    for i in range(n):
        e, d = flips[i // 4], (0, 1, 3, 2)[i % 4]
        copy = pltpu.make_async_copy(hidden_refs[i], hbuf.at[i], hsem.at[i])
        copy.start()
        hcopies.append(copy)
        src_y = lax.rem(x + 4 - d, 4)
        for b in range(4):
            odd = 1 - b // 2
            high = odd if e == 1 else 1 - odd
            member = (src_y * 4 + high * 2 + odd) * 2 + b % 2
            copy = pltpu.make_async_copy(
                w_ref.at[member, pl.ds(slots[0], count)],
                wbuf.at[i, :, :, pl.ds(b * LANES, LANES)],
                wsem.at[i, b],
            )
            copy.start()
            wcopies.append(copy)
    sums = [None] * count
    for i in range(n):
        hcopies[i].wait()
        for b in range(4):
            wcopies[i * 4 + b].wait()
        for j in range(count):
            prod = jnp.dot(hbuf[i], wbuf[i, j], preferred_element_type=F32)
            if i == 0:
                sums[j] = prod if first else prod + acc_refs[j][...]
            else:
                sums[j] = sums[j] + prod
    for j in range(count):
        out_refs[j][...] = sums[j].astype(BF16) if last else sums[j]


def project(where, pieces, weights, flips, slots, acc=(), last=True):
    n, count = len(pieces), len(slots)
    return pl.pallas_call(
        functools.partial(project_kernel, flips, slots, not acc, last),
        out_shape=[jax.ShapeDtypeStruct((ROWS, WIDTH), BF16 if last else F32)] * count,
        in_specs=[SMEM_SPEC] + hspecs(n + 1) + vspecs(len(acc)),
        out_specs=vspecs(count),
        scratch_shapes=[
            pltpu.VMEM((n, ROWS, WIDTH), BF16),
            pltpu.VMEM((n, count, WIDTH, WIDTH), BF16),
            pltpu.SemaphoreType.DMA((n,)),
            pltpu.SemaphoreType.DMA((n, 4)),
        ],
        compiler_params=params(),
        name="project",
    )(where, *pieces, weights, *acc)


def li_gate_kernel(k_ref, v_ref, halo_ref, feat_ref, enter_ref, z_ref, load_ref, kx, vx):
    for block in range(WIDTH // LANES):
        cols = slice(block * LANES, (block + 1) * LANES)
        kx[0:16, :] = halo_ref[0:16, cols].astype(F32)
        kx[16:, :] = k_ref[:, cols].astype(F32)
        vx[0:16, :] = halo_ref[16:32, cols].astype(F32)
        vx[16:, :] = v_ref[:, cols].astype(F32)
        kf = feature(kx, 16, ROWS, feat_ref[1, :, cols])
        vf = feature(vx, 16, ROWS, feat_ref[2, :, cols])
        z = (kf * vf).astype(BF16)
        z_ref[:, cols] = z
        enter = enter_ref[:, cols]
        high = enter.astype(BF16)
        rest = (enter - high.astype(F32)).astype(BF16)
        prod = lax.dot_general(high, z, OVER_FIRST, preferred_element_type=F32)
        prod = prod + lax.dot_general(rest, z, OVER_FIRST, preferred_element_type=F32)
        load = jnp.zeros((GS, LANES), F32)
        for g in range(NG):
            load = jnp.where(own_lanes(g), prod[g * GS : (g + 1) * GS, :], load)
        load_ref[:, cols] = load


def li_gate(k, v, halo, feat, enter):
    return pl.pallas_call(
        li_gate_kernel,
        out_shape=[PIECE, STATE],
        in_specs=vspecs(5),
        out_specs=vspecs(2),
        scratch_shapes=[pltpu.VMEM((16 + ROWS, LANES), F32)] * 2,
        compiler_params=params(),
        name="li_gate",
    )(k, v, halo, feat, enter)


STATE = jax.ShapeDtypeStruct((GS, WIDTH), F32)


def chip_kernel(where_ref, load_ref, other_ref, rates_ref, chip_ref):
    k = where_ref[4]
    load, other = load_ref[...], other_ref[...]
    fade = jnp.exp(-rates_ref[...] * (1.0 * ROWS))
    chip_ref[...] = jnp.where(k == 0, load * fade + other, other * fade + load)


def chip_state(where, load, other, rates):
    return pl.pallas_call(
        chip_kernel,
        out_shape=STATE,
        in_specs=[SMEM_SPEC] + vspecs(3),
        out_specs=pl.BlockSpec(memory_space=pltpu.VMEM),
        compiler_params=params(),
        name="chip_state",
    )(where, load, other, rates)


def line_kernel(where_ref, c0, c1, c2, c3, rates_ref, total_ref, carry_ref):
    zl = where_ref[3]
    rates = rates_ref[...]
    total = jnp.zeros(rates.shape, F32)
    carry = jnp.zeros(rates.shape, F32)
    for s, ref in enumerate((c0, c1, c2, c3)):
        piece = ref[...]
        src = lax.rem(zl + NZ - s, NZ)
        gap = ((NZ - 1 - src) * (2 * ROWS)).astype(F32)
        total = total + jnp.exp(-rates * gap) * piece
        if s > 0:
            part = jnp.exp(-rates * (2.0 * ROWS * (s - 1))) * piece
            carry = carry + jnp.where(zl >= s, part, 0.0)
    total_ref[...] = total
    carry_ref[...] = carry


def line_state(where, pieces, rates):
    return pl.pallas_call(
        line_kernel,
        out_shape=[STATE] * 2,
        in_specs=[SMEM_SPEC] + vspecs(5),
        out_specs=vspecs(2),
        compiler_params=params(),
        name="line_state",
    )(where, *pieces, rates)


def li_inner_kernel(z_ref, toep_ref, conv_ref):
    for block in range(WIDTH // LANES):
        cols = slice(block * LANES, (block + 1) * LANES)
        first = z_ref[0:LANES, cols]
        second = z_ref[LANES:ROWS, cols]
        top, low = filtered(toep_ref, block, jnp.zeros_like(first), first, second)
        conv_ref[0:LANES, cols] = top
        conv_ref[LANES:ROWS, cols] = low


def li_inner(z, toep):
    return pl.pallas_call(
        li_inner_kernel,
        out_shape=jax.ShapeDtypeStruct((ROWS, WIDTH), F32),
        in_specs=vspecs(2),
        out_specs=pl.BlockSpec(memory_space=pltpu.VMEM),
        compiler_params=params(),
        name="li_inner",
    )(z, toep)


def li_outer_kernel(
    where_ref, conv_ref, q_ref, halo_ref, feat_ref, leave_ref, rates_ref,
    carry_ref, other_ref, y1_ref, y2_ref, y3_ref, w_ref,
    y_ref, o0, o1, o2, o3, qx, wbuf, sems,
):
    copies = share_loads(where_ref, w_ref, wbuf, sems, 1)
    zl, k = where_ref[3], where_ref[4]
    rates = rates_ref[...]
    above = y1_ref[...]
    above = above + jnp.exp(-rates * (2.0 * ROWS * NZ)) * y2_ref[...]
    above = above + jnp.exp(-rates * (4.0 * ROWS * NZ)) * y3_ref[...]
    chip = carry_ref[...] + jnp.exp(-rates * (zl * (2 * ROWS)).astype(F32)) * above
    full = jnp.where(k == 0, chip, jnp.exp(-rates * (1.0 * ROWS)) * chip + other_ref[...])
    for block in range(WIDTH // LANES):
        cols = slice(block * LANES, (block + 1) * LANES)
        qx[0:16, :] = halo_ref[:, cols].astype(F32)
        qx[16:, :] = q_ref[:, cols].astype(F32)
        qf = feature(qx, 16, ROWS, feat_ref[0, :, cols])
        state = full[:, cols]
        spread = jnp.concatenate(
            [jnp.where(own_lanes(g), state, 0.0) for g in range(NG)], axis=0
        )
        outer = jnp.dot(
            leave_ref[:, cols], spread, preferred_element_type=F32, precision=lax.Precision.HIGHEST
        )
        y_ref[:, cols] = (qf * (conv_ref[:, cols] + outer)).astype(BF16)
    share_products(copies, y_ref, wbuf, (o0, o1, o2, o3))


def li_outer(where, conv, q, halo, feat, leave, rates, carry, other, above, weight):
    return pl.pallas_call(
        li_outer_kernel,
        out_shape=[PIECE] * 5,
        in_specs=[SMEM_SPEC] + vspecs(11) + hspecs(1),
        out_specs=vspecs(5),
        scratch_shapes=[pltpu.VMEM((16 + ROWS, LANES), F32)] + SHARE_SCRATCH,
        compiler_params=params(),
        name="li_outer",
    )(where, conv, q, halo, feat, leave, rates, carry, other, *above, weight)


def ctx_of(y, zl, k):
    return (y * NZ + zl) * NC + k


def mp_of(x, zh):
    return x * NH + zh


def x_shift(by):
    return [(mp_of(x, h), mp_of((x + by) % NX, h)) for x in range(NX) for h in range(NH)]


H_SWAP = [(mp_of(x, h), mp_of(x, 1 - h)) for x in range(NX) for h in range(NH)]
CORE_SWAP = [(i, i ^ 1) for i in range(NY * NZ * NC)]


def z_shift(by):
    return [
        (ctx_of(y, z, k), ctx_of(y, (z + by) % NZ, k))
        for y in range(NY) for z in range(NZ) for k in range(NC)
    ]


def y_shift(by):
    return [
        (ctx_of(y, z, k), ctx_of((y + by) % NY, z, k))
        for y in range(NY) for z in range(NZ) for k in range(NC)
    ]


def weight_moves():
    moves = []
    for y in range(NY):
        for zl in range(NZ):
            for k in range(NC):
                for x in range(NX):
                    for h in range(NH):
                        x2, h2, y2 = y, zl // 2, x
                        l0 = zl % 2
                        odd = 1 - l0
                        outer = h ^ h2
                        high = odd if outer else 1 - odd
                        z2 = high * 2 + odd
                        src = ctx_of(y, zl, k) * (NX * NH) + mp_of(x, h)
                        dst = ctx_of(y2, z2, k) * (NX * NH) + mp_of(x2, h2)
                        moves.append((src, dst))
    return moves


def tied(*values):
    return lax.optimization_barrier(values)


def sum_shares(where, y, other, weight, own_extra, fillers):
    got = [lax.ppermute(other[d], "mp", x_shift(d)) for d in (1, 3, 2)]
    if fillers:
        held = tied(*got, *fillers)
        got, fillers = held[:3], held[3:]
    total_other = other[0].astype(F32)
    for piece in got:
        total_other = total_other + piece.astype(F32)
    total_other, *mine = tied(total_other.astype(BF16), *shares(where, y, weight, 0))
    crossed = lax.ppermute(total_other, "mp", H_SWAP)
    got_mine = [lax.ppermute(mine[d], "mp", x_shift(d)) for d in (1, 3, 2)]
    total = own_extra.astype(F32) + mine[0].astype(F32)
    for piece in got_mine:
        total = total + piece.astype(F32)
    return (total + crossed.astype(F32)).astype(BF16), fillers


def body(
    query_mr, key_mr, value_mr, featurizer_mr, mr_taps, out_mr,
    residual, in_weight, featurizer_li, li_rates, li_residues, out_li,
):
    ctx = lax.axis_index("ctx")
    mp = lax.axis_index("mp")
    x, zh = mp // NH, mp % NH
    y, zl, k = ctx // (NZ * NC), (ctx // NC) % NZ, ctx % NC
    where = jnp.stack([x, zh, y, zl, k]).astype(jnp.int32)

    forward = [(i, i + 1) for i in range(NY * NZ * NC - 1)]
    moved = lax.ppermute(in_weight, ("ctx", "mp"), weight_moves())
    halo = lax.ppermute(rim_rows(query_mr, key_mr, value_mr), "ctx", forward)
    toep_mr = toeplitz(mr_taps)
    gated_one, *other_one = mr_op(
        where, query_mr, key_mr, value_mr, halo, featurizer_mr, toep_mr, out_mr
    )
    *other_one, moved = tied(*other_one, moved)
    weights = lax.all_gather(moved, "ctx")
    hidden, _ = sum_shares(where, gated_one, other_one, out_mr, residual, ())
    filters = prep(li_rates.T, li_residues.T)

    crossed = lax.ppermute(hidden, "mp", H_SWAP)
    own_pieces = [hidden] + [lax.ppermute(hidden, "mp", x_shift(d)) for d in (1, 3, 2)]
    crossed, *filters = tied(crossed, *filters)
    toep_li, leave, enter, lane_rates = filters
    far_pieces = [crossed] + [lax.ppermute(crossed, "mp", x_shift(d)) for d in (1, 3, 2)]
    pieces = own_pieces + far_pieces
    fresh_k, fresh_v = project(where, pieces, weights, (0, 1), (1, 2))
    halo_kv = lax.ppermute(
        jnp.concatenate([fresh_k[ROWS - 16 :], fresh_v[ROWS - 16 :]], axis=0), "ctx", forward
    )
    product, load = li_gate(fresh_k, fresh_v, halo_kv, featurizer_li, enter)
    other_load = lax.ppermute(load, "ctx", CORE_SWAP)
    chip = chip_state(where, load, other_load, lane_rates)
    before = [lax.ppermute(chip, "ctx", z_shift(s)) for s in (1, 2, 3)]
    line_total, line_carry = line_state(where, [chip] + before, lane_rates)
    above = []
    for s in (1, 2, 3):
        pairs = [
            (ctx_of(a, b, c), ctx_of(a + s, b, c))
            for a in range(NY - s) for b in range(NZ) for c in range(NC)
        ]
        above.append(lax.ppermute(line_total, "ctx", pairs))

    (fresh_q,) = project(where, pieces, weights, (0, 1), (0,))
    halo_q = lax.ppermute(fresh_q[ROWS - 16 :], "ctx", forward)
    conv = li_inner(product, toep_li)

    gated_two, *other_two = li_outer(
        where, conv, fresh_q, halo_q, featurizer_li, leave, lane_rates,
        line_carry, other_load, above, out_li,
    )
    return sum_shares(where, gated_two, other_two, out_li, hidden, ())[0]


def solution(mesh):
    return jax.shard_map(
        body,
        mesh=mesh,
        in_specs=(
            P("ctx", "mp"),
            P("ctx", "mp"),
            P("ctx", "mp"),
            P(None, None, "mp"),
            P(None, "mp"),
            P("mp", None),
            P("ctx", "mp"),
            P(None, "mp", "ctx"),
            P(None, None, "mp"),
            P("mp", None),
            P("mp", None),
            P("mp", None),
        ),
        out_specs=P("ctx", "mp"),
        check_vma=False,
    )
```

```python
import functools
import jax
import jax.numpy as jnp
from jax import lax
from jax.experimental import pallas as pl
from jax.experimental.pallas import tpu as pltpu
from jax.sharding import PartitionSpec as P

F32 = jnp.float32
BF16 = jnp.bfloat16
GS = 16
LANES = 128
NG = LANES // GS
ROWS = 256
WIDTH = 512
HALO = 144


def params(mib=24):
    return pltpu.CompilerParams(vmem_limit_bytes=mib * 1024 * 1024)


def vspecs(n):
    return [pl.BlockSpec(memory_space=pltpu.VMEM)] * n


def hspecs(n):
    return [pl.BlockSpec(memory_space=pltpu.HBM)] * n


SMEM_SPEC = pl.BlockSpec(memory_space=pltpu.SMEM)


def own_lanes(group):
    lane = lax.broadcasted_iota(jnp.int32, (1, LANES), 1)
    return (lane // GS) == group


NY, NZ, NC, NX, NH = 4, 4, 2, 4, 2

def rim_kernel(q_ref, k_ref, v_ref, out_ref, q_out, k_out, v_out, sems):
    parts = ((k_ref, HALO, 0), (v_ref, HALO, HALO), (q_ref, 16, 2 * HALO))
    copies = []
    for i, (ref, depth, at) in enumerate(parts):
        copy = pltpu.make_async_copy(
            ref.at[pl.ds(ROWS - depth, depth)], out_ref.at[pl.ds(at, depth)], sems.at[i]
        )
        copy.start()
        copies.append(copy)
    for i, (ref, out) in enumerate(((q_ref, q_out), (k_ref, k_out), (v_ref, v_out))):
        copy = pltpu.make_async_copy(ref, out, sems.at[3 + i])
        copy.start()
        copies.append(copy)
    for copy in copies:
        copy.wait()


def rim_rows(q, k, v):
    return pl.pallas_call(
        rim_kernel,
        out_shape=[jax.ShapeDtypeStruct((2 * HALO + 16, WIDTH), BF16)] + [PIECE] * 3,
        in_specs=hspecs(3),
        out_specs=vspecs(4),
        scratch_shapes=[pltpu.SemaphoreType.DMA((6,))],
        compiler_params=params(),
        name="rim_rows",
    )(q, k, v)


OVER_FIRST = (((0,), (0,)), ((), ()))


def exact(a, b):
    return lax.dot_general(a, b, OVER_FIRST, preferred_element_type=F32, precision=lax.Precision.HIGHEST)


def toeplitz_rows(near, far):
    row = lax.broadcasted_iota(jnp.int32, (LANES, LANES), 0)
    col = lax.broadcasted_iota(jnp.int32, (LANES, LANES), 1)
    near = pltpu.roll(jnp.broadcast_to(near, (LANES, LANES)), 0, 1, stride=1, stride_axis=0)
    upper = near
    if far is not None:
        far = pltpu.roll(jnp.broadcast_to(far, (LANES, LANES)), 0, 1, stride=1, stride_axis=0)
    else:
        far = 0.0
    upper = jnp.where(col > row, near, far).astype(BF16)
    lower = jnp.where(col <= row, near, 0.0).astype(BF16)
    return upper, lower


def toeplitz_kernel(taps_ref, out_ref, near):
    tap = lax.broadcasted_iota(jnp.int32, (LANES, LANES), 0)
    at = lax.broadcasted_iota(jnp.int32, (LANES, LANES), 1)
    near[...] = exact(taps_ref[...], jnp.where(tap == lax.rem(LANES - at, LANES), 1.0, 0.0))

    def one(g, carry):
        upper, lower = toeplitz_rows(near[pl.ds(g, 1), :], None)
        start = pl.multiple_of(g * LANES, LANES)
        out_ref[pl.ds(start, LANES), 0:LANES] = upper
        out_ref[pl.ds(start, LANES), LANES:] = lower
        return carry

    lax.fori_loop(0, near.shape[0], one, 0)


def toeplitz(taps):
    groups = taps.shape[1]
    return pl.pallas_call(
        toeplitz_kernel,
        out_shape=jax.ShapeDtypeStruct((groups * LANES, 2 * LANES), BF16),
        in_specs=vspecs(1),
        out_specs=pl.BlockSpec(memory_space=pltpu.VMEM),
        scratch_shapes=[pltpu.VMEM((groups, LANES), F32)],
        compiler_params=params(),
        name="toeplitz",
    )(taps)


def prep_kernel(rates_ref, res_ref, toep_ref, leave_ref, enter_ref, lane_ref, near, far):
    modes, groups = rates_ref.shape
    mode_r = lax.broadcasted_iota(jnp.int32, (modes, modes), 0)
    mode_c = lax.broadcasted_iota(jnp.int32, (modes, modes), 1)
    same = jnp.where(mode_r == mode_c, 1.0, 0.0)
    rates = exact(rates_ref[...], same)
    weights = exact(res_ref[...], same)
    back = lax.broadcasted_iota(jnp.int32, (groups, LANES), 1)
    back = jnp.where(back == 0, 0, LANES - back).astype(F32)
    near_sum = jnp.zeros((groups, LANES), F32)
    far_sum = jnp.zeros((groups, LANES), F32)
    for n in range(GS):
        rate = rates[:, n : n + 1]
        weight = weights[:, n : n + 1]
        near_sum = near_sum + weight * jnp.exp(-rate * back)
        far_sum = far_sum + weight * jnp.exp(-rate * (back + LANES))
    near[...] = near_sum
    far[...] = far_sum

    def one(g, carry):
        upper, lower = toeplitz_rows(near[pl.ds(g, 1), :], far[pl.ds(g, 1), :])
        start = pl.multiple_of(g * LANES, LANES)
        toep_ref[pl.ds(start, LANES), 0:LANES] = upper
        toep_ref[pl.ds(start, LANES), LANES:] = lower
        return carry

    lax.fori_loop(0, groups, one, 0)
    lane = lax.broadcasted_iota(jnp.int32, (groups, WIDTH), 1)
    member = lax.broadcasted_iota(jnp.int32, (groups, WIDTH), 0)
    pick = jnp.where(lane // GS == member, 1.0, 0.0)
    lane_rates = exact(rates, pick)
    lane_ref[...] = lane_rates
    lane = lax.broadcasted_iota(jnp.int32, (modes, WIDTH), 1)
    member = lax.broadcasted_iota(jnp.int32, (modes, WIDTH), 0)
    ours = lax.rem(lane, GS) == member
    rate_row = jnp.sum(jnp.where(ours, lane_rates, 0.0), axis=0, keepdims=True)
    weight_row = jnp.sum(jnp.where(ours, exact(weights, pick), 0.0), axis=0, keepdims=True)
    step = lax.broadcasted_iota(jnp.int32, (ROWS, LANES), 0).astype(F32)
    for block in range(WIDTH // LANES):
        cols = slice(block * LANES, (block + 1) * LANES)
        rate = rate_row[:, cols]
        leave_ref[:, cols] = weight_row[:, cols] * jnp.exp(-rate * step)
        enter_ref[:, cols] = jnp.exp(-rate * (ROWS - step))


def prep(rates, residues):
    groups = rates.shape[1]
    return pl.pallas_call(
        prep_kernel,
        out_shape=[
            jax.ShapeDtypeStruct((groups * LANES, 2 * LANES), BF16),
            jax.ShapeDtypeStruct((ROWS, WIDTH), F32),
            jax.ShapeDtypeStruct((ROWS, WIDTH), F32),
            jax.ShapeDtypeStruct((GS, WIDTH), F32),
        ],
        in_specs=vspecs(2),
        out_specs=vspecs(4),
        scratch_shapes=[pltpu.VMEM((groups, LANES), F32)] * 2,
        compiler_params=params(),
        name="prep",
    )(rates, residues)


def feature(ext_ref, base, rows, taps):
    total = taps[0:1] * ext_ref[pl.ds(base, rows), :]
    for k in range(1, 3):
        total = total + taps[k : k + 1] * ext_ref[pl.ds(base - k, rows), :]
    return total


def filtered(toep_ref, block, early, middle, late):
    rhs = jnp.concatenate(
        [
            jnp.concatenate([early, middle], axis=0),
            jnp.concatenate([middle, late], axis=0),
        ],
        axis=1,
    )
    top = jnp.zeros((LANES, LANES), F32)
    low = jnp.zeros((LANES, LANES), F32)
    for g in range(NG):
        start = (block * NG + g) * LANES
        prod = jnp.dot(toep_ref[start : start + LANES, :], rhs, preferred_element_type=F32)
        mine = own_lanes(g)
        top = jnp.where(mine, prod[:, :LANES], top)
        low = jnp.where(mine, prod[:, LANES:], low)
    return top, low


def share_loads(where_ref, w_ref, wbuf, sems, flip):
    x = where_ref[0]
    zh = where_ref[1]
    half = zh if flip == 0 else 1 - zh
    copies = []
    for d in range(4):
        block = lax.rem(x + d, 4) * 2 + half
        copy = pltpu.make_async_copy(
            w_ref.at[:, pl.ds(pl.multiple_of(block * WIDTH, WIDTH), WIDTH)], wbuf.at[d], sems.at[d]
        )
        copy.start()
        copies.append(copy)
    return copies


def share_products(copies, y_ref, wbuf, outs):
    for d in (1, 3, 2, 0):
        copies[d].wait()
        outs[d][...] = jnp.dot(y_ref[...], wbuf[d], preferred_element_type=F32).astype(BF16)


SHARE_SCRATCH = [pltpu.VMEM((4, WIDTH, WIDTH), BF16), pltpu.SemaphoreType.DMA((4,))]
PIECE = jax.ShapeDtypeStruct((ROWS, WIDTH), BF16)


def share_kernel(flip, where_ref, y_ref, w_ref, o0, o1, o2, o3, wbuf, sems):
    copies = share_loads(where_ref, w_ref, wbuf, sems, flip)
    share_products(copies, y_ref, wbuf, (o0, o1, o2, o3))


def shares(where, y, weight, flip):
    return pl.pallas_call(
        functools.partial(share_kernel, flip),
        out_shape=[PIECE] * 4,
        in_specs=[SMEM_SPEC] + vspecs(1) + hspecs(1),
        out_specs=vspecs(4),
        scratch_shapes=SHARE_SCRATCH,
        compiler_params=params(48),
        name="shares",
    )(where, y, weight)


def mr_kernel(
    where_ref, q_ref, k_ref, v_ref, halo_ref, feat_ref, toep_ref, w_ref,
    y_ref, o0, o1, o2, o3, kx, vx, qx, wbuf, sems,
):
    copies = share_loads(where_ref, w_ref, wbuf, sems, 1)
    for block in range(WIDTH // LANES):
        cols = slice(block * LANES, (block + 1) * LANES)
        kx[0:HALO, :] = halo_ref[0:HALO, cols].astype(F32)
        kx[HALO:, :] = k_ref[:, cols].astype(F32)
        vx[0:HALO, :] = halo_ref[HALO : 2 * HALO, cols].astype(F32)
        vx[HALO:, :] = v_ref[:, cols].astype(F32)
        qx[0:16, :] = halo_ref[2 * HALO : 2 * HALO + 16, cols].astype(F32)
        qx[16:, :] = q_ref[:, cols].astype(F32)
        zs = []
        for part in range(3):
            base = HALO - LANES + part * LANES
            kf = feature(kx, base, LANES, feat_ref[1, :, cols])
            vf = feature(vx, base, LANES, feat_ref[2, :, cols])
            zs.append((kf * vf).astype(BF16))
        top, low = filtered(toep_ref, block, *zs)
        for part, conv in ((0, top), (1, low)):
            qf = feature(qx, 16 + part * LANES, LANES, feat_ref[0, :, cols])
            y_ref[part * LANES : (part + 1) * LANES, cols] = (qf * conv).astype(BF16)
    share_products(copies, y_ref, wbuf, (o0, o1, o2, o3))


def mr_op(where, q, k, v, halo, feat, toep, weight):
    return pl.pallas_call(
        mr_kernel,
        out_shape=[PIECE] * 5,
        in_specs=[SMEM_SPEC] + vspecs(6) + hspecs(1),
        out_specs=vspecs(5),
        scratch_shapes=[
            pltpu.VMEM((HALO + ROWS, LANES), F32),
            pltpu.VMEM((HALO + ROWS, LANES), F32),
            pltpu.VMEM((16 + ROWS, LANES), F32),
        ] + SHARE_SCRATCH,
        compiler_params=params(48),
        name="mr_op",
    )(where, q, k, v, halo, feat, toep, weight)


def project_kernel(flips, slots, first, last, where_ref, *refs):
    n = len(flips) * 4
    count = len(slots)
    hidden_refs = refs[:n]
    w_ref = refs[n]
    pos = n + 1
    acc_refs = ()
    if not first:
        acc_refs = refs[pos : pos + count]
        pos += count
    out_refs = refs[pos : pos + count]
    wbuf, wsem = refs[pos + count :]
    x = where_ref[0]
    wcopies = []
    for i in range(n):
        e, d = flips[i // 4], (0, 1, 3, 2)[i % 4]
        src_y = lax.rem(x + 4 - d, 4)
        for b in range(4):
            odd = 1 - b // 2
            high = odd if e == 1 else 1 - odd
            member = gathered_at(src_y, high * 2 + odd, b % 2)
            copy = pltpu.make_async_copy(
                w_ref.at[member, pl.ds(slots[0], count)],
                wbuf.at[i, :, :, pl.ds(b * LANES, LANES)],
                wsem.at[i, b],
            )
            copy.start()
            wcopies.append(copy)
    sums = [None] * count
    for i in range(n):
        for b in range(4):
            wcopies[i * 4 + b].wait()
        for j in range(count):
            prod = jnp.dot(hidden_refs[i][...], wbuf[i, j], preferred_element_type=F32)
            if i == 0:
                sums[j] = prod if first else prod + acc_refs[j][...]
            else:
                sums[j] = sums[j] + prod
    for j in range(count):
        out_refs[j][...] = sums[j].astype(BF16) if last else sums[j]


def project(where, pieces, weights, flips, slots, acc=(), last=True):
    n, count = len(pieces), len(slots)
    return pl.pallas_call(
        functools.partial(project_kernel, flips, slots, not acc, last),
        out_shape=[jax.ShapeDtypeStruct((ROWS, WIDTH), BF16 if last else F32)] * count,
        in_specs=[SMEM_SPEC] + vspecs(n) + hspecs(1) + vspecs(len(acc)),
        out_specs=vspecs(count),
        scratch_shapes=[
            pltpu.VMEM((n, count, WIDTH, WIDTH), BF16),
            pltpu.SemaphoreType.DMA((n, 4)),
        ],
        compiler_params=params(48),
        name="project",
    )(where, *pieces, weights, *acc)


def li_gate_kernel(k_ref, v_ref, halo_ref, feat_ref, enter_ref, z_ref, load_ref, kx, vx):
    for block in range(WIDTH // LANES):
        cols = slice(block * LANES, (block + 1) * LANES)
        kx[0:16, :] = halo_ref[0:16, cols].astype(F32)
        kx[16:, :] = k_ref[:, cols].astype(F32)
        vx[0:16, :] = halo_ref[16:32, cols].astype(F32)
        vx[16:, :] = v_ref[:, cols].astype(F32)
        kf = feature(kx, 16, ROWS, feat_ref[1, :, cols])
        vf = feature(vx, 16, ROWS, feat_ref[2, :, cols])
        z = (kf * vf).astype(BF16)
        z_ref[:, cols] = z
        enter = enter_ref[:, cols]
        high = enter.astype(BF16)
        rest = (enter - high.astype(F32)).astype(BF16)
        prod = lax.dot_general(high, z, OVER_FIRST, preferred_element_type=F32)
        prod = prod + lax.dot_general(rest, z, OVER_FIRST, preferred_element_type=F32)
        load = jnp.zeros((GS, LANES), F32)
        for g in range(NG):
            load = jnp.where(own_lanes(g), prod[g * GS : (g + 1) * GS, :], load)
        load_ref[:, cols] = load


def li_gate(k, v, halo, feat, enter):
    return pl.pallas_call(
        li_gate_kernel,
        out_shape=[PIECE, STATE],
        in_specs=vspecs(5),
        out_specs=vspecs(2),
        scratch_shapes=[pltpu.VMEM((16 + ROWS, LANES), F32)] * 2,
        compiler_params=params(),
        name="li_gate",
    )(k, v, halo, feat, enter)


STATE = jax.ShapeDtypeStruct((GS, WIDTH), F32)


def chip_kernel(where_ref, load_ref, other_ref, rates_ref, chip_ref):
    k = where_ref[4]
    load, other = load_ref[...], other_ref[...]
    fade = jnp.exp(-rates_ref[...] * (1.0 * ROWS))
    chip_ref[...] = jnp.where(k == 0, load * fade + other, other * fade + load)


def chip_state(where, load, other, rates):
    return pl.pallas_call(
        chip_kernel,
        out_shape=STATE,
        in_specs=[SMEM_SPEC] + vspecs(3),
        out_specs=pl.BlockSpec(memory_space=pltpu.VMEM),
        compiler_params=params(),
        name="chip_state",
    )(where, load, other, rates)


def line_kernel(where_ref, c0, c1, c2, c3, rates_ref, total_ref, carry_ref):
    zl = where_ref[3]
    rates = rates_ref[...]
    total = jnp.zeros(rates.shape, F32)
    carry = jnp.zeros(rates.shape, F32)
    for s, ref in enumerate((c0, c1, c2, c3)):
        piece = ref[...]
        src = lax.rem(zl + NZ - s, NZ)
        gap = ((NZ - 1 - src) * (2 * ROWS)).astype(F32)
        total = total + jnp.exp(-rates * gap) * piece
        if s > 0:
            part = jnp.exp(-rates * (2.0 * ROWS * (s - 1))) * piece
            carry = carry + jnp.where(zl >= s, part, 0.0)
    total_ref[...] = total
    carry_ref[...] = carry


def line_state(where, pieces, rates):
    return pl.pallas_call(
        line_kernel,
        out_shape=[STATE] * 2,
        in_specs=[SMEM_SPEC] + vspecs(5),
        out_specs=vspecs(2),
        compiler_params=params(),
        name="line_state",
    )(where, *pieces, rates)


def li_inner_kernel(z_ref, toep_ref, conv_ref):
    for block in range(WIDTH // LANES):
        cols = slice(block * LANES, (block + 1) * LANES)
        first = z_ref[0:LANES, cols]
        second = z_ref[LANES:ROWS, cols]
        top, low = filtered(toep_ref, block, jnp.zeros_like(first), first, second)
        conv_ref[0:LANES, cols] = top
        conv_ref[LANES:ROWS, cols] = low


def li_inner(z, toep):
    return pl.pallas_call(
        li_inner_kernel,
        out_shape=jax.ShapeDtypeStruct((ROWS, WIDTH), F32),
        in_specs=vspecs(2),
        out_specs=pl.BlockSpec(memory_space=pltpu.VMEM),
        compiler_params=params(),
        name="li_inner",
    )(z, toep)


def li_outer_kernel(
    where_ref, conv_ref, q_ref, halo_ref, feat_ref, leave_ref, rates_ref,
    carry_ref, other_ref, y1_ref, y2_ref, y3_ref, w_ref,
    y_ref, o0, o1, o2, o3, qx, wbuf, sems,
):
    copies = share_loads(where_ref, w_ref, wbuf, sems, 1)
    zl, k = where_ref[3], where_ref[4]
    rates = rates_ref[...]
    above = y1_ref[...]
    above = above + jnp.exp(-rates * (2.0 * ROWS * NZ)) * y2_ref[...]
    above = above + jnp.exp(-rates * (4.0 * ROWS * NZ)) * y3_ref[...]
    chip = carry_ref[...] + jnp.exp(-rates * (zl * (2 * ROWS)).astype(F32)) * above
    full = jnp.where(k == 0, chip, jnp.exp(-rates * (1.0 * ROWS)) * chip + other_ref[...])
    for block in range(WIDTH // LANES):
        cols = slice(block * LANES, (block + 1) * LANES)
        qx[0:16, :] = halo_ref[:, cols].astype(F32)
        qx[16:, :] = q_ref[:, cols].astype(F32)
        qf = feature(qx, 16, ROWS, feat_ref[0, :, cols])
        state = full[:, cols]
        spread = jnp.concatenate(
            [jnp.where(own_lanes(g), state, 0.0) for g in range(NG)], axis=0
        )
        outer = jnp.dot(
            leave_ref[:, cols], spread, preferred_element_type=F32, precision=lax.Precision.HIGHEST
        )
        y_ref[:, cols] = (qf * (conv_ref[:, cols] + outer)).astype(BF16)
    share_products(copies, y_ref, wbuf, (o0, o1, o2, o3))


def li_outer(where, conv, q, halo, feat, leave, rates, carry, other, above, weight):
    return pl.pallas_call(
        li_outer_kernel,
        out_shape=[PIECE] * 5,
        in_specs=[SMEM_SPEC] + vspecs(11) + hspecs(1),
        out_specs=vspecs(5),
        scratch_shapes=[pltpu.VMEM((16 + ROWS, LANES), F32)] + SHARE_SCRATCH,
        compiler_params=params(48),
        name="li_outer",
    )(where, conv, q, halo, feat, leave, rates, carry, other, *above, weight)


def ctx_of(y, zl, k):
    return (y * NZ + zl) * NC + k


def mp_of(x, zh):
    return x * NH + zh


def x_shift(by):
    return [(mp_of(x, h), mp_of((x + by) % NX, h)) for x in range(NX) for h in range(NH)]


H_SWAP = [(mp_of(x, h), mp_of(x, 1 - h)) for x in range(NX) for h in range(NH)]
CORE_SWAP = [(i, i ^ 1) for i in range(NY * NZ * NC)]


def z_shift(by):
    return [
        (ctx_of(y, z, k), ctx_of(y, (z + by) % NZ, k))
        for y in range(NY) for z in range(NZ) for k in range(NC)
    ]


def y_shift(by):
    return [
        (ctx_of(y, z, k), ctx_of((y + by) % NY, z, k))
        for y in range(NY) for z in range(NZ) for k in range(NC)
    ]


GATHER_ORDER = [
    ctx_of(y if z % 2 == 0 else NY - 1 - y, z, k)
    for z in range(NZ) for y in range(NY) for k in range(NC)
]


def gathered_at(y, z, k):
    if z % 2 == 1:
        y = NY - 1 - y
    return (z * NY + y) * NC + k


def weight_moves():
    moves = []
    for y in range(NY):
        for zl in range(NZ):
            for k in range(NC):
                for x in range(NX):
                    for h in range(NH):
                        x2, h2, y2 = y, zl // 2, x
                        l0 = zl % 2
                        odd = 1 - l0
                        outer = h ^ h2
                        high = odd if outer else 1 - odd
                        z2 = high * 2 + odd
                        src = ctx_of(y, zl, k) * (NX * NH) + mp_of(x, h)
                        dst = ctx_of(y2, z2, k) * (NX * NH) + mp_of(x2, h2)
                        moves.append((src, dst))
    return moves


def tied(*values):
    return lax.optimization_barrier(values)


def sum_shares(where, y, other, weight, own_extra):
    got = [lax.ppermute(other[d], "mp", x_shift(d)) for d in (1, 3, 2)]
    total_other = other[0].astype(F32)
    for piece in got:
        total_other = total_other + piece.astype(F32)
    total_other, *mine = tied(total_other.astype(BF16), *shares(where, y, weight, 0))
    crossed = lax.ppermute(total_other, "mp", H_SWAP)
    got_mine = [lax.ppermute(mine[d], "mp", x_shift(d)) for d in (1, 3, 2)]
    (total,) = tied(own_extra.astype(F32) + mine[0].astype(F32) + crossed.astype(F32))
    for piece in got_mine:
        total = total + piece.astype(F32)
    return total.astype(BF16)


def body(
    query_mr, key_mr, value_mr, featurizer_mr, mr_taps, out_mr,
    residual, in_weight, featurizer_li, li_rates, li_residues, out_li,
):
    ctx = lax.axis_index("ctx")
    mp = lax.axis_index("mp")
    x, zh = mp // NH, mp % NH
    y, zl, k = ctx // (NZ * NC), (ctx // NC) % NZ, ctx % NC
    where = jnp.stack([x, zh, y, zl, k]).astype(jnp.int32)

    forward = [(i, i + 1) for i in range(NY * NZ * NC - 1)]
    moved = lax.ppermute(in_weight, ("ctx", "mp"), weight_moves())
    rim, query_mr, key_mr, value_mr = rim_rows(query_mr, key_mr, value_mr)
    halo = lax.ppermute(rim, "ctx", forward)
    toep_mr = toeplitz(mr_taps)
    halo, moved, toep_mr = tied(halo, moved, toep_mr)
    weights = lax.all_gather(moved, "ctx", axis_index_groups=[GATHER_ORDER])
    gated_one, *other_one = mr_op(
        where, query_mr, key_mr, value_mr, halo, featurizer_mr, toep_mr, out_mr
    )
    hidden = sum_shares(where, gated_one, other_one, out_mr, residual)
    filters = prep(li_rates.T, li_residues.T)

    crossed = lax.ppermute(hidden, "mp", H_SWAP)
    own_pieces = [hidden] + [lax.ppermute(hidden, "mp", x_shift(d)) for d in (1, 3, 2)]
    crossed, *filters = tied(crossed, *filters)
    toep_li, leave, enter, lane_rates = filters
    far_pieces = [crossed] + [lax.ppermute(crossed, "mp", x_shift(d)) for d in (1, 3, 2)]
    pieces = own_pieces + far_pieces
    fresh_k, fresh_v = project(where, pieces, weights, (0, 1), (1, 2))
    halo_kv = lax.ppermute(
        jnp.concatenate([fresh_k[ROWS - 16 :], fresh_v[ROWS - 16 :]], axis=0), "ctx", forward
    )
    product, load = li_gate(fresh_k, fresh_v, halo_kv, featurizer_li, enter)
    other_load = lax.ppermute(load, "ctx", CORE_SWAP)
    chip = chip_state(where, load, other_load, lane_rates)
    before = [lax.ppermute(chip, "ctx", z_shift(s)) for s in (1, 2, 3)]
    (fresh_q,) = project(where, pieces, weights, (0, 1), (0,))
    conv = li_inner(product, toep_li)
    *before, fresh_q, conv = tied(*before, fresh_q, conv)
    halo_q = lax.ppermute(fresh_q[ROWS - 16 :], "ctx", forward)
    line_total, line_carry = line_state(where, [chip] + before, lane_rates)
    above = []
    for s in (1, 2, 3):
        pairs = [
            (ctx_of(a, b, c), ctx_of(a + s, b, c))
            for a in range(NY - s) for b in range(NZ) for c in range(NC)
        ]
        above.append(lax.ppermute(line_total, "ctx", pairs))

    gated_two, *other_two = li_outer(
        where, conv, fresh_q, halo_q, featurizer_li, leave, lane_rates,
        line_carry, other_load, above, out_li,
    )
    return sum_shares(where, gated_two, other_two, out_li, hidden)


def solution(mesh):
    return jax.shard_map(
        body,
        mesh=mesh,
        in_specs=(
            P("ctx", "mp"),
            P("ctx", "mp"),
            P("ctx", "mp"),
            P(None, None, "mp"),
            P(None, "mp"),
            P("mp", None),
            P("ctx", "mp"),
            P(None, "mp", "ctx"),
            P(None, None, "mp"),
            P("mp", None),
            P("mp", None),
            P("mp", None),
        ),
        out_specs=P("ctx", "mp"),
        check_vma=False,
    )
```

```python
import functools
import jax
import jax.numpy as jnp
from jax import lax
from jax.experimental import pallas as pl
from jax.experimental.pallas import tpu as pltpu
from jax.sharding import PartitionSpec as P

F32 = jnp.float32
BF16 = jnp.bfloat16
GS = 16
LANES = 128
NG = LANES // GS
ROWS = 256
WIDTH = 512
HALO = 144


def params(mib=16):
    return pltpu.CompilerParams(vmem_limit_bytes=mib * 1024 * 1024)


def vspecs(n):
    return [pl.BlockSpec(memory_space=pltpu.VMEM)] * n


def hspecs(n):
    return [pl.BlockSpec(memory_space=pltpu.HBM)] * n


SMEM_SPEC = pl.BlockSpec(memory_space=pltpu.SMEM)


def own_lanes(group):
    lane = lax.broadcasted_iota(jnp.int32, (1, LANES), 1)
    return (lane // GS) == group


NY, NZ, NC, NX, NH = 4, 4, 2, 4, 2

def rim_kernel(q_ref, k_ref, v_ref, out_ref, q_out, k_out, v_out, sems):
    parts = ((k_ref, HALO, 0), (v_ref, HALO, HALO), (q_ref, 16, 2 * HALO))
    copies = []
    for i, (ref, depth, at) in enumerate(parts):
        copy = pltpu.make_async_copy(
            ref.at[pl.ds(ROWS - depth, depth)], out_ref.at[pl.ds(at, depth)], sems.at[i]
        )
        copy.start()
        copies.append(copy)
    for i, (ref, out) in enumerate(((q_ref, q_out), (k_ref, k_out), (v_ref, v_out))):
        copy = pltpu.make_async_copy(ref, out, sems.at[3 + i])
        copy.start()
        copies.append(copy)
    for copy in copies:
        copy.wait()


def rim_rows(q, k, v):
    return pl.pallas_call(
        rim_kernel,
        out_shape=[jax.ShapeDtypeStruct((2 * HALO + 16, WIDTH), BF16)] + [PIECE] * 3,
        in_specs=hspecs(3),
        out_specs=vspecs(4),
        scratch_shapes=[pltpu.SemaphoreType.DMA((6,))],
        compiler_params=params(),
        name="rim_rows",
    )(q, k, v)


OVER_FIRST = (((0,), (0,)), ((), ()))


def exact(a, b):
    return lax.dot_general(a, b, OVER_FIRST, preferred_element_type=F32, precision=lax.Precision.HIGHEST)


def toeplitz_rows(near, far):
    row = lax.broadcasted_iota(jnp.int32, (LANES, LANES), 0)
    col = lax.broadcasted_iota(jnp.int32, (LANES, LANES), 1)
    near = pltpu.roll(jnp.broadcast_to(near, (LANES, LANES)), 0, 1, stride=1, stride_axis=0)
    upper = near
    if far is not None:
        far = pltpu.roll(jnp.broadcast_to(far, (LANES, LANES)), 0, 1, stride=1, stride_axis=0)
    else:
        far = 0.0
    upper = jnp.where(col > row, near, far).astype(BF16)
    lower = jnp.where(col <= row, near, 0.0).astype(BF16)
    return upper, lower


def toeplitz_kernel(taps_ref, out_ref, near):
    tap = lax.broadcasted_iota(jnp.int32, (LANES, LANES), 0)
    at = lax.broadcasted_iota(jnp.int32, (LANES, LANES), 1)
    near[...] = exact(taps_ref[...], jnp.where(tap == lax.rem(LANES - at, LANES), 1.0, 0.0))

    def one(g, carry):
        upper, lower = toeplitz_rows(near[pl.ds(g, 1), :], None)
        start = pl.multiple_of(g * LANES, LANES)
        out_ref[pl.ds(start, LANES), 0:LANES] = upper
        out_ref[pl.ds(start, LANES), LANES:] = lower
        return carry

    lax.fori_loop(0, near.shape[0], one, 0)


def toeplitz(taps):
    groups = taps.shape[1]
    return pl.pallas_call(
        toeplitz_kernel,
        out_shape=jax.ShapeDtypeStruct((groups * LANES, 2 * LANES), BF16),
        in_specs=vspecs(1),
        out_specs=pl.BlockSpec(memory_space=pltpu.VMEM),
        scratch_shapes=[pltpu.VMEM((groups, LANES), F32)],
        compiler_params=params(),
        name="toeplitz",
    )(taps)


def prep_kernel(rates_ref, res_ref, toep_ref, leave_ref, enter_ref, lane_ref, near, far):
    modes, groups = rates_ref.shape
    mode_r = lax.broadcasted_iota(jnp.int32, (modes, modes), 0)
    mode_c = lax.broadcasted_iota(jnp.int32, (modes, modes), 1)
    same = jnp.where(mode_r == mode_c, 1.0, 0.0)
    rates = exact(rates_ref[...], same)
    weights = exact(res_ref[...], same)
    back = lax.broadcasted_iota(jnp.int32, (groups, LANES), 1)
    back = jnp.where(back == 0, 0, LANES - back).astype(F32)
    near_sum = jnp.zeros((groups, LANES), F32)
    far_sum = jnp.zeros((groups, LANES), F32)
    for n in range(GS):
        rate = rates[:, n : n + 1]
        weight = weights[:, n : n + 1]
        near_sum = near_sum + weight * jnp.exp(-rate * back)
        far_sum = far_sum + weight * jnp.exp(-rate * (back + LANES))
    near[...] = near_sum
    far[...] = far_sum

    def one(g, carry):
        upper, lower = toeplitz_rows(near[pl.ds(g, 1), :], far[pl.ds(g, 1), :])
        start = pl.multiple_of(g * LANES, LANES)
        toep_ref[pl.ds(start, LANES), 0:LANES] = upper
        toep_ref[pl.ds(start, LANES), LANES:] = lower
        return carry

    lax.fori_loop(0, groups, one, 0)
    lane = lax.broadcasted_iota(jnp.int32, (groups, WIDTH), 1)
    member = lax.broadcasted_iota(jnp.int32, (groups, WIDTH), 0)
    pick = jnp.where(lane // GS == member, 1.0, 0.0)
    lane_rates = exact(rates, pick)
    lane_ref[...] = lane_rates
    lane = lax.broadcasted_iota(jnp.int32, (modes, WIDTH), 1)
    member = lax.broadcasted_iota(jnp.int32, (modes, WIDTH), 0)
    ours = lax.rem(lane, GS) == member
    rate_row = jnp.sum(jnp.where(ours, lane_rates, 0.0), axis=0, keepdims=True)
    weight_row = jnp.sum(jnp.where(ours, exact(weights, pick), 0.0), axis=0, keepdims=True)
    step = lax.broadcasted_iota(jnp.int32, (ROWS, LANES), 0).astype(F32)
    for block in range(WIDTH // LANES):
        cols = slice(block * LANES, (block + 1) * LANES)
        rate = rate_row[:, cols]
        leave_ref[:, cols] = weight_row[:, cols] * jnp.exp(-rate * step)
        enter_ref[:, cols] = jnp.exp(-rate * (ROWS - step))


def prep(rates, residues):
    groups = rates.shape[1]
    return pl.pallas_call(
        prep_kernel,
        out_shape=[
            jax.ShapeDtypeStruct((groups * LANES, 2 * LANES), BF16),
            jax.ShapeDtypeStruct((ROWS, WIDTH), F32),
            jax.ShapeDtypeStruct((ROWS, WIDTH), F32),
            jax.ShapeDtypeStruct((GS, WIDTH), F32),
        ],
        in_specs=vspecs(2),
        out_specs=vspecs(4),
        scratch_shapes=[pltpu.VMEM((groups, LANES), F32)] * 2,
        compiler_params=params(),
        name="prep",
    )(rates, residues)


def feature(ext_ref, base, rows, taps):
    total = taps[0:1] * ext_ref[pl.ds(base, rows), :]
    for k in range(1, 3):
        total = total + taps[k : k + 1] * ext_ref[pl.ds(base - k, rows), :]
    return total


def filtered(toep_ref, block, early, middle, late):
    rhs = jnp.concatenate(
        [
            jnp.concatenate([early, middle], axis=0),
            jnp.concatenate([middle, late], axis=0),
        ],
        axis=1,
    )
    top = jnp.zeros((LANES, LANES), F32)
    low = jnp.zeros((LANES, LANES), F32)
    for g in range(NG):
        start = (block * NG + g) * LANES
        prod = jnp.dot(toep_ref[start : start + LANES, :], rhs, preferred_element_type=F32)
        mine = own_lanes(g)
        top = jnp.where(mine, prod[:, :LANES], top)
        low = jnp.where(mine, prod[:, LANES:], low)
    return top, low


def share_loads(where_ref, w_ref, wbuf, sems, flip):
    x = where_ref[0]
    zh = where_ref[1]
    half = zh if flip == 0 else 1 - zh
    copies = []
    for d in range(4):
        block = lax.rem(x + d, 4) * 2 + half
        copy = pltpu.make_async_copy(
            w_ref.at[:, pl.ds(pl.multiple_of(block * WIDTH, WIDTH), WIDTH)], wbuf.at[d], sems.at[d]
        )
        copy.start()
        copies.append(copy)
    return copies


def share_products(copies, y_ref, wbuf, outs):
    for d in (1, 3, 2, 0):
        copies[d].wait()
        outs[d][...] = jnp.dot(y_ref[...], wbuf[d], preferred_element_type=F32).astype(BF16)


SHARE_SCRATCH = [pltpu.VMEM((4, WIDTH, WIDTH), BF16), pltpu.SemaphoreType.DMA((4,))]
PIECE = jax.ShapeDtypeStruct((ROWS, WIDTH), BF16)


def share_kernel(flip, where_ref, y_ref, w_ref, o0, o1, o2, o3, wbuf, sems):
    copies = share_loads(where_ref, w_ref, wbuf, sems, flip)
    share_products(copies, y_ref, wbuf, (o0, o1, o2, o3))


def shares(where, y, weight, flip):
    return pl.pallas_call(
        functools.partial(share_kernel, flip),
        out_shape=[PIECE] * 4,
        in_specs=[SMEM_SPEC] + vspecs(1) + hspecs(1),
        out_specs=vspecs(4),
        scratch_shapes=SHARE_SCRATCH,
        compiler_params=params(52),
        name="shares",
    )(where, y, weight)


def mr_kernel(
    where_ref, q_ref, k_ref, v_ref, halo_ref, feat_ref, toep_ref, w_ref,
    y_ref, o0, o1, o2, o3, kx, vx, qx, wbuf, sems,
):
    copies = share_loads(where_ref, w_ref, wbuf, sems, 1)
    for block in range(WIDTH // LANES):
        cols = slice(block * LANES, (block + 1) * LANES)
        kx[0:HALO, :] = halo_ref[0:HALO, cols].astype(F32)
        kx[HALO:, :] = k_ref[:, cols].astype(F32)
        vx[0:HALO, :] = halo_ref[HALO : 2 * HALO, cols].astype(F32)
        vx[HALO:, :] = v_ref[:, cols].astype(F32)
        qx[0:16, :] = halo_ref[2 * HALO : 2 * HALO + 16, cols].astype(F32)
        qx[16:, :] = q_ref[:, cols].astype(F32)
        zs = []
        for part in range(3):
            base = HALO - LANES + part * LANES
            kf = feature(kx, base, LANES, feat_ref[1, :, cols])
            vf = feature(vx, base, LANES, feat_ref[2, :, cols])
            zs.append((kf * vf).astype(BF16))
        top, low = filtered(toep_ref, block, *zs)
        for part, conv in ((0, top), (1, low)):
            qf = feature(qx, 16 + part * LANES, LANES, feat_ref[0, :, cols])
            y_ref[part * LANES : (part + 1) * LANES, cols] = (qf * conv).astype(BF16)
    share_products(copies, y_ref, wbuf, (o0, o1, o2, o3))


def mr_op(where, q, k, v, halo, feat, toep, weight):
    return pl.pallas_call(
        mr_kernel,
        out_shape=[PIECE] * 5,
        in_specs=[SMEM_SPEC] + vspecs(6) + hspecs(1),
        out_specs=vspecs(5),
        scratch_shapes=[
            pltpu.VMEM((HALO + ROWS, LANES), F32),
            pltpu.VMEM((HALO + ROWS, LANES), F32),
            pltpu.VMEM((16 + ROWS, LANES), F32),
        ] + SHARE_SCRATCH,
        compiler_params=params(52),
        name="mr_op",
    )(where, q, k, v, halo, feat, toep, weight)


def pack_kernel(*refs):
    for i in range(8):
        refs[8][i] = refs[i][...]


def packed(pieces):
    return pl.pallas_call(
        pack_kernel,
        out_shape=jax.ShapeDtypeStruct((8, ROWS, WIDTH), BF16),
        in_specs=vspecs(8),
        out_specs=pl.BlockSpec(memory_space=pltpu.VMEM),
        compiler_params=params(),
        name="packed",
    )(*pieces)


def project_kernel(count, sources, where_ref, *refs):
    hidden_ref = refs[0]
    n = len(sources)
    weight_refs = refs[1 : 1 + n]
    out_refs = refs[1 + n : 1 + n + count]
    wbuf, wsem = refs[1 + n + count :]
    x, zh, y, zl, k = [where_ref[i] for i in range(5)]
    for ref, members in zip(weight_refs, sources):
        for at, (sy, sz, sk) in members:
            if at is None:
                src_y, src_z, src_k = sy, sz, sk
                at = (src_z * NY + (NY - 1 - src_y if src_z % 2 else src_y)) * NC + src_k
            else:
                src_y = lax.rem(y + NY - sy, NY)
                src_z = lax.bitwise_xor(zl, jnp.int32(sz))
                src_k = lax.bitwise_xor(k, jnp.int32(sk))
            odd = lax.rem(jnp.int32(src_z), 2)
            high = lax.div(jnp.int32(src_z), 2)
            outer = jnp.where(odd == high, 1, 0)
            piece = outer * 4 + lax.rem(x + 4 - src_y, 4)
            block = (1 - odd) * 2 + src_k
            pltpu.make_async_copy(
                ref.at[at],
                wbuf.at[piece, :, :, pl.ds(pl.multiple_of(block * LANES, LANES), LANES)],
                wsem.at[piece, block],
            ).start()
    sums = [None] * count
    for i in range(8):
        for b in range(4):
            pltpu.make_async_copy(
                weight_refs[0].at[0], wbuf.at[i, :, :, pl.ds(b * LANES, LANES)], wsem.at[i, b]
            ).wait()
        for j in range(count):
            prod = jnp.dot(hidden_ref[i], wbuf[i, j], preferred_element_type=F32)
            sums[j] = prod if i == 0 else sums[j] + prod
    for j in range(count):
        out_refs[j][...] = sums[j].astype(BF16)


PERMUTED = [[(sz, (sy, sz, sk)) for sz in range(4)] for sk in range(2) for sy in range(4)]
GATHERED = [[(None, (sy, sz, sk)) for sy in range(4) for sz in range(4) for sk in range(2)]]


def project(where, pieces, weights, sources, count):
    return pl.pallas_call(
        functools.partial(project_kernel, count, sources),
        out_shape=[PIECE] * count,
        in_specs=[SMEM_SPEC] + vspecs(1) + hspecs(len(weights)),
        out_specs=vspecs(count),
        scratch_shapes=[
            pltpu.VMEM((8, count, WIDTH, WIDTH), BF16),
            pltpu.SemaphoreType.DMA((8, 4)),
        ],
        compiler_params=params(48),
        name="project",
    )(where, pieces, *weights)


def li_gate_kernel(k_ref, v_ref, halo_ref, feat_ref, enter_ref, z_ref, load_ref, kx, vx):
    for block in range(WIDTH // LANES):
        cols = slice(block * LANES, (block + 1) * LANES)
        kx[0:16, :] = halo_ref[0:16, cols].astype(F32)
        kx[16:, :] = k_ref[:, cols].astype(F32)
        vx[0:16, :] = halo_ref[16:32, cols].astype(F32)
        vx[16:, :] = v_ref[:, cols].astype(F32)
        kf = feature(kx, 16, ROWS, feat_ref[1, :, cols])
        vf = feature(vx, 16, ROWS, feat_ref[2, :, cols])
        z = (kf * vf).astype(BF16)
        z_ref[:, cols] = z
        enter = enter_ref[:, cols]
        high = enter.astype(BF16)
        rest = (enter - high.astype(F32)).astype(BF16)
        prod = lax.dot_general(high, z, OVER_FIRST, preferred_element_type=F32)
        prod = prod + lax.dot_general(rest, z, OVER_FIRST, preferred_element_type=F32)
        load = jnp.zeros((GS, LANES), F32)
        for g in range(NG):
            load = jnp.where(own_lanes(g), prod[g * GS : (g + 1) * GS, :], load)
        load_ref[:, cols] = load


def li_gate(k, v, halo, feat, enter):
    return pl.pallas_call(
        li_gate_kernel,
        out_shape=[PIECE, STATE],
        in_specs=vspecs(5),
        out_specs=vspecs(2),
        scratch_shapes=[pltpu.VMEM((16 + ROWS, LANES), F32)] * 2,
        compiler_params=params(),
        name="li_gate",
    )(k, v, halo, feat, enter)


STATE = jax.ShapeDtypeStruct((GS, WIDTH), F32)


def chip_kernel(where_ref, load_ref, other_ref, rates_ref, chip_ref):
    k = where_ref[4]
    load, other = load_ref[...], other_ref[...]
    fade = jnp.exp(-rates_ref[...] * (1.0 * ROWS))
    chip_ref[...] = jnp.where(k == 0, load * fade + other, other * fade + load)


def chip_state(where, load, other, rates):
    return pl.pallas_call(
        chip_kernel,
        out_shape=STATE,
        in_specs=[SMEM_SPEC] + vspecs(3),
        out_specs=pl.BlockSpec(memory_space=pltpu.VMEM),
        compiler_params=params(),
        name="chip_state",
    )(where, load, other, rates)


def line_kernel(where_ref, c0, c1, c2, c3, rates_ref, total_ref, carry_ref):
    zl = where_ref[3]
    rates = rates_ref[...]
    total = jnp.zeros(rates.shape, F32)
    carry = jnp.zeros(rates.shape, F32)
    for s, ref in enumerate((c0, c1, c2, c3)):
        piece = ref[...]
        src = lax.rem(zl + NZ - s, NZ)
        gap = ((NZ - 1 - src) * (2 * ROWS)).astype(F32)
        total = total + jnp.exp(-rates * gap) * piece
        if s > 0:
            part = jnp.exp(-rates * (2.0 * ROWS * (s - 1))) * piece
            carry = carry + jnp.where(zl >= s, part, 0.0)
    total_ref[...] = total
    carry_ref[...] = carry


def line_state(where, pieces, rates):
    return pl.pallas_call(
        line_kernel,
        out_shape=[STATE] * 2,
        in_specs=[SMEM_SPEC] + vspecs(5),
        out_specs=vspecs(2),
        compiler_params=params(),
        name="line_state",
    )(where, *pieces, rates)


def li_inner_kernel(z_ref, toep_ref, conv_ref):
    for block in range(WIDTH // LANES):
        cols = slice(block * LANES, (block + 1) * LANES)
        first = z_ref[0:LANES, cols]
        second = z_ref[LANES:ROWS, cols]
        top, low = filtered(toep_ref, block, jnp.zeros_like(first), first, second)
        conv_ref[0:LANES, cols] = top
        conv_ref[LANES:ROWS, cols] = low


def li_inner(z, toep):
    return pl.pallas_call(
        li_inner_kernel,
        out_shape=jax.ShapeDtypeStruct((ROWS, WIDTH), F32),
        in_specs=vspecs(2),
        out_specs=pl.BlockSpec(memory_space=pltpu.VMEM),
        compiler_params=params(),
        name="li_inner",
    )(z, toep)


def li_outer_kernel(
    where_ref, conv_ref, q_ref, halo_ref, feat_ref, leave_ref, rates_ref,
    carry_ref, other_ref, y1_ref, y2_ref, y3_ref, w_ref,
    y_ref, o0, o1, o2, o3, qx, wbuf, sems,
):
    copies = share_loads(where_ref, w_ref, wbuf, sems, 1)
    zl, k = where_ref[3], where_ref[4]
    rates = rates_ref[...]
    above = y1_ref[...]
    above = above + jnp.exp(-rates * (2.0 * ROWS * NZ)) * y2_ref[...]
    above = above + jnp.exp(-rates * (4.0 * ROWS * NZ)) * y3_ref[...]
    chip = carry_ref[...] + jnp.exp(-rates * (zl * (2 * ROWS)).astype(F32)) * above
    full = jnp.where(k == 0, chip, jnp.exp(-rates * (1.0 * ROWS)) * chip + other_ref[...])
    for block in range(WIDTH // LANES):
        cols = slice(block * LANES, (block + 1) * LANES)
        qx[0:16, :] = halo_ref[:, cols].astype(F32)
        qx[16:, :] = q_ref[:, cols].astype(F32)
        qf = feature(qx, 16, ROWS, feat_ref[0, :, cols])
        state = full[:, cols]
        spread = jnp.concatenate(
            [jnp.where(own_lanes(g), state, 0.0) for g in range(NG)], axis=0
        )
        outer = jnp.dot(
            leave_ref[:, cols], spread, preferred_element_type=F32, precision=lax.Precision.HIGHEST
        )
        y_ref[:, cols] = (qf * (conv_ref[:, cols] + outer)).astype(BF16)
    share_products(copies, y_ref, wbuf, (o0, o1, o2, o3))


def li_outer(where, conv, q, halo, feat, leave, rates, carry, other, above, weight):
    return pl.pallas_call(
        li_outer_kernel,
        out_shape=[PIECE] * 5,
        in_specs=[SMEM_SPEC] + vspecs(11) + hspecs(1),
        out_specs=vspecs(5),
        scratch_shapes=[pltpu.VMEM((16 + ROWS, LANES), F32)] + SHARE_SCRATCH,
        compiler_params=params(52),
        name="li_outer",
    )(where, conv, q, halo, feat, leave, rates, carry, other, *above, weight)


def ctx_of(y, zl, k):
    return (y * NZ + zl) * NC + k


def mp_of(x, zh):
    return x * NH + zh


def x_shift(by):
    return [(mp_of(x, h), mp_of((x + by) % NX, h)) for x in range(NX) for h in range(NH)]


H_SWAP = [(mp_of(x, h), mp_of(x, 1 - h)) for x in range(NX) for h in range(NH)]
CORE_SWAP = [(i, i ^ 1) for i in range(NY * NZ * NC)]


def z_shift(by):
    return [
        (ctx_of(y, z, k), ctx_of(y, (z + by) % NZ, k))
        for y in range(NY) for z in range(NZ) for k in range(NC)
    ]


def y_shift(by):
    return [
        (ctx_of(y, z, k), ctx_of((y + by) % NY, z, k))
        for y in range(NY) for z in range(NZ) for k in range(NC)
    ]


GATHER_ORDER = [
    ctx_of(y if z % 2 == 0 else NY - 1 - y, z, k)
    for z in range(NZ) for y in range(NY) for k in range(NC)
]


def z_swap(by):
    return [
        (ctx_of(y, z, k), ctx_of(y, z ^ by, k))
        for y in range(NY) for z in range(NZ) for k in range(NC)
    ]


def weight_moves():
    moves = []
    for y in range(NY):
        for zl in range(NZ):
            for k in range(NC):
                for x in range(NX):
                    for h in range(NH):
                        x2, h2, y2 = y, zl // 2, x
                        l0 = zl % 2
                        odd = 1 - l0
                        outer = h ^ h2
                        high = odd if outer else 1 - odd
                        z2 = high * 2 + odd
                        src = ctx_of(y, zl, k) * (NX * NH) + mp_of(x, h)
                        dst = ctx_of(y2, z2, k) * (NX * NH) + mp_of(x2, h2)
                        moves.append((src, dst))
    return moves


def tied(*values):
    return lax.optimization_barrier(values)


def sum_shares(where, y, other, weight, own_extra, rider=None):
    got = [lax.ppermute(other[d], "mp", x_shift(d)) for d in (1, 3, 2)]
    total_other = other[0].astype(F32)
    for piece in got:
        total_other = total_other + piece.astype(F32)
    total_other = total_other.astype(BF16)
    mine = shares(where, y, weight, 0)
    if rider is None:
        total_other, *mine = tied(total_other, *mine)
    else:
        total_other, rider, *mine = tied(total_other, rider, *mine)
    crossed = lax.ppermute(total_other, "mp", H_SWAP)
    got_mine = [lax.ppermute(mine[d], "mp", x_shift(d)) for d in (1, 3, 2)]
    (total,) = tied(own_extra.astype(F32) + mine[0].astype(F32) + crossed.astype(F32))
    for piece in got_mine:
        total = total + piece.astype(F32)
    return total.astype(BF16), rider


def body(
    query_mr, key_mr, value_mr, featurizer_mr, mr_taps, out_mr,
    residual, in_weight, featurizer_li, li_rates, li_residues, out_li,
):
    ctx = lax.axis_index("ctx")
    mp = lax.axis_index("mp")
    x, zh = mp // NH, mp % NH
    y, zl, k = ctx // (NZ * NC), (ctx // NC) % NZ, ctx % NC
    where = jnp.stack([x, zh, y, zl, k]).astype(jnp.int32)

    forward = [(i, i + 1) for i in range(NY * NZ * NC - 1)]
    moved_kv = lax.ppermute(in_weight[1:3], ("ctx", "mp"), weight_moves())
    rim, query_mr, key_mr, value_mr = rim_rows(query_mr, key_mr, value_mr)
    halo = lax.ppermute(rim, "ctx", forward)
    toep_mr = toeplitz(mr_taps)
    halo, raw_q, toep_mr = tied(halo, in_weight[0:1], toep_mr)
    gated_one, *other_one = mr_op(
        where, query_mr, key_mr, value_mr, halo, featurizer_mr, toep_mr, out_mr
    )
    *other_one, moved_kv = tied(*other_one, moved_kv)
    weights_kv = lax.all_gather(moved_kv, "ctx", axis_index_groups=[GATHER_ORDER])
    moved_q = lax.ppermute(raw_q, ("ctx", "mp"), weight_moves())
    hidden, moved_q = sum_shares(where, gated_one, other_one, out_mr, residual, moved_q)
    near_q = lax.ppermute(moved_q, "ctx", z_swap(1))
    filters = prep(li_rates.T, li_residues.T)

    hidden, near_q = tied(hidden, near_q)
    crossed = lax.ppermute(hidden, "mp", H_SWAP)
    own_pieces = [lax.ppermute(hidden, "mp", x_shift(d)) for d in (1, 2, 3)]
    pair_q = jnp.stack([moved_q, near_q])
    far_q = lax.ppermute(pair_q, "ctx", z_swap(2))
    crossed, far_q, *held = tied(crossed, far_q, *own_pieces, *filters)
    own_pieces = [hidden] + held[:3]
    toep_li, leave, enter, lane_rates = held[3:]
    far_pieces = [lax.ppermute(crossed, "mp", x_shift(d)) for d in (1, 2, 3)]
    line_q = jnp.concatenate([pair_q, far_q], axis=0)
    up_q = lax.ppermute(line_q, "ctx", y_shift(1))
    down_q = lax.ppermute(line_q, "ctx", y_shift(3))
    up_q, down_q, line_q, *far_pieces = tied(up_q, down_q, line_q, *far_pieces)
    over_q = lax.ppermute(line_q, "ctx", y_shift(2))
    swapped_q = [lax.ppermute(piece, "ctx", CORE_SWAP) for piece in (line_q, up_q, down_q)]
    pieces = packed(own_pieces + [crossed] + far_pieces)
    pieces, line_x, up_x, down_x = tied(pieces, *swapped_q)
    fresh_k, fresh_v = project(where, pieces, [weights_kv], GATHERED, 2)
    halo_kv = lax.ppermute(
        jnp.concatenate([fresh_k[ROWS - 16 :], fresh_v[ROWS - 16 :]], axis=0), "ctx", forward
    )
    product, load = li_gate(fresh_k, fresh_v, halo_kv, featurizer_li, enter)
    load, over_q = tied(load, over_q)
    other_load = lax.ppermute(load, "ctx", CORE_SWAP)
    over_x = lax.ppermute(over_q, "ctx", CORE_SWAP)
    chip = chip_state(where, load, other_load, lane_rates)
    before = [lax.ppermute(chip, "ctx", z_shift(s)) for s in (1, 2, 3)]
    weights_q = [line_q, up_q, over_q, down_q, line_x, up_x, over_x, down_x]
    (fresh_q,) = project(where, pieces, weights_q, PERMUTED, 1)
    conv = li_inner(product, toep_li)
    *before, fresh_q, conv = tied(*before, fresh_q, conv)
    halo_q = lax.ppermute(fresh_q[ROWS - 16 :], "ctx", forward)
    line_total, line_carry = line_state(where, [chip] + before, lane_rates)
    above = []
    for s in (1, 2, 3):
        pairs = [
            (ctx_of(a, b, c), ctx_of(a + s, b, c))
            for a in range(NY - s) for b in range(NZ) for c in range(NC)
        ]
        above.append(lax.ppermute(line_total, "ctx", pairs))

    gated_two, *other_two = li_outer(
        where, conv, fresh_q, halo_q, featurizer_li, leave, lane_rates,
        line_carry, other_load, above, out_li,
    )
    return sum_shares(where, gated_two, other_two, out_li, hidden)[0]


def solution(mesh):
    return jax.shard_map(
        body,
        mesh=mesh,
        in_specs=(
            P("ctx", "mp"),
            P("ctx", "mp"),
            P("ctx", "mp"),
            P(None, None, "mp"),
            P(None, "mp"),
            P("mp", None),
            P("ctx", "mp"),
            P(None, "mp", "ctx"),
            P(None, None, "mp"),
            P("mp", None),
            P("mp", None),
            P("mp", None),
        ),
        out_specs=P("ctx", "mp"),
        check_vma=False,
    )
```

```python
import functools
import jax
import jax.numpy as jnp
from jax import lax
from jax.experimental import pallas as pl
from jax.experimental.pallas import tpu as pltpu
from jax.sharding import PartitionSpec as P

F32 = jnp.float32
BF16 = jnp.bfloat16
GS = 16
LANES = 128
NG = LANES // GS
ROWS = 256
WIDTH = 512
HALO = 144


def params(mib=16):
    return pltpu.CompilerParams(vmem_limit_bytes=mib * 1024 * 1024)


def vspecs(n):
    return [pl.BlockSpec(memory_space=pltpu.VMEM)] * n


def hspecs(n):
    return [pl.BlockSpec(memory_space=pltpu.HBM)] * n


SMEM_SPEC = pl.BlockSpec(memory_space=pltpu.SMEM)


def own_lanes(group):
    lane = lax.broadcasted_iota(jnp.int32, (1, LANES), 1)
    return (lane // GS) == group


NY, NZ, NC, NX, NH = 4, 4, 2, 4, 2

def rim_kernel(q_ref, k_ref, v_ref, out_ref, q_out, k_out, v_out, sems):
    parts = ((k_ref, HALO, 0), (v_ref, HALO, HALO), (q_ref, 16, 2 * HALO))
    copies = []
    for i, (ref, depth, at) in enumerate(parts):
        copy = pltpu.make_async_copy(
            ref.at[pl.ds(ROWS - depth, depth)], out_ref.at[pl.ds(at, depth)], sems.at[i]
        )
        copy.start()
        copies.append(copy)
    for i, (ref, out) in enumerate(((q_ref, q_out), (k_ref, k_out), (v_ref, v_out))):
        copy = pltpu.make_async_copy(ref, out, sems.at[3 + i])
        copy.start()
        copies.append(copy)
    for copy in copies:
        copy.wait()


def rim_rows(q, k, v):
    return pl.pallas_call(
        rim_kernel,
        out_shape=[jax.ShapeDtypeStruct((2 * HALO + 16, WIDTH), BF16)] + [PIECE] * 3,
        in_specs=hspecs(3),
        out_specs=vspecs(4),
        scratch_shapes=[pltpu.SemaphoreType.DMA((6,))],
        compiler_params=params(),
        name="rim_rows",
    )(q, k, v)


OVER_FIRST = (((0,), (0,)), ((), ()))


def exact(a, b):
    return lax.dot_general(a, b, OVER_FIRST, preferred_element_type=F32, precision=lax.Precision.HIGHEST)


def toeplitz_rows(near, far):
    row = lax.broadcasted_iota(jnp.int32, (LANES, LANES), 0)
    col = lax.broadcasted_iota(jnp.int32, (LANES, LANES), 1)
    near = pltpu.roll(jnp.broadcast_to(near, (LANES, LANES)), 0, 1, stride=1, stride_axis=0)
    upper = near
    if far is not None:
        far = pltpu.roll(jnp.broadcast_to(far, (LANES, LANES)), 0, 1, stride=1, stride_axis=0)
    else:
        far = 0.0
    upper = jnp.where(col > row, near, far).astype(BF16)
    lower = jnp.where(col <= row, near, 0.0).astype(BF16)
    return upper, lower


def toeplitz_kernel(taps_ref, out_ref, near):
    tap = lax.broadcasted_iota(jnp.int32, (LANES, LANES), 0)
    at = lax.broadcasted_iota(jnp.int32, (LANES, LANES), 1)
    near[...] = exact(taps_ref[...], jnp.where(tap == lax.rem(LANES - at, LANES), 1.0, 0.0))

    def one(g, carry):
        upper, lower = toeplitz_rows(near[pl.ds(g, 1), :], None)
        start = pl.multiple_of(g * LANES, LANES)
        out_ref[pl.ds(start, LANES), 0:LANES] = upper
        out_ref[pl.ds(start, LANES), LANES:] = lower
        return carry

    lax.fori_loop(0, near.shape[0], one, 0)


def toeplitz(taps):
    groups = taps.shape[1]
    return pl.pallas_call(
        toeplitz_kernel,
        out_shape=jax.ShapeDtypeStruct((groups * LANES, 2 * LANES), BF16),
        in_specs=vspecs(1),
        out_specs=pl.BlockSpec(memory_space=pltpu.VMEM),
        scratch_shapes=[pltpu.VMEM((groups, LANES), F32)],
        compiler_params=params(),
        name="toeplitz",
    )(taps)


def prep_kernel(rates_ref, res_ref, toep_ref, leave_ref, enter_ref, lane_ref, near, far):
    modes, groups = rates_ref.shape
    mode_r = lax.broadcasted_iota(jnp.int32, (modes, modes), 0)
    mode_c = lax.broadcasted_iota(jnp.int32, (modes, modes), 1)
    same = jnp.where(mode_r == mode_c, 1.0, 0.0)
    rates = exact(rates_ref[...], same)
    weights = exact(res_ref[...], same)
    back = lax.broadcasted_iota(jnp.int32, (groups, LANES), 1)
    back = jnp.where(back == 0, 0, LANES - back).astype(F32)
    near_sum = jnp.zeros((groups, LANES), F32)
    far_sum = jnp.zeros((groups, LANES), F32)
    for n in range(GS):
        rate = rates[:, n : n + 1]
        weight = weights[:, n : n + 1]
        near_sum = near_sum + weight * jnp.exp(-rate * back)
        far_sum = far_sum + weight * jnp.exp(-rate * (back + LANES))
    near[...] = near_sum
    far[...] = far_sum

    def one(g, carry):
        upper, lower = toeplitz_rows(near[pl.ds(g, 1), :], far[pl.ds(g, 1), :])
        start = pl.multiple_of(g * LANES, LANES)
        toep_ref[pl.ds(start, LANES), 0:LANES] = upper
        toep_ref[pl.ds(start, LANES), LANES:] = lower
        return carry

    lax.fori_loop(0, groups, one, 0)
    lane = lax.broadcasted_iota(jnp.int32, (groups, WIDTH), 1)
    member = lax.broadcasted_iota(jnp.int32, (groups, WIDTH), 0)
    pick = jnp.where(lane // GS == member, 1.0, 0.0)
    lane_rates = exact(rates, pick)
    lane_ref[...] = lane_rates
    lane = lax.broadcasted_iota(jnp.int32, (modes, WIDTH), 1)
    member = lax.broadcasted_iota(jnp.int32, (modes, WIDTH), 0)
    ours = lax.rem(lane, GS) == member
    rate_row = jnp.sum(jnp.where(ours, lane_rates, 0.0), axis=0, keepdims=True)
    weight_row = jnp.sum(jnp.where(ours, exact(weights, pick), 0.0), axis=0, keepdims=True)
    step = lax.broadcasted_iota(jnp.int32, (ROWS, LANES), 0).astype(F32)
    for block in range(WIDTH // LANES):
        cols = slice(block * LANES, (block + 1) * LANES)
        rate = rate_row[:, cols]
        leave_ref[:, cols] = weight_row[:, cols] * jnp.exp(-rate * step)
        enter_ref[:, cols] = jnp.exp(-rate * (ROWS - step))


def prep(rates, residues):
    groups = rates.shape[1]
    return pl.pallas_call(
        prep_kernel,
        out_shape=[
            jax.ShapeDtypeStruct((groups * LANES, 2 * LANES), BF16),
            jax.ShapeDtypeStruct((ROWS, WIDTH), F32),
            jax.ShapeDtypeStruct((ROWS, WIDTH), F32),
            jax.ShapeDtypeStruct((GS, WIDTH), F32),
        ],
        in_specs=vspecs(2),
        out_specs=vspecs(4),
        scratch_shapes=[pltpu.VMEM((groups, LANES), F32)] * 2,
        compiler_params=params(),
        name="prep",
    )(rates, residues)


def feature(ext_ref, base, rows, taps):
    total = taps[0:1] * ext_ref[pl.ds(base, rows), :]
    for k in range(1, 3):
        total = total + taps[k : k + 1] * ext_ref[pl.ds(base - k, rows), :]
    return total


def filtered(toep_ref, block, early, middle, late):
    rhs = jnp.concatenate(
        [
            jnp.concatenate([early, middle], axis=0),
            jnp.concatenate([middle, late], axis=0),
        ],
        axis=1,
    )
    top = jnp.zeros((LANES, LANES), F32)
    low = jnp.zeros((LANES, LANES), F32)
    for g in range(NG):
        start = (block * NG + g) * LANES
        prod = jnp.dot(toep_ref[start : start + LANES, :], rhs, preferred_element_type=F32)
        mine = own_lanes(g)
        top = jnp.where(mine, prod[:, :LANES], top)
        low = jnp.where(mine, prod[:, LANES:], low)
    return top, low


def share_loads(where_ref, w_ref, wbuf, sems, flip):
    x = where_ref[0]
    zh = where_ref[1]
    half = zh if flip == 0 else 1 - zh
    copies = []
    for d in range(4):
        block = lax.rem(x + d, 4) * 2 + half
        copy = pltpu.make_async_copy(
            w_ref.at[:, pl.ds(pl.multiple_of(block * WIDTH, WIDTH), WIDTH)], wbuf.at[d], sems.at[d]
        )
        copy.start()
        copies.append(copy)
    return copies


def share_products(copies, y_ref, wbuf, outs):
    for d in (1, 3, 2, 0):
        copies[d].wait()
        outs[d][...] = jnp.dot(y_ref[...], wbuf[d], preferred_element_type=F32).astype(BF16)


SHARE_SCRATCH = [pltpu.VMEM((4, WIDTH, WIDTH), BF16), pltpu.SemaphoreType.DMA((4,))]
PIECE = jax.ShapeDtypeStruct((ROWS, WIDTH), BF16)


def share_kernel(flip, where_ref, y_ref, w_ref, o0, o1, o2, o3, wbuf, sems):
    copies = share_loads(where_ref, w_ref, wbuf, sems, flip)
    share_products(copies, y_ref, wbuf, (o0, o1, o2, o3))


def shares(where, y, weight, flip):
    return pl.pallas_call(
        functools.partial(share_kernel, flip),
        out_shape=[PIECE] * 4,
        in_specs=[SMEM_SPEC] + vspecs(1) + hspecs(1),
        out_specs=vspecs(4),
        scratch_shapes=SHARE_SCRATCH,
        compiler_params=params(52),
        name="shares",
    )(where, y, weight)


def mr_kernel(
    where_ref, q_ref, k_ref, v_ref, halo_ref, feat_ref, toep_ref, w_ref,
    y_ref, o0, o1, o2, o3, kx, vx, qx, wbuf, sems,
):
    copies = share_loads(where_ref, w_ref, wbuf, sems, 1)
    for block in range(WIDTH // LANES):
        cols = slice(block * LANES, (block + 1) * LANES)
        kx[0:HALO, :] = halo_ref[0:HALO, cols].astype(F32)
        kx[HALO:, :] = k_ref[:, cols].astype(F32)
        vx[0:HALO, :] = halo_ref[HALO : 2 * HALO, cols].astype(F32)
        vx[HALO:, :] = v_ref[:, cols].astype(F32)
        qx[0:16, :] = halo_ref[2 * HALO : 2 * HALO + 16, cols].astype(F32)
        qx[16:, :] = q_ref[:, cols].astype(F32)
        zs = []
        for part in range(3):
            base = HALO - LANES + part * LANES
            kf = feature(kx, base, LANES, feat_ref[1, :, cols])
            vf = feature(vx, base, LANES, feat_ref[2, :, cols])
            zs.append((kf * vf).astype(BF16))
        top, low = filtered(toep_ref, block, *zs)
        for part, conv in ((0, top), (1, low)):
            qf = feature(qx, 16 + part * LANES, LANES, feat_ref[0, :, cols])
            y_ref[part * LANES : (part + 1) * LANES, cols] = (qf * conv).astype(BF16)
    share_products(copies, y_ref, wbuf, (o0, o1, o2, o3))


def mr_op(where, q, k, v, halo, feat, toep, weight):
    return pl.pallas_call(
        mr_kernel,
        out_shape=[PIECE] * 5,
        in_specs=[SMEM_SPEC] + vspecs(6) + hspecs(1),
        out_specs=vspecs(5),
        scratch_shapes=[
            pltpu.VMEM((HALO + ROWS, LANES), F32),
            pltpu.VMEM((HALO + ROWS, LANES), F32),
            pltpu.VMEM((16 + ROWS, LANES), F32),
        ] + SHARE_SCRATCH,
        compiler_params=params(52),
        name="mr_op",
    )(where, q, k, v, halo, feat, toep, weight)


EXT = 16 + ROWS
EXT_PIECE = jax.ShapeDtypeStruct((EXT, WIDTH), BF16)


def pack_kernel(*refs):
    for i in range(8):
        refs[8][i] = refs[i][...]


def packed(pieces):
    return pl.pallas_call(
        pack_kernel,
        out_shape=jax.ShapeDtypeStruct((8, EXT, WIDTH), BF16),
        in_specs=vspecs(8),
        out_specs=pl.BlockSpec(memory_space=pltpu.VMEM),
        compiler_params=params(),
        name="packed",
    )(*pieces)


def project_kernel(slots, where_ref, hidden_ref, w_ref, *refs):
    count = len(slots)
    out_refs = refs[:count]
    wbuf, wsem = refs[count:]
    x = where_ref[0]
    copies = []
    for i in range(8):
        e, d = i // 4, i % 4
        src_y = lax.rem(x + 4 - d, 4)
        for b in range(4):
            odd = 1 - b // 2
            high = odd if e == 1 else 1 - odd
            copy = pltpu.make_async_copy(
                w_ref.at[gathered_at(src_y, high * 2 + odd, b % 2), pl.ds(slots[0], count)],
                wbuf.at[i, :, :, pl.ds(b * LANES, LANES)],
                wsem.at[i, b],
            )
            copy.start()
            copies.append(copy)
    sums = [None] * count
    for i in range(8):
        for b in range(4):
            copies[i * 4 + b].wait()
        for j in range(count):
            prod = jnp.dot(hidden_ref[i], wbuf[i, j], preferred_element_type=F32)
            sums[j] = prod if i == 0 else sums[j] + prod
    for j in range(count):
        out_refs[j][...] = sums[j].astype(BF16)


def project(where, pieces, weights, slots):
    count = len(slots)
    return pl.pallas_call(
        functools.partial(project_kernel, slots),
        out_shape=[EXT_PIECE] * count,
        in_specs=[SMEM_SPEC] + vspecs(1) + hspecs(1),
        out_specs=vspecs(count),
        scratch_shapes=[
            pltpu.VMEM((8, count, WIDTH, WIDTH), BF16),
            pltpu.SemaphoreType.DMA((8, 4)),
        ],
        compiler_params=params(48),
        name="project",
    )(where, pieces, weights)


def li_gate_kernel(k_ref, v_ref, feat_ref, enter_ref, z_ref, load_ref, kx, vx):
    for block in range(WIDTH // LANES):
        cols = slice(block * LANES, (block + 1) * LANES)
        kx[...] = k_ref[:, cols].astype(F32)
        vx[...] = v_ref[:, cols].astype(F32)
        kf = feature(kx, 16, ROWS, feat_ref[1, :, cols])
        vf = feature(vx, 16, ROWS, feat_ref[2, :, cols])
        z = (kf * vf).astype(BF16)
        z_ref[:, cols] = z
        enter = enter_ref[:, cols]
        high = enter.astype(BF16)
        rest = (enter - high.astype(F32)).astype(BF16)
        prod = lax.dot_general(high, z, OVER_FIRST, preferred_element_type=F32)
        prod = prod + lax.dot_general(rest, z, OVER_FIRST, preferred_element_type=F32)
        load = jnp.zeros((GS, LANES), F32)
        for g in range(NG):
            load = jnp.where(own_lanes(g), prod[g * GS : (g + 1) * GS, :], load)
        load_ref[:, cols] = load


def li_gate(k, v, feat, enter):
    return pl.pallas_call(
        li_gate_kernel,
        out_shape=[PIECE, STATE],
        in_specs=vspecs(4),
        out_specs=vspecs(2),
        scratch_shapes=[pltpu.VMEM((16 + ROWS, LANES), F32)] * 2,
        compiler_params=params(),
        name="li_gate",
    )(k, v, feat, enter)


STATE = jax.ShapeDtypeStruct((GS, WIDTH), F32)


def chip_kernel(where_ref, load_ref, other_ref, rates_ref, chip_ref):
    k = where_ref[4]
    load, other = load_ref[...], other_ref[...]
    fade = jnp.exp(-rates_ref[...] * (1.0 * ROWS))
    chip_ref[...] = jnp.where(k == 0, load * fade + other, other * fade + load)


def chip_state(where, load, other, rates):
    return pl.pallas_call(
        chip_kernel,
        out_shape=STATE,
        in_specs=[SMEM_SPEC] + vspecs(3),
        out_specs=pl.BlockSpec(memory_space=pltpu.VMEM),
        compiler_params=params(),
        name="chip_state",
    )(where, load, other, rates)


def line_kernel(where_ref, c0, c1, c2, c3, rates_ref, total_ref, carry_ref):
    zl = where_ref[3]
    rates = rates_ref[...]
    total = jnp.zeros(rates.shape, F32)
    carry = jnp.zeros(rates.shape, F32)
    for s, ref in enumerate((c0, c1, c2, c3)):
        piece = ref[...]
        src = lax.rem(zl + NZ - s, NZ)
        gap = ((NZ - 1 - src) * (2 * ROWS)).astype(F32)
        total = total + jnp.exp(-rates * gap) * piece
        if s > 0:
            part = jnp.exp(-rates * (2.0 * ROWS * (s - 1))) * piece
            carry = carry + jnp.where(zl >= s, part, 0.0)
    total_ref[...] = total
    carry_ref[...] = carry


def line_state(where, pieces, rates):
    return pl.pallas_call(
        line_kernel,
        out_shape=[STATE] * 2,
        in_specs=[SMEM_SPEC] + vspecs(5),
        out_specs=vspecs(2),
        compiler_params=params(),
        name="line_state",
    )(where, *pieces, rates)


def li_inner_kernel(z_ref, toep_ref, conv_ref):
    for block in range(WIDTH // LANES):
        cols = slice(block * LANES, (block + 1) * LANES)
        first = z_ref[0:LANES, cols]
        second = z_ref[LANES:ROWS, cols]
        top, low = filtered(toep_ref, block, jnp.zeros_like(first), first, second)
        conv_ref[0:LANES, cols] = top
        conv_ref[LANES:ROWS, cols] = low


def li_inner(z, toep):
    return pl.pallas_call(
        li_inner_kernel,
        out_shape=jax.ShapeDtypeStruct((ROWS, WIDTH), F32),
        in_specs=vspecs(2),
        out_specs=pl.BlockSpec(memory_space=pltpu.VMEM),
        compiler_params=params(),
        name="li_inner",
    )(z, toep)


def li_outer_kernel(
    where_ref, conv_ref, q_ref, feat_ref, leave_ref, rates_ref,
    carry_ref, other_ref, y1_ref, y2_ref, y3_ref, w_ref,
    y_ref, o0, o1, o2, o3, qx, wbuf, sems,
):
    copies = share_loads(where_ref, w_ref, wbuf, sems, 1)
    zl, k = where_ref[3], where_ref[4]
    rates = rates_ref[...]
    above = y1_ref[...]
    above = above + jnp.exp(-rates * (2.0 * ROWS * NZ)) * y2_ref[...]
    above = above + jnp.exp(-rates * (4.0 * ROWS * NZ)) * y3_ref[...]
    chip = carry_ref[...] + jnp.exp(-rates * (zl * (2 * ROWS)).astype(F32)) * above
    full = jnp.where(k == 0, chip, jnp.exp(-rates * (1.0 * ROWS)) * chip + other_ref[...])
    for block in range(WIDTH // LANES):
        cols = slice(block * LANES, (block + 1) * LANES)
        qx[...] = q_ref[:, cols].astype(F32)
        qf = feature(qx, 16, ROWS, feat_ref[0, :, cols])
        state = full[:, cols]
        spread = jnp.concatenate(
            [jnp.where(own_lanes(g), state, 0.0) for g in range(NG)], axis=0
        )
        outer = jnp.dot(
            leave_ref[:, cols], spread, preferred_element_type=F32, precision=lax.Precision.HIGHEST
        )
        y_ref[:, cols] = (qf * (conv_ref[:, cols] + outer)).astype(BF16)
    share_products(copies, y_ref, wbuf, (o0, o1, o2, o3))


def li_outer(where, conv, q, feat, leave, rates, carry, other, above, weight):
    return pl.pallas_call(
        li_outer_kernel,
        out_shape=[PIECE] * 5,
        in_specs=[SMEM_SPEC] + vspecs(10) + hspecs(1),
        out_specs=vspecs(5),
        scratch_shapes=[pltpu.VMEM((16 + ROWS, LANES), F32)] + SHARE_SCRATCH,
        compiler_params=params(52),
        name="li_outer",
    )(where, conv, q, feat, leave, rates, carry, other, *above, weight)


def ctx_of(y, zl, k):
    return (y * NZ + zl) * NC + k


def mp_of(x, zh):
    return x * NH + zh


def x_shift(by):
    return [(mp_of(x, h), mp_of((x + by) % NX, h)) for x in range(NX) for h in range(NH)]


H_SWAP = [(mp_of(x, h), mp_of(x, 1 - h)) for x in range(NX) for h in range(NH)]
CORE_SWAP = [(i, i ^ 1) for i in range(NY * NZ * NC)]


def z_shift(by):
    return [
        (ctx_of(y, z, k), ctx_of(y, (z + by) % NZ, k))
        for y in range(NY) for z in range(NZ) for k in range(NC)
    ]


def y_shift(by):
    return [
        (ctx_of(y, z, k), ctx_of((y + by) % NY, z, k))
        for y in range(NY) for z in range(NZ) for k in range(NC)
    ]


GATHER_ORDER = [
    ctx_of(y if z % 2 == 0 else NY - 1 - y, z, k)
    for z in range(NZ) for y in range(NY) for k in range(NC)
]


def gathered_at(y, z, k):
    if z % 2 == 1:
        y = NY - 1 - y
    return (z * NY + y) * NC + k


def weight_moves():
    moves = []
    for y in range(NY):
        for zl in range(NZ):
            for k in range(NC):
                for x in range(NX):
                    for h in range(NH):
                        x2, h2, y2 = y, zl // 2, x
                        l0 = zl % 2
                        odd = 1 - l0
                        outer = h ^ h2
                        high = odd if outer else 1 - odd
                        z2 = high * 2 + odd
                        src = ctx_of(y, zl, k) * (NX * NH) + mp_of(x, h)
                        dst = ctx_of(y2, z2, k) * (NX * NH) + mp_of(x2, h2)
                        moves.append((src, dst))
    return moves


def tied(*values):
    return lax.optimization_barrier(values)


def sum_shares(where, y, other, weight, own_extra):
    got = [lax.ppermute(other[d], "mp", x_shift(d)) for d in (1, 3, 2)]
    total_other = other[0].astype(F32)
    for piece in got:
        total_other = total_other + piece.astype(F32)
    total_other, *mine = tied(total_other.astype(BF16), *shares(where, y, weight, 0))
    crossed = lax.ppermute(total_other, "mp", H_SWAP)
    got_mine = [lax.ppermute(mine[d], "mp", x_shift(d)) for d in (1, 3, 2)]
    (total,) = tied(own_extra.astype(F32) + mine[0].astype(F32) + crossed.astype(F32))
    for piece in got_mine:
        total = total + piece.astype(F32)
    return total.astype(BF16)


def body(
    query_mr, key_mr, value_mr, featurizer_mr, mr_taps, out_mr,
    residual, in_weight, featurizer_li, li_rates, li_residues, out_li,
):
    ctx = lax.axis_index("ctx")
    mp = lax.axis_index("mp")
    x, zh = mp // NH, mp % NH
    y, zl, k = ctx // (NZ * NC), (ctx // NC) % NZ, ctx % NC
    where = jnp.stack([x, zh, y, zl, k]).astype(jnp.int32)

    forward = [(i, i + 1) for i in range(NY * NZ * NC - 1)]
    moved = lax.ppermute(in_weight, ("ctx", "mp"), weight_moves())
    rim, query_mr, key_mr, value_mr = rim_rows(query_mr, key_mr, value_mr)
    halo = lax.ppermute(rim, "ctx", forward)
    toep_mr = toeplitz(mr_taps)
    halo, moved, toep_mr = tied(halo, moved, toep_mr)
    weights = lax.all_gather(moved, "ctx", axis_index_groups=[GATHER_ORDER])
    gated_one, *other_one = mr_op(
        where, query_mr, key_mr, value_mr, halo, featurizer_mr, toep_mr, out_mr
    )
    hidden = sum_shares(where, gated_one, other_one, out_mr, residual)
    filters = prep(li_rates.T, li_residues.T)

    before_rows = lax.ppermute(hidden[ROWS - 16 :], "ctx", forward)
    extended = jnp.concatenate([before_rows, hidden], axis=0)
    crossed = lax.ppermute(extended, "mp", H_SWAP)
    own_pieces = [extended] + [lax.ppermute(extended, "mp", x_shift(d)) for d in (1, 2, 3)]
    crossed, *filters = tied(crossed, *filters)
    toep_li, leave, enter, lane_rates = filters
    far_pieces = [crossed] + [lax.ppermute(crossed, "mp", x_shift(d)) for d in (1, 2, 3)]
    pieces = packed(own_pieces + far_pieces)
    fresh_k, fresh_v = project(where, pieces, weights, (1, 2))
    product, load = li_gate(fresh_k, fresh_v, featurizer_li, enter)
    other_load = lax.ppermute(load, "ctx", CORE_SWAP)
    chip = chip_state(where, load, other_load, lane_rates)
    before = [lax.ppermute(chip, "ctx", z_shift(s)) for s in (1, 2, 3)]
    (fresh_q,) = project(where, pieces, weights, (0,))
    conv = li_inner(product, toep_li)
    *before, fresh_q, conv = tied(*before, fresh_q, conv)
    line_total, line_carry = line_state(where, [chip] + before, lane_rates)
    above = []
    for s in (1, 2, 3):
        pairs = [
            (ctx_of(a, b, c), ctx_of(a + s, b, c))
            for a in range(NY - s) for b in range(NZ) for c in range(NC)
        ]
        above.append(lax.ppermute(line_total, "ctx", pairs))

    gated_two, *other_two = li_outer(
        where, conv, fresh_q, featurizer_li, leave, lane_rates,
        line_carry, other_load, above, out_li,
    )
    return sum_shares(where, gated_two, other_two, out_li, hidden)


def solution(mesh):
    return jax.shard_map(
        body,
        mesh=mesh,
        in_specs=(
            P("ctx", "mp"),
            P("ctx", "mp"),
            P("ctx", "mp"),
            P(None, None, "mp"),
            P(None, "mp"),
            P("mp", None),
            P("ctx", "mp"),
            P(None, "mp", "ctx"),
            P(None, None, "mp"),
            P("mp", None),
            P("mp", None),
            P("mp", None),
        ),
        out_specs=P("ctx", "mp"),
        check_vma=False,
    )
```

```python
import functools
import jax
import jax.numpy as jnp
from jax import lax
from jax.experimental import pallas as pl
from jax.experimental.pallas import tpu as pltpu
from jax.sharding import PartitionSpec as P

F32 = jnp.float32
BF16 = jnp.bfloat16
GS = 16
LANES = 128
NG = LANES // GS
ROWS = 256
WIDTH = 512
HALO = 144


def params(mib=16):
    return pltpu.CompilerParams(vmem_limit_bytes=mib * 1024 * 1024)


def vspecs(n):
    return [pl.BlockSpec(memory_space=pltpu.VMEM)] * n


def hspecs(n):
    return [pl.BlockSpec(memory_space=pltpu.HBM)] * n


SMEM_SPEC = pl.BlockSpec(memory_space=pltpu.SMEM)


def own_lanes(group):
    lane = lax.broadcasted_iota(jnp.int32, (1, LANES), 1)
    return (lane // GS) == group


NY, NZ, NC, NX, NH = 4, 4, 2, 4, 2

def rim_kernel(q_ref, k_ref, v_ref, out_ref, q_out, k_out, v_out, sems):
    parts = ((k_ref, HALO, 0), (v_ref, HALO, HALO), (q_ref, 16, 2 * HALO))
    copies = []
    for i, (ref, depth, at) in enumerate(parts):
        copy = pltpu.make_async_copy(
            ref.at[pl.ds(ROWS - depth, depth)], out_ref.at[pl.ds(at, depth)], sems.at[i]
        )
        copy.start()
        copies.append(copy)
    for i, (ref, out) in enumerate(((q_ref, q_out), (k_ref, k_out), (v_ref, v_out))):
        copy = pltpu.make_async_copy(ref, out, sems.at[3 + i])
        copy.start()
        copies.append(copy)
    for copy in copies:
        copy.wait()


def rim_rows(q, k, v):
    return pl.pallas_call(
        rim_kernel,
        out_shape=[jax.ShapeDtypeStruct((2 * HALO + 16, WIDTH), BF16)] + [PIECE] * 3,
        in_specs=hspecs(3),
        out_specs=vspecs(4),
        scratch_shapes=[pltpu.SemaphoreType.DMA((6,))],
        compiler_params=params(),
        name="rim_rows",
    )(q, k, v)


OVER_FIRST = (((0,), (0,)), ((), ()))


def exact(a, b):
    return lax.dot_general(a, b, OVER_FIRST, preferred_element_type=F32, precision=lax.Precision.HIGHEST)


def toeplitz_rows(near, far):
    row = lax.broadcasted_iota(jnp.int32, (LANES, LANES), 0)
    col = lax.broadcasted_iota(jnp.int32, (LANES, LANES), 1)
    near = pltpu.roll(jnp.broadcast_to(near, (LANES, LANES)), 0, 1, stride=1, stride_axis=0)
    upper = near
    if far is not None:
        far = pltpu.roll(jnp.broadcast_to(far, (LANES, LANES)), 0, 1, stride=1, stride_axis=0)
    else:
        far = 0.0
    upper = jnp.where(col > row, near, far).astype(BF16)
    lower = jnp.where(col <= row, near, 0.0).astype(BF16)
    return upper, lower


def toeplitz_kernel(taps_ref, out_ref, near):
    tap = lax.broadcasted_iota(jnp.int32, (LANES, LANES), 0)
    at = lax.broadcasted_iota(jnp.int32, (LANES, LANES), 1)
    near[...] = exact(taps_ref[...], jnp.where(tap == lax.rem(LANES - at, LANES), 1.0, 0.0))

    def one(g, carry):
        upper, lower = toeplitz_rows(near[pl.ds(g, 1), :], None)
        start = pl.multiple_of(g * LANES, LANES)
        out_ref[pl.ds(start, LANES), 0:LANES] = upper
        out_ref[pl.ds(start, LANES), LANES:] = lower
        return carry

    lax.fori_loop(0, near.shape[0], one, 0)


def toeplitz(taps):
    groups = taps.shape[1]
    return pl.pallas_call(
        toeplitz_kernel,
        out_shape=jax.ShapeDtypeStruct((groups * LANES, 2 * LANES), BF16),
        in_specs=vspecs(1),
        out_specs=pl.BlockSpec(memory_space=pltpu.VMEM),
        scratch_shapes=[pltpu.VMEM((groups, LANES), F32)],
        compiler_params=params(),
        name="toeplitz",
    )(taps)


def prep_kernel(rates_ref, res_ref, toep_ref, leave_ref, enter_ref, lane_ref, near, far):
    modes, groups = rates_ref.shape
    mode_r = lax.broadcasted_iota(jnp.int32, (modes, modes), 0)
    mode_c = lax.broadcasted_iota(jnp.int32, (modes, modes), 1)
    same = jnp.where(mode_r == mode_c, 1.0, 0.0)
    rates = exact(rates_ref[...], same)
    weights = exact(res_ref[...], same)
    back = lax.broadcasted_iota(jnp.int32, (groups, LANES), 1)
    back = jnp.where(back == 0, 0, LANES - back).astype(F32)
    near_sum = jnp.zeros((groups, LANES), F32)
    far_sum = jnp.zeros((groups, LANES), F32)
    for n in range(GS):
        rate = rates[:, n : n + 1]
        weight = weights[:, n : n + 1]
        near_sum = near_sum + weight * jnp.exp(-rate * back)
        far_sum = far_sum + weight * jnp.exp(-rate * (back + LANES))
    near[...] = near_sum
    far[...] = far_sum

    def one(g, carry):
        upper, lower = toeplitz_rows(near[pl.ds(g, 1), :], far[pl.ds(g, 1), :])
        start = pl.multiple_of(g * LANES, LANES)
        toep_ref[pl.ds(start, LANES), 0:LANES] = upper
        toep_ref[pl.ds(start, LANES), LANES:] = lower
        return carry

    lax.fori_loop(0, groups, one, 0)
    lane = lax.broadcasted_iota(jnp.int32, (groups, WIDTH), 1)
    member = lax.broadcasted_iota(jnp.int32, (groups, WIDTH), 0)
    pick = jnp.where(lane // GS == member, 1.0, 0.0)
    lane_rates = exact(rates, pick)
    lane_ref[...] = lane_rates
    lane = lax.broadcasted_iota(jnp.int32, (modes, WIDTH), 1)
    member = lax.broadcasted_iota(jnp.int32, (modes, WIDTH), 0)
    ours = lax.rem(lane, GS) == member
    rate_row = jnp.sum(jnp.where(ours, lane_rates, 0.0), axis=0, keepdims=True)
    weight_row = jnp.sum(jnp.where(ours, exact(weights, pick), 0.0), axis=0, keepdims=True)
    step = lax.broadcasted_iota(jnp.int32, (ROWS, LANES), 0).astype(F32)
    for block in range(WIDTH // LANES):
        cols = slice(block * LANES, (block + 1) * LANES)
        rate = rate_row[:, cols]
        leave_ref[:, cols] = weight_row[:, cols] * jnp.exp(-rate * step)
        enter_ref[:, cols] = jnp.exp(-rate * (ROWS - step))


def prep(rates, residues):
    groups = rates.shape[1]
    return pl.pallas_call(
        prep_kernel,
        out_shape=[
            jax.ShapeDtypeStruct((groups * LANES, 2 * LANES), BF16),
            jax.ShapeDtypeStruct((ROWS, WIDTH), F32),
            jax.ShapeDtypeStruct((ROWS, WIDTH), F32),
            jax.ShapeDtypeStruct((GS, WIDTH), F32),
        ],
        in_specs=vspecs(2),
        out_specs=vspecs(4),
        scratch_shapes=[pltpu.VMEM((groups, LANES), F32)] * 2,
        compiler_params=params(),
        name="prep",
    )(rates, residues)


def feature(ext_ref, base, rows, taps):
    total = taps[0:1] * ext_ref[pl.ds(base, rows), :]
    for k in range(1, 3):
        total = total + taps[k : k + 1] * ext_ref[pl.ds(base - k, rows), :]
    return total


def filtered(toep_ref, block, early, middle, late):
    rhs = jnp.concatenate(
        [
            jnp.concatenate([early, middle], axis=0),
            jnp.concatenate([middle, late], axis=0),
        ],
        axis=1,
    )
    top = jnp.zeros((LANES, LANES), F32)
    low = jnp.zeros((LANES, LANES), F32)
    for g in range(NG):
        start = (block * NG + g) * LANES
        prod = jnp.dot(toep_ref[start : start + LANES, :], rhs, preferred_element_type=F32)
        mine = own_lanes(g)
        top = jnp.where(mine, prod[:, :LANES], top)
        low = jnp.where(mine, prod[:, LANES:], low)
    return top, low


def share_loads(where_ref, w_ref, wbuf, sems, flip):
    x = where_ref[0]
    zh = where_ref[1]
    half = zh if flip == 0 else 1 - zh
    copies = []
    for d in range(4):
        block = lax.rem(x + d, 4) * 2 + half
        copy = pltpu.make_async_copy(
            w_ref.at[:, pl.ds(pl.multiple_of(block * WIDTH, WIDTH), WIDTH)], wbuf.at[d], sems.at[d]
        )
        copy.start()
        copies.append(copy)
    return copies


def share_products(copies, y_ref, wbuf, outs):
    for d in (1, 3, 2, 0):
        copies[d].wait()
        outs[d][...] = jnp.dot(y_ref[...], wbuf[d], preferred_element_type=F32).astype(BF16)


SHARE_SCRATCH = [pltpu.VMEM((4, WIDTH, WIDTH), BF16), pltpu.SemaphoreType.DMA((4,))]
PIECE = jax.ShapeDtypeStruct((ROWS, WIDTH), BF16)


def share_kernel(flip, where_ref, y_ref, w_ref, o0, o1, o2, o3, wbuf, sems):
    copies = share_loads(where_ref, w_ref, wbuf, sems, flip)
    share_products(copies, y_ref, wbuf, (o0, o1, o2, o3))


def shares(where, y, weight, flip):
    return pl.pallas_call(
        functools.partial(share_kernel, flip),
        out_shape=[PIECE] * 4,
        in_specs=[SMEM_SPEC] + vspecs(1) + hspecs(1),
        out_specs=vspecs(4),
        scratch_shapes=SHARE_SCRATCH,
        compiler_params=params(48),
        name="shares",
    )(where, y, weight)


def mr_kernel(
    where_ref, q_ref, k_ref, v_ref, halo_ref, feat_ref, toep_ref, w_ref,
    y_ref, o0, o1, o2, o3, kx, vx, qx, wbuf, sems,
):
    copies = share_loads(where_ref, w_ref, wbuf, sems, 1)
    for block in range(WIDTH // LANES):
        cols = slice(block * LANES, (block + 1) * LANES)
        kx[0:HALO, :] = halo_ref[0:HALO, cols].astype(F32)
        kx[HALO:, :] = k_ref[:, cols].astype(F32)
        vx[0:HALO, :] = halo_ref[HALO : 2 * HALO, cols].astype(F32)
        vx[HALO:, :] = v_ref[:, cols].astype(F32)
        qx[0:16, :] = halo_ref[2 * HALO : 2 * HALO + 16, cols].astype(F32)
        qx[16:, :] = q_ref[:, cols].astype(F32)
        zs = []
        for part in range(3):
            base = HALO - LANES + part * LANES
            kf = feature(kx, base, LANES, feat_ref[1, :, cols])
            vf = feature(vx, base, LANES, feat_ref[2, :, cols])
            zs.append((kf * vf).astype(BF16))
        top, low = filtered(toep_ref, block, *zs)
        for part, conv in ((0, top), (1, low)):
            qf = feature(qx, 16 + part * LANES, LANES, feat_ref[0, :, cols])
            y_ref[part * LANES : (part + 1) * LANES, cols] = (qf * conv).astype(BF16)
    share_products(copies, y_ref, wbuf, (o0, o1, o2, o3))


def mr_op(where, q, k, v, halo, feat, toep, weight):
    return pl.pallas_call(
        mr_kernel,
        out_shape=[PIECE] * 5,
        in_specs=[SMEM_SPEC] + vspecs(6) + hspecs(1),
        out_specs=vspecs(5),
        scratch_shapes=[
            pltpu.VMEM((HALO + ROWS, LANES), F32),
            pltpu.VMEM((HALO + ROWS, LANES), F32),
            pltpu.VMEM((16 + ROWS, LANES), F32),
        ] + SHARE_SCRATCH,
        compiler_params=params(48),
        name="mr_op",
    )(where, q, k, v, halo, feat, toep, weight)


EXT = 16 + ROWS
EXT_PIECE = jax.ShapeDtypeStruct((EXT, WIDTH), BF16)


def pack_kernel(*refs):
    for i in range(8):
        refs[8][:, i * WIDTH : (i + 1) * WIDTH] = refs[i][...]


def packed(pieces):
    return pl.pallas_call(
        pack_kernel,
        out_shape=jax.ShapeDtypeStruct((EXT, 8 * WIDTH), BF16),
        in_specs=vspecs(8),
        out_specs=pl.BlockSpec(memory_space=pltpu.VMEM),
        compiler_params=params(),
        name="packed",
    )(*pieces)


def project_kernel(slots, where_ref, hidden_ref, w_ref, *refs):
    count = len(slots)
    out_refs = refs[:count]
    wbuf, wsem = refs[count:]
    x = where_ref[0]
    copies = []
    for i in range(8):
        e, d = i // 4, i % 4
        src_y = lax.bitwise_xor(lax.rem(x + 4 - d, 4), x)
        for b in range(4):
            odd = 1 - b // 2
            high = odd if e == 1 else 1 - odd
            copy = pltpu.make_async_copy(
                w_ref.at[gathered_at(src_y, high * 2 + odd, b % 2), pl.ds(slots[0], count)],
                wbuf.at[:, pl.ds(i * WIDTH, WIDTH), pl.ds(b * LANES, LANES)],
                wsem.at[i, b],
            )
            copy.start()
            copies.append(copy)
    sums = [None] * count
    for half in range(2):
        for copy in copies[half * 16 : (half + 1) * 16]:
            copy.wait()
        deep = slice(half * 4 * WIDTH, (half + 1) * 4 * WIDTH)
        for j in range(count):
            prod = jnp.dot(hidden_ref[:, deep], wbuf[j, deep, :], preferred_element_type=F32)
            sums[j] = prod if half == 0 else sums[j] + prod
    for j in range(count):
        out_refs[j][...] = sums[j].astype(BF16)


def project(where, pieces, weights, slots):
    count = len(slots)
    return pl.pallas_call(
        functools.partial(project_kernel, slots),
        out_shape=[EXT_PIECE] * count,
        in_specs=[SMEM_SPEC] + vspecs(1) + hspecs(1),
        out_specs=vspecs(count),
        scratch_shapes=[
            pltpu.VMEM((count, 8 * WIDTH, WIDTH), BF16),
            pltpu.SemaphoreType.DMA((8, 4)),
        ],
        compiler_params=params(48),
        name="project",
    )(where, pieces, weights)


def li_gate_kernel(k_ref, v_ref, feat_ref, enter_ref, z_ref, load_ref, kx, vx):
    for block in range(WIDTH // LANES):
        cols = slice(block * LANES, (block + 1) * LANES)
        kx[...] = k_ref[:, cols].astype(F32)
        vx[...] = v_ref[:, cols].astype(F32)
        kf = feature(kx, 16, ROWS, feat_ref[1, :, cols])
        vf = feature(vx, 16, ROWS, feat_ref[2, :, cols])
        z = (kf * vf).astype(BF16)
        z_ref[:, cols] = z
        enter = enter_ref[:, cols]
        high = enter.astype(BF16)
        rest = (enter - high.astype(F32)).astype(BF16)
        prod = lax.dot_general(high, z, OVER_FIRST, preferred_element_type=F32)
        prod = prod + lax.dot_general(rest, z, OVER_FIRST, preferred_element_type=F32)
        load = jnp.zeros((GS, LANES), F32)
        for g in range(NG):
            load = jnp.where(own_lanes(g), prod[g * GS : (g + 1) * GS, :], load)
        load_ref[:, cols] = load


def li_gate(k, v, feat, enter):
    return pl.pallas_call(
        li_gate_kernel,
        out_shape=[PIECE, STATE],
        in_specs=vspecs(4),
        out_specs=vspecs(2),
        scratch_shapes=[pltpu.VMEM((16 + ROWS, LANES), F32)] * 2,
        compiler_params=params(),
        name="li_gate",
    )(k, v, feat, enter)


STATE = jax.ShapeDtypeStruct((GS, WIDTH), F32)


def chip_kernel(where_ref, load_ref, other_ref, rates_ref, chip_ref):
    k = where_ref[4]
    load, other = load_ref[...], other_ref[...]
    fade = jnp.exp(-rates_ref[...] * (1.0 * ROWS))
    chip_ref[...] = jnp.where(k == 0, load * fade + other, other * fade + load)


def chip_state(where, load, other, rates):
    return pl.pallas_call(
        chip_kernel,
        out_shape=STATE,
        in_specs=[SMEM_SPEC] + vspecs(3),
        out_specs=pl.BlockSpec(memory_space=pltpu.VMEM),
        compiler_params=params(),
        name="chip_state",
    )(where, load, other, rates)


def line_kernel(where_ref, c0, c1, c2, c3, rates_ref, total_ref, carry_ref):
    zl = where_ref[3]
    rates = rates_ref[...]
    total = jnp.zeros(rates.shape, F32)
    carry = jnp.zeros(rates.shape, F32)
    for s, ref in enumerate((c0, c1, c2, c3)):
        piece = ref[...]
        src = lax.rem(zl + NZ - s, NZ)
        gap = ((NZ - 1 - src) * (2 * ROWS)).astype(F32)
        total = total + jnp.exp(-rates * gap) * piece
        if s > 0:
            part = jnp.exp(-rates * (2.0 * ROWS * (s - 1))) * piece
            carry = carry + jnp.where(zl >= s, part, 0.0)
    total_ref[...] = total
    carry_ref[...] = carry


def line_state(where, pieces, rates):
    return pl.pallas_call(
        line_kernel,
        out_shape=[STATE] * 2,
        in_specs=[SMEM_SPEC] + vspecs(5),
        out_specs=vspecs(2),
        compiler_params=params(),
        name="line_state",
    )(where, *pieces, rates)


def li_inner_kernel(z_ref, toep_ref, conv_ref):
    for block in range(WIDTH // LANES):
        cols = slice(block * LANES, (block + 1) * LANES)
        first = z_ref[0:LANES, cols]
        second = z_ref[LANES:ROWS, cols]
        top, low = filtered(toep_ref, block, jnp.zeros_like(first), first, second)
        conv_ref[0:LANES, cols] = top
        conv_ref[LANES:ROWS, cols] = low


def li_inner(z, toep):
    return pl.pallas_call(
        li_inner_kernel,
        out_shape=jax.ShapeDtypeStruct((ROWS, WIDTH), F32),
        in_specs=vspecs(2),
        out_specs=pl.BlockSpec(memory_space=pltpu.VMEM),
        compiler_params=params(),
        name="li_inner",
    )(z, toep)


def li_outer_kernel(
    where_ref, conv_ref, q_ref, feat_ref, leave_ref, rates_ref,
    carry_ref, other_ref, y1_ref, y2_ref, y3_ref, w_ref,
    y_ref, o0, o1, o2, o3, qx, wbuf, sems,
):
    copies = share_loads(where_ref, w_ref, wbuf, sems, 1)
    y, zl, k = where_ref[2], where_ref[3], where_ref[4]
    rates = rates_ref[...]
    above = jnp.where(y >= 1, y1_ref[...], 0.0)
    above = above + jnp.where(y >= 2, jnp.exp(-rates * (2.0 * ROWS * NZ)) * y2_ref[...], 0.0)
    above = above + jnp.where(y >= 3, jnp.exp(-rates * (4.0 * ROWS * NZ)) * y3_ref[...], 0.0)
    chip = carry_ref[...] + jnp.exp(-rates * (zl * (2 * ROWS)).astype(F32)) * above
    full = jnp.where(k == 0, chip, jnp.exp(-rates * (1.0 * ROWS)) * chip + other_ref[...])
    for block in range(WIDTH // LANES):
        cols = slice(block * LANES, (block + 1) * LANES)
        qx[...] = q_ref[:, cols].astype(F32)
        qf = feature(qx, 16, ROWS, feat_ref[0, :, cols])
        state = full[:, cols]
        spread = jnp.concatenate(
            [jnp.where(own_lanes(g), state, 0.0) for g in range(NG)], axis=0
        )
        outer = jnp.dot(
            leave_ref[:, cols], spread, preferred_element_type=F32, precision=lax.Precision.HIGHEST
        )
        y_ref[:, cols] = (qf * (conv_ref[:, cols] + outer)).astype(BF16)
    share_products(copies, y_ref, wbuf, (o0, o1, o2, o3))


def li_outer(where, conv, q, feat, leave, rates, carry, other, above, weight):
    return pl.pallas_call(
        li_outer_kernel,
        out_shape=[PIECE] * 5,
        in_specs=[SMEM_SPEC] + vspecs(10) + hspecs(1),
        out_specs=vspecs(5),
        scratch_shapes=[pltpu.VMEM((16 + ROWS, LANES), F32)] + SHARE_SCRATCH,
        compiler_params=params(48),
        name="li_outer",
    )(where, conv, q, feat, leave, rates, carry, other, *above, weight)


def ctx_of(y, zl, k):
    return (y * NZ + zl) * NC + k


def mp_of(x, zh):
    return x * NH + zh


def x_shift(by):
    return [(mp_of(x, h), mp_of((x + by) % NX, h)) for x in range(NX) for h in range(NH)]


H_SWAP = [(mp_of(x, h), mp_of(x, 1 - h)) for x in range(NX) for h in range(NH)]
CORE_SWAP = [(i, i ^ 1) for i in range(NY * NZ * NC)]


def z_shift(by):
    return [
        (ctx_of(y, z, k), ctx_of(y, (z + by) % NZ, k))
        for y in range(NY) for z in range(NZ) for k in range(NC)
    ]


def y_shift(by):
    return [
        (ctx_of(y, z, k), ctx_of((y + by) % NY, z, k))
        for y in range(NY) for z in range(NZ) for k in range(NC)
    ]


GATHER_ORDER = [
    ctx_of(y if z % 2 == 0 else NY - 1 - y, z, k)
    for z in range(NZ) for y in range(NY) for k in range(NC)
]


def gathered_at(y, z, k):
    if z % 2 == 1:
        y = NY - 1 - y
    return (z * NY + y) * NC + k


def flat(y, zl, k, x, h):
    return ctx_of(y, zl, k) * (NX * NH) + mp_of(x, h)


def weight_moves():
    first, second = [], []
    for y in range(NY):
        for zl in range(NZ):
            for k in range(NC):
                for x in range(NX):
                    for h in range(NH):
                        h2, odd = zl // 2, 1 - zl % 2
                        high = odd if h ^ h2 else 1 - odd
                        z2 = high * 2 + odd
                        via = flat(x ^ y, z2, k, x, h2)
                        first.append((flat(y, zl, k, x, h), via))
                        second.append((via, flat(x ^ y, z2, k, y, h2)))
    return first, second


def tied(*values):
    return lax.optimization_barrier(values)


def sum_shares(where, y, other, weight, own_extra):
    got = [lax.ppermute(other[d], "mp", x_shift(d)) for d in (1, 3, 2)]
    total_other = other[0].astype(F32)
    for piece in got:
        total_other = total_other + piece.astype(F32)
    total_other, *mine = tied(total_other.astype(BF16), *shares(where, y, weight, 0))
    crossed = lax.ppermute(total_other, "mp", H_SWAP)
    got_mine = [lax.ppermute(mine[d], "mp", x_shift(d)) for d in (1, 3, 2)]
    (total,) = tied(own_extra.astype(F32) + mine[0].astype(F32) + crossed.astype(F32))
    for piece in got_mine:
        total = total + piece.astype(F32)
    return total.astype(BF16)


def body(
    query_mr, key_mr, value_mr, featurizer_mr, mr_taps, out_mr,
    residual, in_weight, featurizer_li, li_rates, li_residues, out_li,
):
    ctx = lax.axis_index("ctx")
    mp = lax.axis_index("mp")
    x, zh = mp // NH, mp % NH
    y, zl, k = ctx // (NZ * NC), (ctx // NC) % NZ, ctx % NC
    where = jnp.stack([x, zh, y, zl, k]).astype(jnp.int32)

    forward = [(i, i + 1) for i in range(NY * NZ * NC - 1)]
    first, second = weight_moves()
    moved = lax.ppermute(in_weight, ("ctx", "mp"), first)
    rim, query_mr, key_mr, value_mr = rim_rows(query_mr, key_mr, value_mr)
    moved, rim = tied(moved, rim)
    moved = lax.ppermute(moved, ("ctx", "mp"), second)
    halo = lax.ppermute(rim, "ctx", forward)
    toep_mr = toeplitz(mr_taps)
    halo, moved, toep_mr = tied(halo, moved, toep_mr)
    weights = lax.all_gather(moved, "ctx", axis_index_groups=[GATHER_ORDER])
    gated_one, *other_one = mr_op(
        where, query_mr, key_mr, value_mr, halo, featurizer_mr, toep_mr, out_mr
    )
    hidden = sum_shares(where, gated_one, other_one, out_mr, residual)
    filters = prep(li_rates.T, li_residues.T)

    before_rows = lax.ppermute(hidden[ROWS - 16 :], "ctx", forward)
    extended = jnp.concatenate([before_rows, hidden], axis=0)
    crossed = lax.ppermute(extended, "mp", H_SWAP)
    own_pieces = [extended] + [lax.ppermute(extended, "mp", x_shift(d)) for d in (1, 2, 3)]
    crossed, *filters = tied(crossed, *filters)
    toep_li, leave, enter, lane_rates = filters
    far_pieces = [crossed] + [lax.ppermute(crossed, "mp", x_shift(d)) for d in (1, 2, 3)]
    pieces = packed(own_pieces + far_pieces)
    fresh_k, fresh_v = project(where, pieces, weights, (1, 2))
    product, load = li_gate(fresh_k, fresh_v, featurizer_li, enter)
    other_load = lax.ppermute(load, "ctx", CORE_SWAP)
    chip = chip_state(where, load, other_load, lane_rates)
    before = [lax.ppermute(chip, "ctx", z_shift(s)) for s in (1, 2, 3)]
    (fresh_q,) = project(where, pieces, weights, (0,))
    *before, fresh_q = tied(*before, fresh_q)
    conv = li_inner(product, toep_li)
    line_total, line_carry = line_state(where, [chip] + before, lane_rates)
    above = [lax.ppermute(line_total, "ctx", y_shift(s)) for s in (1, 2, 3)]
    gated_two, *other_two = li_outer(
        where, conv, fresh_q, featurizer_li, leave, lane_rates,
        line_carry, other_load, above, out_li,
    )
    return sum_shares(where, gated_two, other_two, out_li, hidden)


def solution(mesh):
    return jax.shard_map(
        body,
        mesh=mesh,
        in_specs=(
            P("ctx", "mp"),
            P("ctx", "mp"),
            P("ctx", "mp"),
            P(None, None, "mp"),
            P(None, "mp"),
            P("mp", None),
            P("ctx", "mp"),
            P(None, "mp", "ctx"),
            P(None, None, "mp"),
            P("mp", None),
            P("mp", None),
            P("mp", None),
        ),
        out_specs=P("ctx", "mp"),
        check_vma=False,
    )
```

```python
import functools
import jax
import jax.numpy as jnp
from jax import lax
from jax.experimental import pallas as pl
from jax.experimental.pallas import tpu as pltpu
from jax.sharding import PartitionSpec as P

F32 = jnp.float32
BF16 = jnp.bfloat16
GS = 16
LANES = 128
NG = LANES // GS
ROWS = 256
WIDTH = 512
HALO = 144


def params(mib=16):
    return pltpu.CompilerParams(vmem_limit_bytes=mib * 1024 * 1024)


def vspecs(n):
    return [pl.BlockSpec(memory_space=pltpu.VMEM)] * n


def hspecs(n):
    return [pl.BlockSpec(memory_space=pltpu.HBM)] * n


SMEM_SPEC = pl.BlockSpec(memory_space=pltpu.SMEM)


def own_lanes(group):
    lane = lax.broadcasted_iota(jnp.int32, (1, LANES), 1)
    return (lane // GS) == group


NY, NZ, NC, NX, NH = 4, 4, 2, 4, 2

def rim_kernel(q_ref, k_ref, v_ref, out_ref, q_out, k_out, v_out, sems):
    parts = ((k_ref, HALO, 0), (v_ref, HALO, HALO), (q_ref, 16, 2 * HALO))
    copies = []
    for i, (ref, depth, at) in enumerate(parts):
        copy = pltpu.make_async_copy(
            ref.at[pl.ds(ROWS - depth, depth)], out_ref.at[pl.ds(at, depth)], sems.at[i]
        )
        copy.start()
        copies.append(copy)
    for i, (ref, out) in enumerate(((q_ref, q_out), (k_ref, k_out), (v_ref, v_out))):
        copy = pltpu.make_async_copy(ref, out, sems.at[3 + i])
        copy.start()
        copies.append(copy)
    for copy in copies:
        copy.wait()


def rim_rows(q, k, v):
    return pl.pallas_call(
        rim_kernel,
        out_shape=[jax.ShapeDtypeStruct((2 * HALO + 16, WIDTH), BF16)] + [PIECE] * 3,
        in_specs=hspecs(3),
        out_specs=vspecs(4),
        scratch_shapes=[pltpu.SemaphoreType.DMA((6,))],
        compiler_params=params(),
        name="rim_rows",
    )(q, k, v)


OVER_FIRST = (((0,), (0,)), ((), ()))


def exact(a, b):
    return lax.dot_general(a, b, OVER_FIRST, preferred_element_type=F32, precision=lax.Precision.HIGHEST)


def toeplitz_rows(near, far):
    row = lax.broadcasted_iota(jnp.int32, (LANES, LANES), 0)
    col = lax.broadcasted_iota(jnp.int32, (LANES, LANES), 1)
    near = pltpu.roll(jnp.broadcast_to(near, (LANES, LANES)), 0, 1, stride=1, stride_axis=0)
    upper = near
    if far is not None:
        far = pltpu.roll(jnp.broadcast_to(far, (LANES, LANES)), 0, 1, stride=1, stride_axis=0)
    else:
        far = 0.0
    upper = jnp.where(col > row, near, far).astype(BF16)
    lower = jnp.where(col <= row, near, 0.0).astype(BF16)
    return upper, lower


def toeplitz_kernel(taps_ref, out_ref, near):
    tap = lax.broadcasted_iota(jnp.int32, (LANES, LANES), 0)
    at = lax.broadcasted_iota(jnp.int32, (LANES, LANES), 1)
    near[...] = exact(taps_ref[...], jnp.where(tap == lax.rem(LANES - at, LANES), 1.0, 0.0))

    def one(g, carry):
        upper, lower = toeplitz_rows(near[pl.ds(g, 1), :], None)
        start = pl.multiple_of(g * LANES, LANES)
        out_ref[pl.ds(start, LANES), 0:LANES] = upper
        out_ref[pl.ds(start, LANES), LANES:] = lower
        return carry

    lax.fori_loop(0, near.shape[0], one, 0)


def toeplitz(taps):
    groups = taps.shape[1]
    return pl.pallas_call(
        toeplitz_kernel,
        out_shape=jax.ShapeDtypeStruct((groups * LANES, 2 * LANES), BF16),
        in_specs=vspecs(1),
        out_specs=pl.BlockSpec(memory_space=pltpu.VMEM),
        scratch_shapes=[pltpu.VMEM((groups, LANES), F32)],
        compiler_params=params(),
        name="toeplitz",
    )(taps)


def prep_kernel(rates_ref, res_ref, toep_ref, leave_ref, enter_ref, lane_ref, near, far):
    modes, groups = rates_ref.shape
    mode_r = lax.broadcasted_iota(jnp.int32, (modes, modes), 0)
    mode_c = lax.broadcasted_iota(jnp.int32, (modes, modes), 1)
    same = jnp.where(mode_r == mode_c, 1.0, 0.0)
    rates = exact(rates_ref[...], same)
    weights = exact(res_ref[...], same)
    back = lax.broadcasted_iota(jnp.int32, (groups, LANES), 1)
    back = jnp.where(back == 0, 0, LANES - back).astype(F32)
    near_sum = jnp.zeros((groups, LANES), F32)
    far_sum = jnp.zeros((groups, LANES), F32)
    for n in range(GS):
        rate = rates[:, n : n + 1]
        weight = weights[:, n : n + 1]
        near_sum = near_sum + weight * jnp.exp(-rate * back)
        far_sum = far_sum + weight * jnp.exp(-rate * (back + LANES))
    near[...] = near_sum
    far[...] = far_sum

    def one(g, carry):
        upper, lower = toeplitz_rows(near[pl.ds(g, 1), :], far[pl.ds(g, 1), :])
        start = pl.multiple_of(g * LANES, LANES)
        toep_ref[pl.ds(start, LANES), 0:LANES] = upper
        toep_ref[pl.ds(start, LANES), LANES:] = lower
        return carry

    lax.fori_loop(0, groups, one, 0)
    lane = lax.broadcasted_iota(jnp.int32, (groups, WIDTH), 1)
    member = lax.broadcasted_iota(jnp.int32, (groups, WIDTH), 0)
    pick = jnp.where(lane // GS == member, 1.0, 0.0)
    lane_rates = exact(rates, pick)
    lane_ref[...] = lane_rates
    lane = lax.broadcasted_iota(jnp.int32, (modes, WIDTH), 1)
    member = lax.broadcasted_iota(jnp.int32, (modes, WIDTH), 0)
    ours = lax.rem(lane, GS) == member
    rate_row = jnp.sum(jnp.where(ours, lane_rates, 0.0), axis=0, keepdims=True)
    weight_row = jnp.sum(jnp.where(ours, exact(weights, pick), 0.0), axis=0, keepdims=True)
    step = lax.broadcasted_iota(jnp.int32, (ROWS, LANES), 0).astype(F32)
    for block in range(WIDTH // LANES):
        cols = slice(block * LANES, (block + 1) * LANES)
        rate = rate_row[:, cols]
        leave_ref[:, cols] = weight_row[:, cols] * jnp.exp(-rate * step)
        enter_ref[:, cols] = jnp.exp(-rate * (ROWS - step))


def prep(rates, residues):
    groups = rates.shape[1]
    return pl.pallas_call(
        prep_kernel,
        out_shape=[
            jax.ShapeDtypeStruct((groups * LANES, 2 * LANES), BF16),
            jax.ShapeDtypeStruct((ROWS, WIDTH), F32),
            jax.ShapeDtypeStruct((ROWS, WIDTH), F32),
            jax.ShapeDtypeStruct((GS, WIDTH), F32),
        ],
        in_specs=vspecs(2),
        out_specs=vspecs(4),
        scratch_shapes=[pltpu.VMEM((groups, LANES), F32)] * 2,
        compiler_params=params(),
        name="prep",
    )(rates, residues)


def feature(ext_ref, base, rows, taps):
    total = taps[0:1] * ext_ref[pl.ds(base, rows), :]
    for k in range(1, 3):
        total = total + taps[k : k + 1] * ext_ref[pl.ds(base - k, rows), :]
    return total


def filtered(toep_ref, block, early, middle, late):
    rhs = jnp.concatenate(
        [
            jnp.concatenate([early, middle], axis=0),
            jnp.concatenate([middle, late], axis=0),
        ],
        axis=1,
    )
    top = jnp.zeros((LANES, LANES), F32)
    low = jnp.zeros((LANES, LANES), F32)
    for g in range(NG):
        start = (block * NG + g) * LANES
        prod = jnp.dot(toep_ref[start : start + LANES, :], rhs, preferred_element_type=F32)
        mine = own_lanes(g)
        top = jnp.where(mine, prod[:, :LANES], top)
        low = jnp.where(mine, prod[:, LANES:], low)
    return top, low


def share_loads(where_ref, w_ref, wbuf, sems, flip):
    x = where_ref[0]
    zh = where_ref[1]
    half = zh if flip == 0 else 1 - zh
    copies = []
    for d in range(4):
        block = lax.rem(x + d, 4) * 2 + half
        copy = pltpu.make_async_copy(
            w_ref.at[:, pl.ds(pl.multiple_of(block * WIDTH, WIDTH), WIDTH)], wbuf.at[d], sems.at[d]
        )
        copy.start()
        copies.append(copy)
    return copies


def share_products(copies, y_ref, wbuf, outs):
    for d in (1, 3, 2, 0):
        copies[d].wait()
        outs[d][...] = jnp.dot(y_ref[...], wbuf[d], preferred_element_type=F32).astype(BF16)


SHARE_SCRATCH = [pltpu.VMEM((4, WIDTH, WIDTH), BF16), pltpu.SemaphoreType.DMA((4,))]
PIECE = jax.ShapeDtypeStruct((ROWS, WIDTH), BF16)


def share_kernel(flip, where_ref, y_ref, w_ref, o0, o1, o2, o3, wbuf, sems):
    copies = share_loads(where_ref, w_ref, wbuf, sems, flip)
    share_products(copies, y_ref, wbuf, (o0, o1, o2, o3))


def shares(where, y, weight, flip):
    return pl.pallas_call(
        functools.partial(share_kernel, flip),
        out_shape=[PIECE] * 4,
        in_specs=[SMEM_SPEC] + vspecs(1) + hspecs(1),
        out_specs=vspecs(4),
        scratch_shapes=SHARE_SCRATCH,
        compiler_params=params(48),
        name="shares",
    )(where, y, weight)


def mr_kernel(
    where_ref, q_ref, k_ref, v_ref, halo_ref, feat_ref, toep_ref, w_ref,
    y_ref, o0, o1, o2, o3, kx, vx, qx, wbuf, sems,
):
    copies = share_loads(where_ref, w_ref, wbuf, sems, 1)
    for block in range(WIDTH // LANES):
        cols = slice(block * LANES, (block + 1) * LANES)
        kx[0:HALO, :] = halo_ref[0:HALO, cols].astype(F32)
        kx[HALO:, :] = k_ref[:, cols].astype(F32)
        vx[0:HALO, :] = halo_ref[HALO : 2 * HALO, cols].astype(F32)
        vx[HALO:, :] = v_ref[:, cols].astype(F32)
        qx[0:16, :] = halo_ref[2 * HALO : 2 * HALO + 16, cols].astype(F32)
        qx[16:, :] = q_ref[:, cols].astype(F32)
        zs = []
        for part in range(3):
            base = HALO - LANES + part * LANES
            kf = feature(kx, base, LANES, feat_ref[1, :, cols])
            vf = feature(vx, base, LANES, feat_ref[2, :, cols])
            zs.append((kf * vf).astype(BF16))
        top, low = filtered(toep_ref, block, *zs)
        for part, conv in ((0, top), (1, low)):
            qf = feature(qx, 16 + part * LANES, LANES, feat_ref[0, :, cols])
            y_ref[part * LANES : (part + 1) * LANES, cols] = (qf * conv).astype(BF16)
    share_products(copies, y_ref, wbuf, (o0, o1, o2, o3))


def mr_op(where, q, k, v, halo, feat, toep, weight):
    return pl.pallas_call(
        mr_kernel,
        out_shape=[PIECE] * 5,
        in_specs=[SMEM_SPEC] + vspecs(6) + hspecs(1),
        out_specs=vspecs(5),
        scratch_shapes=[
            pltpu.VMEM((HALO + ROWS, LANES), F32),
            pltpu.VMEM((HALO + ROWS, LANES), F32),
            pltpu.VMEM((16 + ROWS, LANES), F32),
        ] + SHARE_SCRATCH,
        compiler_params=params(48),
        name="mr_op",
    )(where, q, k, v, halo, feat, toep, weight)


EXT = 16 + ROWS
EXT_PIECE = jax.ShapeDtypeStruct((EXT, WIDTH), BF16)


def pack_kernel(*refs):
    for i in range(8):
        refs[8][i] = refs[i][...]


def packed(pieces):
    return pl.pallas_call(
        pack_kernel,
        out_shape=jax.ShapeDtypeStruct((8, EXT, WIDTH), BF16),
        in_specs=vspecs(8),
        out_specs=pl.BlockSpec(memory_space=pltpu.VMEM),
        compiler_params=params(),
        name="packed",
    )(*pieces)


def project_kernel(slots, where_ref, hidden_ref, w_ref, *refs):
    count = len(slots)
    out_refs = refs[:count]
    wbuf, wsem = refs[count:]
    x = where_ref[0]
    copies = []
    for i in range(8):
        e, d = i // 4, i % 4
        src_y = lax.rem(x + 4 - d, 4)
        for b in range(4):
            odd = 1 - b // 2
            high = odd if e == 1 else 1 - odd
            copy = pltpu.make_async_copy(
                w_ref.at[gathered_at(src_y, high * 2 + odd, b % 2), pl.ds(slots[0], count)],
                wbuf.at[i, :, :, pl.ds(b * LANES, LANES)],
                wsem.at[i, b],
            )
            copy.start()
            copies.append(copy)
    sums = [None] * count
    for i in range(8):
        for b in range(4):
            copies[i * 4 + b].wait()
        for j in range(count):
            prod = jnp.dot(hidden_ref[i], wbuf[i, j], preferred_element_type=F32)
            sums[j] = prod if i == 0 else sums[j] + prod
    for j in range(count):
        out_refs[j][...] = sums[j].astype(BF16)


def project(where, pieces, weights, slots):
    count = len(slots)
    return pl.pallas_call(
        functools.partial(project_kernel, slots),
        out_shape=[EXT_PIECE] * count,
        in_specs=[SMEM_SPEC] + vspecs(1) + hspecs(1),
        out_specs=vspecs(count),
        scratch_shapes=[
            pltpu.VMEM((8, count, WIDTH, WIDTH), BF16),
            pltpu.SemaphoreType.DMA((8, 4)),
        ],
        compiler_params=params(48),
        name="project",
    )(where, pieces, weights)


def li_gate_kernel(k_ref, v_ref, feat_ref, enter_ref, z_ref, load_ref, kx, vx):
    for block in range(WIDTH // LANES):
        cols = slice(block * LANES, (block + 1) * LANES)
        kx[...] = k_ref[:, cols].astype(F32)
        vx[...] = v_ref[:, cols].astype(F32)
        kf = feature(kx, 16, ROWS, feat_ref[1, :, cols])
        vf = feature(vx, 16, ROWS, feat_ref[2, :, cols])
        z = (kf * vf).astype(BF16)
        z_ref[:, cols] = z
        enter = enter_ref[:, cols]
        high = enter.astype(BF16)
        rest = (enter - high.astype(F32)).astype(BF16)
        prod = lax.dot_general(high, z, OVER_FIRST, preferred_element_type=F32)
        prod = prod + lax.dot_general(rest, z, OVER_FIRST, preferred_element_type=F32)
        load = jnp.zeros((GS, LANES), F32)
        for g in range(NG):
            load = jnp.where(own_lanes(g), prod[g * GS : (g + 1) * GS, :], load)
        load_ref[:, cols] = load


def li_gate(k, v, feat, enter):
    return pl.pallas_call(
        li_gate_kernel,
        out_shape=[PIECE, STATE],
        in_specs=vspecs(4),
        out_specs=vspecs(2),
        scratch_shapes=[pltpu.VMEM((16 + ROWS, LANES), F32)] * 2,
        compiler_params=params(),
        name="li_gate",
    )(k, v, feat, enter)


STATE = jax.ShapeDtypeStruct((GS, WIDTH), F32)


def chip_kernel(where_ref, load_ref, other_ref, rates_ref, chip_ref):
    k = where_ref[4]
    load, other = load_ref[...], other_ref[...]
    fade = jnp.exp(-rates_ref[...] * (1.0 * ROWS))
    chip_ref[...] = jnp.where(k == 0, load * fade + other, other * fade + load)


def chip_state(where, load, other, rates):
    return pl.pallas_call(
        chip_kernel,
        out_shape=STATE,
        in_specs=[SMEM_SPEC] + vspecs(3),
        out_specs=pl.BlockSpec(memory_space=pltpu.VMEM),
        compiler_params=params(),
        name="chip_state",
    )(where, load, other, rates)


def line_kernel(where_ref, c0, c1, c2, c3, rates_ref, total_ref, carry_ref):
    zl = where_ref[3]
    rates = rates_ref[...]
    total = jnp.zeros(rates.shape, F32)
    carry = jnp.zeros(rates.shape, F32)
    for s, ref in enumerate((c0, c1, c2, c3)):
        piece = ref[...]
        src = lax.rem(zl + NZ - s, NZ)
        gap = ((NZ - 1 - src) * (2 * ROWS)).astype(F32)
        total = total + jnp.exp(-rates * gap) * piece
        if s > 0:
            part = jnp.exp(-rates * (2.0 * ROWS * (s - 1))) * piece
            carry = carry + jnp.where(zl >= s, part, 0.0)
    total_ref[...] = total
    carry_ref[...] = carry


def line_state(where, pieces, rates):
    return pl.pallas_call(
        line_kernel,
        out_shape=[STATE] * 2,
        in_specs=[SMEM_SPEC] + vspecs(5),
        out_specs=vspecs(2),
        compiler_params=params(),
        name="line_state",
    )(where, *pieces, rates)


def li_inner_kernel(z_ref, toep_ref, conv_ref):
    for block in range(WIDTH // LANES):
        cols = slice(block * LANES, (block + 1) * LANES)
        first = z_ref[0:LANES, cols]
        second = z_ref[LANES:ROWS, cols]
        top, low = filtered(toep_ref, block, jnp.zeros_like(first), first, second)
        conv_ref[0:LANES, cols] = top
        conv_ref[LANES:ROWS, cols] = low


def li_inner(z, toep):
    return pl.pallas_call(
        li_inner_kernel,
        out_shape=jax.ShapeDtypeStruct((ROWS, WIDTH), F32),
        in_specs=vspecs(2),
        out_specs=pl.BlockSpec(memory_space=pltpu.VMEM),
        compiler_params=params(),
        name="li_inner",
    )(z, toep)


def li_outer_kernel(
    where_ref, conv_ref, q_ref, feat_ref, leave_ref, rates_ref,
    carry_ref, other_ref, y1_ref, y2_ref, y3_ref, w_ref,
    y_ref, o0, o1, o2, o3, qx, wbuf, sems,
):
    copies = share_loads(where_ref, w_ref, wbuf, sems, 1)
    y, zl, k = where_ref[2], where_ref[3], where_ref[4]
    rates = rates_ref[...]
    above = jnp.where(y >= 1, y1_ref[...], 0.0)
    above = above + jnp.where(y >= 2, jnp.exp(-rates * (2.0 * ROWS * NZ)) * y2_ref[...], 0.0)
    above = above + jnp.where(y >= 3, jnp.exp(-rates * (4.0 * ROWS * NZ)) * y3_ref[...], 0.0)
    chip = carry_ref[...] + jnp.exp(-rates * (zl * (2 * ROWS)).astype(F32)) * above
    full = jnp.where(k == 0, chip, jnp.exp(-rates * (1.0 * ROWS)) * chip + other_ref[...])
    for block in range(WIDTH // LANES):
        cols = slice(block * LANES, (block + 1) * LANES)
        qx[...] = q_ref[:, cols].astype(F32)
        qf = feature(qx, 16, ROWS, feat_ref[0, :, cols])
        state = full[:, cols]
        spread = jnp.concatenate(
            [jnp.where(own_lanes(g), state, 0.0) for g in range(NG)], axis=0
        )
        outer = jnp.dot(
            leave_ref[:, cols], spread, preferred_element_type=F32, precision=lax.Precision.HIGHEST
        )
        y_ref[:, cols] = (qf * (conv_ref[:, cols] + outer)).astype(BF16)
    share_products(copies, y_ref, wbuf, (o0, o1, o2, o3))


def li_outer(where, conv, q, feat, leave, rates, carry, other, above, weight):
    return pl.pallas_call(
        li_outer_kernel,
        out_shape=[PIECE] * 5,
        in_specs=[SMEM_SPEC] + vspecs(10) + hspecs(1),
        out_specs=vspecs(5),
        scratch_shapes=[pltpu.VMEM((16 + ROWS, LANES), F32)] + SHARE_SCRATCH,
        compiler_params=params(48),
        name="li_outer",
    )(where, conv, q, feat, leave, rates, carry, other, *above, weight)


def ctx_of(y, zl, k):
    return (y * NZ + zl) * NC + k


def mp_of(x, zh):
    return x * NH + zh


def x_shift(by):
    return [(mp_of(x, h), mp_of((x + by) % NX, h)) for x in range(NX) for h in range(NH)]


H_SWAP = [(mp_of(x, h), mp_of(x, 1 - h)) for x in range(NX) for h in range(NH)]
CORE_SWAP = [(i, i ^ 1) for i in range(NY * NZ * NC)]


def z_shift(by):
    return [
        (ctx_of(y, z, k), ctx_of(y, (z + by) % NZ, k))
        for y in range(NY) for z in range(NZ) for k in range(NC)
    ]


def y_shift(by):
    return [
        (ctx_of(y, z, k), ctx_of((y + by) % NY, z, k))
        for y in range(NY) for z in range(NZ) for k in range(NC)
    ]


GATHER_RING = [
    (y, z) for z in range(NZ) for y in (range(1, NY) if z % 2 == 0 else range(NY - 1, 0, -1))
] + [(0, z) for z in range(NZ - 1, -1, -1)]
GATHER_ORDER = [ctx_of(y, z, k) for y, z in GATHER_RING for k in range(NC)]


def gathered_at(y, z, k):
    along = y - 1 if z % 2 == 0 else NY - 1 - y
    return jnp.where(y == 0, NZ * (NY - 1) + NZ - 1 - z, z * (NY - 1) + along) * NC + k


def weight_moves():
    moves = []
    for y in range(NY):
        for zl in range(NZ):
            for k in range(NC):
                for x in range(NX):
                    for h in range(NH):
                        x2, h2, y2 = y, zl // 2, x
                        l0 = zl % 2
                        odd = 1 - l0
                        outer = h ^ h2
                        high = odd if outer else 1 - odd
                        z2 = high * 2 + odd
                        src = ctx_of(y, zl, k) * (NX * NH) + mp_of(x, h)
                        dst = ctx_of(y2, z2, k) * (NX * NH) + mp_of(x2, h2)
                        moves.append((src, dst))
    return moves


def tied(*values):
    return lax.optimization_barrier(values)


def sum_shares(where, y, other, weight, own_extra):
    got = [lax.ppermute(other[d], "mp", x_shift(d)) for d in (1, 3, 2)]
    total_other = other[0].astype(F32)
    for piece in got:
        total_other = total_other + piece.astype(F32)
    total_other, *mine = tied(total_other.astype(BF16), *shares(where, y, weight, 0))
    crossed = lax.ppermute(total_other, "mp", H_SWAP)
    got_mine = [lax.ppermute(mine[d], "mp", x_shift(d)) for d in (1, 3, 2)]
    (total,) = tied(own_extra.astype(F32) + mine[0].astype(F32) + crossed.astype(F32))
    for piece in got_mine:
        total = total + piece.astype(F32)
    return total.astype(BF16)


def body(
    query_mr, key_mr, value_mr, featurizer_mr, mr_taps, out_mr,
    residual, in_weight, featurizer_li, li_rates, li_residues, out_li,
):
    ctx = lax.axis_index("ctx")
    mp = lax.axis_index("mp")
    x, zh = mp // NH, mp % NH
    y, zl, k = ctx // (NZ * NC), (ctx // NC) % NZ, ctx % NC
    where = jnp.stack([x, zh, y, zl, k]).astype(jnp.int32)

    forward = [(i, i + 1) for i in range(NY * NZ * NC - 1)]
    moved = lax.ppermute(in_weight, ("ctx", "mp"), weight_moves())
    rim, query_mr, key_mr, value_mr = rim_rows(query_mr, key_mr, value_mr)
    halo = lax.ppermute(rim, "ctx", forward)
    toep_mr = toeplitz(mr_taps)
    halo, moved, toep_mr = tied(halo, moved, toep_mr)
    weights = lax.all_gather(moved, "ctx", axis_index_groups=[GATHER_ORDER])
    gated_one, *other_one = mr_op(
        where, query_mr, key_mr, value_mr, halo, featurizer_mr, toep_mr, out_mr
    )
    hidden = sum_shares(where, gated_one, other_one, out_mr, residual)
    filters = prep(li_rates.T, li_residues.T)

    before_rows = lax.ppermute(hidden[ROWS - 16 :], "ctx", forward)
    extended = jnp.concatenate([before_rows, hidden], axis=0)
    crossed = lax.ppermute(extended, "mp", H_SWAP)
    own_pieces = [extended] + [lax.ppermute(extended, "mp", x_shift(d)) for d in (1, 2, 3)]
    crossed, *filters = tied(crossed, *filters)
    toep_li, leave, enter, lane_rates = filters
    far_pieces = [crossed] + [lax.ppermute(crossed, "mp", x_shift(d)) for d in (1, 2, 3)]
    pieces = packed(own_pieces + far_pieces)
    fresh_k, fresh_v = project(where, pieces, weights, (1, 2))
    product, load = li_gate(fresh_k, fresh_v, featurizer_li, enter)
    other_load = lax.ppermute(load, "ctx", CORE_SWAP)
    chip = chip_state(where, load, other_load, lane_rates)
    before = [lax.ppermute(chip, "ctx", z_shift(s)) for s in (1, 2, 3)]
    (fresh_q,) = project(where, pieces, weights, (0,))
    *before, fresh_q = tied(*before, fresh_q)
    conv = li_inner(product, toep_li)
    line_total, line_carry = line_state(where, [chip] + before, lane_rates)
    above = [lax.ppermute(line_total, "ctx", y_shift(s)) for s in (1, 2, 3)]
    gated_two, *other_two = li_outer(
        where, conv, fresh_q, featurizer_li, leave, lane_rates,
        line_carry, other_load, above, out_li,
    )
    return sum_shares(where, gated_two, other_two, out_li, hidden)


def solution(mesh):
    return jax.shard_map(
        body,
        mesh=mesh,
        in_specs=(
            P("ctx", "mp"),
            P("ctx", "mp"),
            P("ctx", "mp"),
            P(None, None, "mp"),
            P(None, "mp"),
            P("mp", None),
            P("ctx", "mp"),
            P(None, "mp", "ctx"),
            P(None, None, "mp"),
            P("mp", None),
            P("mp", None),
            P("mp", None),
        ),
        out_specs=P("ctx", "mp"),
        check_vma=False,
    )
```

```python
import functools
import jax
import jax.numpy as jnp
from jax import lax
from jax.experimental import pallas as pl
from jax.experimental.pallas import tpu as pltpu
from jax.sharding import PartitionSpec as P

F32 = jnp.float32
BF16 = jnp.bfloat16
GS = 16
LANES = 128
NG = LANES // GS
ROWS = 256
WIDTH = 512
HALO = 144


def params(mib=16):
    return pltpu.CompilerParams(vmem_limit_bytes=mib * 1024 * 1024)


def vspecs(n):
    return [pl.BlockSpec(memory_space=pltpu.VMEM)] * n


def hspecs(n):
    return [pl.BlockSpec(memory_space=pltpu.HBM)] * n


SMEM_SPEC = pl.BlockSpec(memory_space=pltpu.SMEM)


def own_lanes(group):
    lane = lax.broadcasted_iota(jnp.int32, (1, LANES), 1)
    return (lane // GS) == group


NY, NZ, NC, NX, NH = 4, 4, 2, 4, 2

def rim_kernel(q_ref, k_ref, v_ref, out_ref, q_out, k_out, v_out, sems):
    parts = ((k_ref, HALO, 0), (v_ref, HALO, HALO), (q_ref, 16, 2 * HALO))
    copies = []
    for i, (ref, depth, at) in enumerate(parts):
        copy = pltpu.make_async_copy(
            ref.at[pl.ds(ROWS - depth, depth)], out_ref.at[pl.ds(at, depth)], sems.at[i]
        )
        copy.start()
        copies.append(copy)
    for i, (ref, out) in enumerate(((q_ref, q_out), (k_ref, k_out), (v_ref, v_out))):
        copy = pltpu.make_async_copy(ref, out, sems.at[3 + i])
        copy.start()
        copies.append(copy)
    for copy in copies:
        copy.wait()


def rim_rows(q, k, v):
    return pl.pallas_call(
        rim_kernel,
        out_shape=[jax.ShapeDtypeStruct((2 * HALO + 16, WIDTH), BF16)] + [PIECE] * 3,
        in_specs=hspecs(3),
        out_specs=vspecs(4),
        scratch_shapes=[pltpu.SemaphoreType.DMA((6,))],
        compiler_params=params(),
        name="rim_rows",
    )(q, k, v)


OVER_FIRST = (((0,), (0,)), ((), ()))


def exact(a, b):
    return lax.dot_general(a, b, OVER_FIRST, preferred_element_type=F32, precision=lax.Precision.HIGHEST)


def toeplitz_rows(near, far):
    row = lax.broadcasted_iota(jnp.int32, (LANES, LANES), 0)
    col = lax.broadcasted_iota(jnp.int32, (LANES, LANES), 1)
    near = pltpu.roll(jnp.broadcast_to(near, (LANES, LANES)), 0, 1, stride=1, stride_axis=0)
    upper = near
    if far is not None:
        far = pltpu.roll(jnp.broadcast_to(far, (LANES, LANES)), 0, 1, stride=1, stride_axis=0)
    else:
        far = 0.0
    upper = jnp.where(col > row, near, far).astype(BF16)
    lower = jnp.where(col <= row, near, 0.0).astype(BF16)
    return upper, lower


def toeplitz_kernel(taps_ref, out_ref, near):
    tap = lax.broadcasted_iota(jnp.int32, (LANES, LANES), 0)
    at = lax.broadcasted_iota(jnp.int32, (LANES, LANES), 1)
    near[...] = exact(taps_ref[...], jnp.where(tap == lax.rem(LANES - at, LANES), 1.0, 0.0))

    def one(g, carry):
        upper, lower = toeplitz_rows(near[pl.ds(g, 1), :], None)
        start = pl.multiple_of(g * LANES, LANES)
        out_ref[pl.ds(start, LANES), 0:LANES] = upper
        out_ref[pl.ds(start, LANES), LANES:] = lower
        return carry

    lax.fori_loop(0, near.shape[0], one, 0)


def toeplitz(taps):
    groups = taps.shape[1]
    return pl.pallas_call(
        toeplitz_kernel,
        out_shape=jax.ShapeDtypeStruct((groups * LANES, 2 * LANES), BF16),
        in_specs=vspecs(1),
        out_specs=pl.BlockSpec(memory_space=pltpu.VMEM),
        scratch_shapes=[pltpu.VMEM((groups, LANES), F32)],
        compiler_params=params(),
        name="toeplitz",
    )(taps)


def prep_kernel(rates_ref, res_ref, toep_ref, leave_ref, enter_ref, lane_ref, near, far):
    modes, groups = rates_ref.shape
    mode_r = lax.broadcasted_iota(jnp.int32, (modes, modes), 0)
    mode_c = lax.broadcasted_iota(jnp.int32, (modes, modes), 1)
    same = jnp.where(mode_r == mode_c, 1.0, 0.0)
    rates = exact(rates_ref[...], same)
    weights = exact(res_ref[...], same)
    back = lax.broadcasted_iota(jnp.int32, (groups, LANES), 1)
    back = jnp.where(back == 0, 0, LANES - back).astype(F32)
    near_sum = jnp.zeros((groups, LANES), F32)
    far_sum = jnp.zeros((groups, LANES), F32)
    for n in range(GS):
        rate = rates[:, n : n + 1]
        weight = weights[:, n : n + 1]
        near_sum = near_sum + weight * jnp.exp(-rate * back)
        far_sum = far_sum + weight * jnp.exp(-rate * (back + LANES))
    near[...] = near_sum
    far[...] = far_sum

    def one(g, carry):
        upper, lower = toeplitz_rows(near[pl.ds(g, 1), :], far[pl.ds(g, 1), :])
        start = pl.multiple_of(g * LANES, LANES)
        toep_ref[pl.ds(start, LANES), 0:LANES] = upper
        toep_ref[pl.ds(start, LANES), LANES:] = lower
        return carry

    lax.fori_loop(0, groups, one, 0)
    lane = lax.broadcasted_iota(jnp.int32, (groups, WIDTH), 1)
    member = lax.broadcasted_iota(jnp.int32, (groups, WIDTH), 0)
    pick = jnp.where(lane // GS == member, 1.0, 0.0)
    lane_rates = exact(rates, pick)
    lane_ref[...] = lane_rates
    lane = lax.broadcasted_iota(jnp.int32, (modes, WIDTH), 1)
    member = lax.broadcasted_iota(jnp.int32, (modes, WIDTH), 0)
    ours = lax.rem(lane, GS) == member
    rate_row = jnp.sum(jnp.where(ours, lane_rates, 0.0), axis=0, keepdims=True)
    weight_row = jnp.sum(jnp.where(ours, exact(weights, pick), 0.0), axis=0, keepdims=True)
    step = lax.broadcasted_iota(jnp.int32, (ROWS, LANES), 0).astype(F32)
    for block in range(WIDTH // LANES):
        cols = slice(block * LANES, (block + 1) * LANES)
        rate = rate_row[:, cols]
        leave_ref[:, cols] = weight_row[:, cols] * jnp.exp(-rate * step)
        enter_ref[:, cols] = jnp.exp(-rate * (ROWS - step))


def prep(rates, residues):
    groups = rates.shape[1]
    return pl.pallas_call(
        prep_kernel,
        out_shape=[
            jax.ShapeDtypeStruct((groups * LANES, 2 * LANES), BF16),
            jax.ShapeDtypeStruct((ROWS, WIDTH), F32),
            jax.ShapeDtypeStruct((ROWS, WIDTH), F32),
            jax.ShapeDtypeStruct((GS, WIDTH), F32),
        ],
        in_specs=vspecs(2),
        out_specs=vspecs(4),
        scratch_shapes=[pltpu.VMEM((groups, LANES), F32)] * 2,
        compiler_params=params(),
        name="prep",
    )(rates, residues)


def feature(ext_ref, base, rows, taps):
    total = taps[0:1] * ext_ref[pl.ds(base, rows), :]
    for k in range(1, 3):
        total = total + taps[k : k + 1] * ext_ref[pl.ds(base - k, rows), :]
    return total


def filtered(toep_ref, block, early, middle, late):
    rhs = jnp.concatenate(
        [
            jnp.concatenate([early, middle], axis=0),
            jnp.concatenate([middle, late], axis=0),
        ],
        axis=1,
    )
    top = jnp.zeros((LANES, LANES), F32)
    low = jnp.zeros((LANES, LANES), F32)
    for g in range(NG):
        start = (block * NG + g) * LANES
        prod = jnp.dot(toep_ref[start : start + LANES, :], rhs, preferred_element_type=F32)
        mine = own_lanes(g)
        top = jnp.where(mine, prod[:, :LANES], top)
        low = jnp.where(mine, prod[:, LANES:], low)
    return top, low


def share_loads(where_ref, w_ref, wbuf, sems, flip):
    x = where_ref[0]
    zh = where_ref[1]
    half = zh if flip == 0 else 1 - zh
    copies = []
    for d in range(4):
        block = lax.rem(x + d, 4) * 2 + half
        copy = pltpu.make_async_copy(
            w_ref.at[:, pl.ds(pl.multiple_of(block * WIDTH, WIDTH), WIDTH)], wbuf.at[d], sems.at[d]
        )
        copy.start()
        copies.append(copy)
    return copies


def share_products(copies, y_ref, wbuf, outs):
    for d in (1, 3, 2, 0):
        copies[d].wait()
        outs[d][...] = jnp.dot(y_ref[...], wbuf[d], preferred_element_type=F32).astype(BF16)


SHARE_SCRATCH = [pltpu.VMEM((4, WIDTH, WIDTH), BF16), pltpu.SemaphoreType.DMA((4,))]
PIECE = jax.ShapeDtypeStruct((ROWS, WIDTH), BF16)


def share_kernel(flip, where_ref, y_ref, w_ref, o0, o1, o2, o3, wbuf, sems):
    copies = share_loads(where_ref, w_ref, wbuf, sems, flip)
    share_products(copies, y_ref, wbuf, (o0, o1, o2, o3))


def shares(where, y, weight, flip):
    return pl.pallas_call(
        functools.partial(share_kernel, flip),
        out_shape=[PIECE] * 4,
        in_specs=[SMEM_SPEC] + vspecs(1) + hspecs(1),
        out_specs=vspecs(4),
        scratch_shapes=SHARE_SCRATCH,
        compiler_params=params(48),
        name="shares",
    )(where, y, weight)


def mr_kernel(
    where_ref, q_ref, k_ref, v_ref, halo_ref, feat_ref, toep_ref, w_ref,
    y_ref, o0, o1, o2, o3, kx, vx, qx, wbuf, sems,
):
    copies = share_loads(where_ref, w_ref, wbuf, sems, 1)
    for block in range(WIDTH // LANES):
        cols = slice(block * LANES, (block + 1) * LANES)
        kx[0:HALO, :] = halo_ref[0:HALO, cols].astype(F32)
        kx[HALO:, :] = k_ref[:, cols].astype(F32)
        vx[0:HALO, :] = halo_ref[HALO : 2 * HALO, cols].astype(F32)
        vx[HALO:, :] = v_ref[:, cols].astype(F32)
        qx[0:16, :] = halo_ref[2 * HALO : 2 * HALO + 16, cols].astype(F32)
        qx[16:, :] = q_ref[:, cols].astype(F32)
        zs = []
        for part in range(3):
            base = HALO - LANES + part * LANES
            kf = feature(kx, base, LANES, feat_ref[1, :, cols])
            vf = feature(vx, base, LANES, feat_ref[2, :, cols])
            zs.append((kf * vf).astype(BF16))
        top, low = filtered(toep_ref, block, *zs)
        for part, conv in ((0, top), (1, low)):
            qf = feature(qx, 16 + part * LANES, LANES, feat_ref[0, :, cols])
            y_ref[part * LANES : (part + 1) * LANES, cols] = (qf * conv).astype(BF16)
    share_products(copies, y_ref, wbuf, (o0, o1, o2, o3))


def mr_op(where, q, k, v, halo, feat, toep, weight):
    return pl.pallas_call(
        mr_kernel,
        out_shape=[PIECE] * 5,
        in_specs=[SMEM_SPEC] + vspecs(6) + hspecs(1),
        out_specs=vspecs(5),
        scratch_shapes=[
            pltpu.VMEM((HALO + ROWS, LANES), F32),
            pltpu.VMEM((HALO + ROWS, LANES), F32),
            pltpu.VMEM((16 + ROWS, LANES), F32),
        ] + SHARE_SCRATCH,
        compiler_params=params(48),
        name="mr_op",
    )(where, q, k, v, halo, feat, toep, weight)


EXT = 16 + ROWS
EXT_PIECE = jax.ShapeDtypeStruct((EXT, WIDTH), BF16)


def pack_kernel(*refs):
    for i in range(8):
        refs[8][i] = refs[i][...]


def packed(pieces):
    return pl.pallas_call(
        pack_kernel,
        out_shape=jax.ShapeDtypeStruct((8, EXT, WIDTH), BF16),
        in_specs=vspecs(8),
        out_specs=pl.BlockSpec(memory_space=pltpu.VMEM),
        compiler_params=params(),
        name="packed",
    )(*pieces)


def project_kernel(slots, where_ref, hidden_ref, w_ref, *refs):
    count = len(slots)
    out_refs = refs[:count]
    wbuf, wsem = refs[count:]
    x = where_ref[0]
    copies = []
    for i in range(8):
        e, d = i // 4, i % 4
        src_y = lax.rem(x + 6 - d, 4)
        for b in range(4):
            odd = 1 - b // 2
            high = odd if e == 1 else 1 - odd
            copy = pltpu.make_async_copy(
                w_ref.at[gathered_at(src_y, high * 2 + odd, b % 2), pl.ds(slots[0], count)],
                wbuf.at[i, :, :, pl.ds(b * LANES, LANES)],
                wsem.at[i, b],
            )
            copy.start()
            copies.append(copy)
    sums = [None] * count
    for i in range(8):
        for b in range(4):
            copies[i * 4 + b].wait()
        for j in range(count):
            prod = jnp.dot(hidden_ref[i], wbuf[i, j], preferred_element_type=F32)
            sums[j] = prod if i == 0 else sums[j] + prod
    for j in range(count):
        out_refs[j][...] = sums[j].astype(BF16)


def project(where, pieces, weights, slots):
    count = len(slots)
    return pl.pallas_call(
        functools.partial(project_kernel, slots),
        out_shape=[EXT_PIECE] * count,
        in_specs=[SMEM_SPEC] + vspecs(1) + hspecs(1),
        out_specs=vspecs(count),
        scratch_shapes=[
            pltpu.VMEM((8, count, WIDTH, WIDTH), BF16),
            pltpu.SemaphoreType.DMA((8, 4)),
        ],
        compiler_params=params(48),
        name="project",
    )(where, pieces, weights)


def li_gate_kernel(k_ref, v_ref, feat_ref, enter_ref, z_ref, load_ref, kx, vx):
    for block in range(WIDTH // LANES):
        cols = slice(block * LANES, (block + 1) * LANES)
        kx[...] = k_ref[:, cols].astype(F32)
        vx[...] = v_ref[:, cols].astype(F32)
        kf = feature(kx, 16, ROWS, feat_ref[1, :, cols])
        vf = feature(vx, 16, ROWS, feat_ref[2, :, cols])
        z = (kf * vf).astype(BF16)
        z_ref[:, cols] = z
        enter = enter_ref[:, cols]
        high = enter.astype(BF16)
        rest = (enter - high.astype(F32)).astype(BF16)
        prod = lax.dot_general(high, z, OVER_FIRST, preferred_element_type=F32)
        prod = prod + lax.dot_general(rest, z, OVER_FIRST, preferred_element_type=F32)
        load = jnp.zeros((GS, LANES), F32)
        for g in range(NG):
            load = jnp.where(own_lanes(g), prod[g * GS : (g + 1) * GS, :], load)
        load_ref[:, cols] = load


def li_gate(k, v, feat, enter):
    return pl.pallas_call(
        li_gate_kernel,
        out_shape=[PIECE, STATE],
        in_specs=vspecs(4),
        out_specs=vspecs(2),
        scratch_shapes=[pltpu.VMEM((16 + ROWS, LANES), F32)] * 2,
        compiler_params=params(),
        name="li_gate",
    )(k, v, feat, enter)


STATE = jax.ShapeDtypeStruct((GS, WIDTH), F32)


def chip_kernel(where_ref, load_ref, other_ref, rates_ref, chip_ref):
    k = where_ref[4]
    load, other = load_ref[...], other_ref[...]
    fade = jnp.exp(-rates_ref[...] * (1.0 * ROWS))
    chip_ref[...] = jnp.where(k == 0, load * fade + other, other * fade + load)


def chip_state(where, load, other, rates):
    return pl.pallas_call(
        chip_kernel,
        out_shape=STATE,
        in_specs=[SMEM_SPEC] + vspecs(3),
        out_specs=pl.BlockSpec(memory_space=pltpu.VMEM),
        compiler_params=params(),
        name="chip_state",
    )(where, load, other, rates)


def line_kernel(where_ref, c0, c1, c2, c3, rates_ref, total_ref, carry_ref):
    zl = where_ref[3]
    rates = rates_ref[...]
    total = jnp.zeros(rates.shape, F32)
    carry = jnp.zeros(rates.shape, F32)
    for s, ref in enumerate((c0, c1, c2, c3)):
        piece = ref[...]
        src = lax.rem(zl + NZ - s, NZ)
        gap = ((NZ - 1 - src) * (2 * ROWS)).astype(F32)
        total = total + jnp.exp(-rates * gap) * piece
        if s > 0:
            part = jnp.exp(-rates * (2.0 * ROWS * (s - 1))) * piece
            carry = carry + jnp.where(zl >= s, part, 0.0)
    total_ref[...] = total
    carry_ref[...] = carry


def line_state(where, pieces, rates):
    return pl.pallas_call(
        line_kernel,
        out_shape=[STATE] * 2,
        in_specs=[SMEM_SPEC] + vspecs(5),
        out_specs=vspecs(2),
        compiler_params=params(),
        name="line_state",
    )(where, *pieces, rates)


def li_inner_kernel(z_ref, toep_ref, conv_ref):
    for block in range(WIDTH // LANES):
        cols = slice(block * LANES, (block + 1) * LANES)
        first = z_ref[0:LANES, cols]
        second = z_ref[LANES:ROWS, cols]
        top, low = filtered(toep_ref, block, jnp.zeros_like(first), first, second)
        conv_ref[0:LANES, cols] = top
        conv_ref[LANES:ROWS, cols] = low


def li_inner(z, toep):
    return pl.pallas_call(
        li_inner_kernel,
        out_shape=jax.ShapeDtypeStruct((ROWS, WIDTH), F32),
        in_specs=vspecs(2),
        out_specs=pl.BlockSpec(memory_space=pltpu.VMEM),
        compiler_params=params(),
        name="li_inner",
    )(z, toep)


def li_outer_kernel(
    where_ref, conv_ref, q_ref, feat_ref, leave_ref, rates_ref,
    carry_ref, other_ref, y1_ref, y2_ref, y3_ref, w_ref,
    y_ref, o0, o1, o2, o3, qx, wbuf, sems,
):
    copies = share_loads(where_ref, w_ref, wbuf, sems, 1)
    y, zl, k = where_ref[2], where_ref[3], where_ref[4]
    rates = rates_ref[...]
    above = jnp.where(y >= 1, y1_ref[...], 0.0)
    above = above + jnp.where(y >= 2, jnp.exp(-rates * (2.0 * ROWS * NZ)) * y2_ref[...], 0.0)
    above = above + jnp.where(y >= 3, jnp.exp(-rates * (4.0 * ROWS * NZ)) * y3_ref[...], 0.0)
    chip = carry_ref[...] + jnp.exp(-rates * (zl * (2 * ROWS)).astype(F32)) * above
    full = jnp.where(k == 0, chip, jnp.exp(-rates * (1.0 * ROWS)) * chip + other_ref[...])
    for block in range(WIDTH // LANES):
        cols = slice(block * LANES, (block + 1) * LANES)
        qx[...] = q_ref[:, cols].astype(F32)
        qf = feature(qx, 16, ROWS, feat_ref[0, :, cols])
        state = full[:, cols]
        spread = jnp.concatenate(
            [jnp.where(own_lanes(g), state, 0.0) for g in range(NG)], axis=0
        )
        outer = jnp.dot(
            leave_ref[:, cols], spread, preferred_element_type=F32, precision=lax.Precision.HIGHEST
        )
        y_ref[:, cols] = (qf * (conv_ref[:, cols] + outer)).astype(BF16)
    share_products(copies, y_ref, wbuf, (o0, o1, o2, o3))


def li_outer(where, conv, q, feat, leave, rates, carry, other, above, weight):
    return pl.pallas_call(
        li_outer_kernel,
        out_shape=[PIECE] * 5,
        in_specs=[SMEM_SPEC] + vspecs(10) + hspecs(1),
        out_specs=vspecs(5),
        scratch_shapes=[pltpu.VMEM((16 + ROWS, LANES), F32)] + SHARE_SCRATCH,
        compiler_params=params(48),
        name="li_outer",
    )(where, conv, q, feat, leave, rates, carry, other, *above, weight)


def ctx_of(y, zl, k):
    return (y * NZ + zl) * NC + k


def mp_of(x, zh):
    return x * NH + zh


def x_shift(by):
    return [(mp_of(x, h), mp_of((x + by) % NX, h)) for x in range(NX) for h in range(NH)]


H_SWAP = [(mp_of(x, h), mp_of(x, 1 - h)) for x in range(NX) for h in range(NH)]
CORE_SWAP = [(i, i ^ 1) for i in range(NY * NZ * NC)]


def z_shift(by):
    return [
        (ctx_of(y, z, k), ctx_of(y, (z + by) % NZ, k))
        for y in range(NY) for z in range(NZ) for k in range(NC)
    ]


def y_shift(by):
    return [
        (ctx_of(y, z, k), ctx_of((y + by) % NY, z, k))
        for y in range(NY) for z in range(NZ) for k in range(NC)
    ]


GATHER_RING = [
    (y, z) for z in range(NZ) for y in (range(1, NY) if z % 2 == 0 else range(NY - 1, 0, -1))
] + [(0, z) for z in range(NZ - 1, -1, -1)]
GATHER_ORDER = [ctx_of(y, z, k) for y, z in GATHER_RING for k in range(NC)]


def gathered_at(y, z, k):
    along = y - 1 if z % 2 == 0 else NY - 1 - y
    return jnp.where(y == 0, NZ * (NY - 1) + NZ - 1 - z, z * (NY - 1) + along) * NC + k


def weight_moves():
    moves = []
    for y in range(NY):
        for zl in range(NZ):
            for k in range(NC):
                for x in range(NX):
                    for h in range(NH):
                        x2, h2, y2 = y, zl // 2, (x + 2) % NY
                        l0 = zl % 2
                        odd = 1 - l0
                        outer = h ^ h2
                        high = odd if outer else 1 - odd
                        z2 = high * 2 + odd
                        src = ctx_of(y, zl, k) * (NX * NH) + mp_of(x, h)
                        dst = ctx_of(y2, z2, k) * (NX * NH) + mp_of(x2, h2)
                        moves.append((src, dst))
    return moves


def tied(*values):
    return lax.optimization_barrier(values)


def sum_shares(where, y, other, weight, own_extra):
    got = [lax.ppermute(other[d], "mp", x_shift(d)) for d in (1, 3, 2)]
    total_other = other[0].astype(F32)
    for piece in got:
        total_other = total_other + piece.astype(F32)
    total_other, *mine = tied(total_other.astype(BF16), *shares(where, y, weight, 0))
    crossed = lax.ppermute(total_other, "mp", H_SWAP)
    got_mine = [lax.ppermute(mine[d], "mp", x_shift(d)) for d in (1, 3, 2)]
    (total,) = tied(own_extra.astype(F32) + mine[0].astype(F32) + crossed.astype(F32))
    for piece in got_mine:
        total = total + piece.astype(F32)
    return total.astype(BF16)


def body(
    query_mr, key_mr, value_mr, featurizer_mr, mr_taps, out_mr,
    residual, in_weight, featurizer_li, li_rates, li_residues, out_li,
):
    ctx = lax.axis_index("ctx")
    mp = lax.axis_index("mp")
    x, zh = mp // NH, mp % NH
    y, zl, k = ctx // (NZ * NC), (ctx // NC) % NZ, ctx % NC
    where = jnp.stack([x, zh, y, zl, k]).astype(jnp.int32)

    forward = [(i, i + 1) for i in range(NY * NZ * NC - 1)]
    moved = lax.ppermute(in_weight, ("ctx", "mp"), weight_moves())
    rim, query_mr, key_mr, value_mr = rim_rows(query_mr, key_mr, value_mr)
    halo = lax.ppermute(rim, "ctx", forward)
    toep_mr = toeplitz(mr_taps)
    halo, moved, toep_mr = tied(halo, moved, toep_mr)
    weights = lax.all_gather(moved, "ctx", axis_index_groups=[GATHER_ORDER])
    gated_one, *other_one = mr_op(
        where, query_mr, key_mr, value_mr, halo, featurizer_mr, toep_mr, out_mr
    )
    hidden = sum_shares(where, gated_one, other_one, out_mr, residual)
    filters = prep(li_rates.T, li_residues.T)

    before_rows = lax.ppermute(hidden[ROWS - 16 :], "ctx", forward)
    extended = jnp.concatenate([before_rows, hidden], axis=0)
    crossed = lax.ppermute(extended, "mp", H_SWAP)
    own_pieces = [extended] + [lax.ppermute(extended, "mp", x_shift(d)) for d in (1, 2, 3)]
    crossed, *filters = tied(crossed, *filters)
    toep_li, leave, enter, lane_rates = filters
    far_pieces = [crossed] + [lax.ppermute(crossed, "mp", x_shift(d)) for d in (1, 2, 3)]
    pieces = packed(own_pieces + far_pieces)
    fresh_q, fresh_k, fresh_v = project(where, pieces, weights, (0, 1, 2))
    product, load = li_gate(fresh_k, fresh_v, featurizer_li, enter)
    other_load = lax.ppermute(load, "ctx", CORE_SWAP)
    chip = chip_state(where, load, other_load, lane_rates)
    before = [lax.ppermute(chip, "ctx", z_shift(s)) for s in (1, 2, 3)]
    conv = li_inner(product, toep_li)
    *before, conv = tied(*before, conv)
    line_total, line_carry = line_state(where, [chip] + before, lane_rates)
    above = [lax.ppermute(line_total, "ctx", y_shift(s)) for s in (1, 2, 3)]
    gated_two, *other_two = li_outer(
        where, conv, fresh_q, featurizer_li, leave, lane_rates,
        line_carry, other_load, above, out_li,
    )
    return sum_shares(where, gated_two, other_two, out_li, hidden)


def solution(mesh):
    return jax.shard_map(
        body,
        mesh=mesh,
        in_specs=(
            P("ctx", "mp"),
            P("ctx", "mp"),
            P("ctx", "mp"),
            P(None, None, "mp"),
            P(None, "mp"),
            P("mp", None),
            P("ctx", "mp"),
            P(None, "mp", "ctx"),
            P(None, None, "mp"),
            P("mp", None),
            P("mp", None),
            P("mp", None),
        ),
        out_specs=P("ctx", "mp"),
        check_vma=False,
    )
```

```python
import functools
import jax
import jax.numpy as jnp
from jax import lax
from jax.experimental import pallas as pl
from jax.experimental.pallas import tpu as pltpu
from jax.sharding import PartitionSpec as P

F32 = jnp.float32
BF16 = jnp.bfloat16
GS = 16
LANES = 128
NG = LANES // GS
ROWS = 256
WIDTH = 512
HALO = 144


def params(mib=16):
    return pltpu.CompilerParams(vmem_limit_bytes=mib * 1024 * 1024)


def vspecs(n):
    return [pl.BlockSpec(memory_space=pltpu.VMEM)] * n


def hspecs(n):
    return [pl.BlockSpec(memory_space=pltpu.HBM)] * n


SMEM_SPEC = pl.BlockSpec(memory_space=pltpu.SMEM)


def own_lanes(group):
    lane = lax.broadcasted_iota(jnp.int32, (1, LANES), 1)
    return (lane // GS) == group


NY, NZ, NC, NX, NH = 4, 4, 2, 4, 2

def rim_kernel(q_ref, k_ref, v_ref, out_ref, q_out, k_out, v_out, sems):
    parts = ((k_ref, HALO, 0), (v_ref, HALO, HALO), (q_ref, 16, 2 * HALO))
    copies = []
    for i, (ref, depth, at) in enumerate(parts):
        copy = pltpu.make_async_copy(
            ref.at[pl.ds(ROWS - depth, depth)], out_ref.at[pl.ds(at, depth)], sems.at[i]
        )
        copy.start()
        copies.append(copy)
    for i, (ref, out) in enumerate(((q_ref, q_out), (k_ref, k_out), (v_ref, v_out))):
        copy = pltpu.make_async_copy(ref, out, sems.at[3 + i])
        copy.start()
        copies.append(copy)
    for copy in copies:
        copy.wait()


def rim_rows(q, k, v):
    return pl.pallas_call(
        rim_kernel,
        out_shape=[jax.ShapeDtypeStruct((2 * HALO + 16, WIDTH), BF16)] + [PIECE] * 3,
        in_specs=hspecs(3),
        out_specs=vspecs(4),
        scratch_shapes=[pltpu.SemaphoreType.DMA((6,))],
        compiler_params=params(),
        name="rim_rows",
    )(q, k, v)


OVER_FIRST = (((0,), (0,)), ((), ()))


def exact(a, b):
    return lax.dot_general(a, b, OVER_FIRST, preferred_element_type=F32, precision=lax.Precision.HIGHEST)


def toeplitz_rows(near, far):
    row = lax.broadcasted_iota(jnp.int32, (LANES, LANES), 0)
    col = lax.broadcasted_iota(jnp.int32, (LANES, LANES), 1)
    near = pltpu.roll(jnp.broadcast_to(near, (LANES, LANES)), 0, 1, stride=1, stride_axis=0)
    upper = near
    if far is not None:
        far = pltpu.roll(jnp.broadcast_to(far, (LANES, LANES)), 0, 1, stride=1, stride_axis=0)
    else:
        far = 0.0
    upper = jnp.where(col > row, near, far).astype(BF16)
    lower = jnp.where(col <= row, near, 0.0).astype(BF16)
    return upper, lower


def toeplitz_kernel(taps_ref, out_ref, near):
    tap = lax.broadcasted_iota(jnp.int32, (LANES, LANES), 0)
    at = lax.broadcasted_iota(jnp.int32, (LANES, LANES), 1)
    near[...] = exact(taps_ref[...], jnp.where(tap == lax.rem(LANES - at, LANES), 1.0, 0.0))

    def one(g, carry):
        upper, lower = toeplitz_rows(near[pl.ds(g, 1), :], None)
        start = pl.multiple_of(g * LANES, LANES)
        out_ref[pl.ds(start, LANES), 0:LANES] = upper
        out_ref[pl.ds(start, LANES), LANES:] = lower
        return carry

    lax.fori_loop(0, near.shape[0], one, 0)


def toeplitz(taps):
    groups = taps.shape[1]
    return pl.pallas_call(
        toeplitz_kernel,
        out_shape=jax.ShapeDtypeStruct((groups * LANES, 2 * LANES), BF16),
        in_specs=vspecs(1),
        out_specs=pl.BlockSpec(memory_space=pltpu.VMEM),
        scratch_shapes=[pltpu.VMEM((groups, LANES), F32)],
        compiler_params=params(),
        name="toeplitz",
    )(taps)


def prep_kernel(rates_ref, res_ref, toep_ref, leave_ref, enter_ref, lane_ref, near, far):
    modes, groups = rates_ref.shape
    mode_r = lax.broadcasted_iota(jnp.int32, (modes, modes), 0)
    mode_c = lax.broadcasted_iota(jnp.int32, (modes, modes), 1)
    same = jnp.where(mode_r == mode_c, 1.0, 0.0)
    rates = exact(rates_ref[...], same)
    weights = exact(res_ref[...], same)
    back = lax.broadcasted_iota(jnp.int32, (groups, LANES), 1)
    back = jnp.where(back == 0, 0, LANES - back).astype(F32)
    near_sum = jnp.zeros((groups, LANES), F32)
    far_sum = jnp.zeros((groups, LANES), F32)
    for n in range(GS):
        rate = rates[:, n : n + 1]
        weight = weights[:, n : n + 1]
        near_sum = near_sum + weight * jnp.exp(-rate * back)
        far_sum = far_sum + weight * jnp.exp(-rate * (back + LANES))
    near[...] = near_sum
    far[...] = far_sum

    def one(g, carry):
        upper, lower = toeplitz_rows(near[pl.ds(g, 1), :], far[pl.ds(g, 1), :])
        start = pl.multiple_of(g * LANES, LANES)
        toep_ref[pl.ds(start, LANES), 0:LANES] = upper
        toep_ref[pl.ds(start, LANES), LANES:] = lower
        return carry

    lax.fori_loop(0, groups, one, 0)
    lane = lax.broadcasted_iota(jnp.int32, (groups, WIDTH), 1)
    member = lax.broadcasted_iota(jnp.int32, (groups, WIDTH), 0)
    pick = jnp.where(lane // GS == member, 1.0, 0.0)
    lane_rates = exact(rates, pick)
    lane_ref[...] = lane_rates
    lane = lax.broadcasted_iota(jnp.int32, (modes, WIDTH), 1)
    member = lax.broadcasted_iota(jnp.int32, (modes, WIDTH), 0)
    ours = lax.rem(lane, GS) == member
    rate_row = jnp.sum(jnp.where(ours, lane_rates, 0.0), axis=0, keepdims=True)
    weight_row = jnp.sum(jnp.where(ours, exact(weights, pick), 0.0), axis=0, keepdims=True)
    step = lax.broadcasted_iota(jnp.int32, (ROWS, LANES), 0).astype(F32)
    for block in range(WIDTH // LANES):
        cols = slice(block * LANES, (block + 1) * LANES)
        rate = rate_row[:, cols]
        leave_ref[:, cols] = weight_row[:, cols] * jnp.exp(-rate * step)
        enter_ref[:, cols] = jnp.exp(-rate * (ROWS - step))


def prep(rates, residues):
    groups = rates.shape[1]
    return pl.pallas_call(
        prep_kernel,
        out_shape=[
            jax.ShapeDtypeStruct((groups * LANES, 2 * LANES), BF16),
            jax.ShapeDtypeStruct((ROWS, WIDTH), F32),
            jax.ShapeDtypeStruct((ROWS, WIDTH), F32),
            jax.ShapeDtypeStruct((GS, WIDTH), F32),
        ],
        in_specs=vspecs(2),
        out_specs=vspecs(4),
        scratch_shapes=[pltpu.VMEM((groups, LANES), F32)] * 2,
        compiler_params=params(),
        name="prep",
    )(rates, residues)


def feature(ext_ref, base, rows, taps):
    total = taps[0:1] * ext_ref[pl.ds(base, rows), :]
    for k in range(1, 3):
        total = total + taps[k : k + 1] * ext_ref[pl.ds(base - k, rows), :]
    return total


def filtered(toep_ref, block, early, middle, late):
    rhs = jnp.concatenate(
        [
            jnp.concatenate([early, middle], axis=0),
            jnp.concatenate([middle, late], axis=0),
        ],
        axis=1,
    )
    top = jnp.zeros((LANES, LANES), F32)
    low = jnp.zeros((LANES, LANES), F32)
    for g in range(NG):
        start = (block * NG + g) * LANES
        prod = jnp.dot(toep_ref[start : start + LANES, :], rhs, preferred_element_type=F32)
        mine = own_lanes(g)
        top = jnp.where(mine, prod[:, :LANES], top)
        low = jnp.where(mine, prod[:, LANES:], low)
    return top, low


def share_loads(where_ref, w_ref, wbuf, sems, flip):
    x = where_ref[0]
    zh = where_ref[1]
    half = zh if flip == 0 else 1 - zh
    copies = []
    for d in range(4):
        block = lax.rem(x + d, 4) * 2 + half
        copy = pltpu.make_async_copy(
            w_ref.at[:, pl.ds(pl.multiple_of(block * WIDTH, WIDTH), WIDTH)], wbuf.at[d], sems.at[d]
        )
        copy.start()
        copies.append(copy)
    return copies


def share_products(copies, y_ref, wbuf, outs):
    for d in (1, 3, 2, 0):
        copies[d].wait()
        outs[d][...] = jnp.dot(y_ref[...], wbuf[d], preferred_element_type=F32).astype(BF16)


SHARE_SCRATCH = [pltpu.VMEM((4, WIDTH, WIDTH), BF16), pltpu.SemaphoreType.DMA((4,))]
PIECE = jax.ShapeDtypeStruct((ROWS, WIDTH), BF16)


def share_kernel(flip, where_ref, y_ref, w_ref, o0, o1, o2, o3, wbuf, sems):
    copies = share_loads(where_ref, w_ref, wbuf, sems, flip)
    share_products(copies, y_ref, wbuf, (o0, o1, o2, o3))


def shares(where, y, weight, flip):
    return pl.pallas_call(
        functools.partial(share_kernel, flip),
        out_shape=[PIECE] * 4,
        in_specs=[SMEM_SPEC] + vspecs(1) + hspecs(1),
        out_specs=vspecs(4),
        scratch_shapes=SHARE_SCRATCH,
        compiler_params=params(48),
        name="shares",
    )(where, y, weight)


def mr_kernel(
    where_ref, q_ref, k_ref, v_ref, halo_ref, feat_ref, toep_ref, w_ref,
    y_ref, o0, o1, o2, o3, kx, vx, qx, wbuf, sems,
):
    copies = share_loads(where_ref, w_ref, wbuf, sems, 1)
    for block in range(WIDTH // LANES):
        cols = slice(block * LANES, (block + 1) * LANES)
        kx[0:HALO, :] = halo_ref[0:HALO, cols].astype(F32)
        kx[HALO:, :] = k_ref[:, cols].astype(F32)
        vx[0:HALO, :] = halo_ref[HALO : 2 * HALO, cols].astype(F32)
        vx[HALO:, :] = v_ref[:, cols].astype(F32)
        qx[0:16, :] = halo_ref[2 * HALO : 2 * HALO + 16, cols].astype(F32)
        qx[16:, :] = q_ref[:, cols].astype(F32)
        zs = []
        for part in range(3):
            base = HALO - LANES + part * LANES
            kf = feature(kx, base, LANES, feat_ref[1, :, cols])
            vf = feature(vx, base, LANES, feat_ref[2, :, cols])
            zs.append((kf * vf).astype(BF16))
        top, low = filtered(toep_ref, block, *zs)
        for part, conv in ((0, top), (1, low)):
            qf = feature(qx, 16 + part * LANES, LANES, feat_ref[0, :, cols])
            y_ref[part * LANES : (part + 1) * LANES, cols] = (qf * conv).astype(BF16)
    share_products(copies, y_ref, wbuf, (o0, o1, o2, o3))


def mr_op(where, q, k, v, halo, feat, toep, weight):
    return pl.pallas_call(
        mr_kernel,
        out_shape=[PIECE] * 5,
        in_specs=[SMEM_SPEC] + vspecs(6) + hspecs(1),
        out_specs=vspecs(5),
        scratch_shapes=[
            pltpu.VMEM((HALO + ROWS, LANES), F32),
            pltpu.VMEM((HALO + ROWS, LANES), F32),
            pltpu.VMEM((16 + ROWS, LANES), F32),
        ] + SHARE_SCRATCH,
        compiler_params=params(48),
        name="mr_op",
    )(where, q, k, v, halo, feat, toep, weight)


EXT = 16 + ROWS
EXT_PIECE = jax.ShapeDtypeStruct((EXT, WIDTH), BF16)


def pack_kernel(*refs):
    for i in range(8):
        refs[8][i] = refs[i][...]


def packed(pieces):
    return pl.pallas_call(
        pack_kernel,
        out_shape=jax.ShapeDtypeStruct((8, EXT, WIDTH), BF16),
        in_specs=vspecs(8),
        out_specs=pl.BlockSpec(memory_space=pltpu.VMEM),
        compiler_params=params(),
        name="packed",
    )(*pieces)


STATE = jax.ShapeDtypeStruct((GS, WIDTH), F32)
AHEAD = 3


def project_kernel(
    where_ref, hidden_ref, w_ref, feat_ref, enter_ref, q_ref, z_ref, load_ref, wbuf, kx, vx, wsem
):
    x = where_ref[0]

    def piece_copies(i):
        e, d = i // 4, i % 4
        src_y = lax.rem(x + 6 - d, 4)
        copies = []
        for b in range(4):
            odd = 1 - b // 2
            high = odd if e == 1 else 1 - odd
            copy = pltpu.make_async_copy(
                w_ref.at[gathered_at(src_y, high * 2 + odd, b % 2)],
                wbuf.at[i, :, :, pl.ds(b * LANES, LANES)],
                wsem.at[i, b],
            )
            copy.start()
            copies.append(copy)
        return copies

    pending = [piece_copies(i) for i in range(AHEAD)]
    sums = [None] * 3
    for i in range(8):
        for copy in pending[i]:
            copy.wait()
        if i + AHEAD < 8:
            pending.append(piece_copies(i + AHEAD))
        for j in range(3):
            prod = jnp.dot(hidden_ref[i], wbuf[i, j], preferred_element_type=F32)
            sums[j] = prod if i == 0 else sums[j] + prod
    q_ref[...] = sums[0].astype(BF16)
    for block in range(WIDTH // LANES):
        cols = slice(block * LANES, (block + 1) * LANES)
        kx[...] = sums[1][:, cols].astype(BF16).astype(F32)
        vx[...] = sums[2][:, cols].astype(BF16).astype(F32)
        kf = feature(kx, 16, ROWS, feat_ref[1, :, cols])
        vf = feature(vx, 16, ROWS, feat_ref[2, :, cols])
        z = (kf * vf).astype(BF16)
        z_ref[:, cols] = z
        enter = enter_ref[:, cols]
        high = enter.astype(BF16)
        rest = (enter - high.astype(F32)).astype(BF16)
        prod = lax.dot_general(high, z, OVER_FIRST, preferred_element_type=F32)
        prod = prod + lax.dot_general(rest, z, OVER_FIRST, preferred_element_type=F32)
        load = jnp.zeros((GS, LANES), F32)
        for g in range(NG):
            load = jnp.where(own_lanes(g), prod[g * GS : (g + 1) * GS, :], load)
        load_ref[:, cols] = load


def project(where, pieces, weights, feat, enter):
    return pl.pallas_call(
        project_kernel,
        out_shape=[EXT_PIECE, PIECE, STATE],
        in_specs=[SMEM_SPEC] + vspecs(1) + hspecs(1) + vspecs(2),
        out_specs=vspecs(3),
        scratch_shapes=[
            pltpu.VMEM((8, 3, WIDTH, WIDTH), BF16),
            pltpu.VMEM((EXT, LANES), F32),
            pltpu.VMEM((EXT, LANES), F32),
            pltpu.SemaphoreType.DMA((8, 4)),
        ],
        compiler_params=params(48),
        name="project",
    )(where, pieces, weights, feat, enter)


def chip_kernel(where_ref, load_ref, other_ref, rates_ref, chip_ref):
    k = where_ref[4]
    load, other = load_ref[...], other_ref[...]
    fade = jnp.exp(-rates_ref[...] * (1.0 * ROWS))
    chip_ref[...] = jnp.where(k == 0, load * fade + other, other * fade + load)


def chip_state(where, load, other, rates):
    return pl.pallas_call(
        chip_kernel,
        out_shape=STATE,
        in_specs=[SMEM_SPEC] + vspecs(3),
        out_specs=pl.BlockSpec(memory_space=pltpu.VMEM),
        compiler_params=params(),
        name="chip_state",
    )(where, load, other, rates)


def line_kernel(where_ref, c0, c1, c2, c3, rates_ref, total_ref, carry_ref):
    zl = where_ref[3]
    rates = rates_ref[...]
    total = jnp.zeros(rates.shape, F32)
    carry = jnp.zeros(rates.shape, F32)
    for s, ref in enumerate((c0, c1, c2, c3)):
        piece = ref[...]
        src = lax.rem(zl + NZ - s, NZ)
        gap = ((NZ - 1 - src) * (2 * ROWS)).astype(F32)
        total = total + jnp.exp(-rates * gap) * piece
        if s > 0:
            part = jnp.exp(-rates * (2.0 * ROWS * (s - 1))) * piece
            carry = carry + jnp.where(zl >= s, part, 0.0)
    total_ref[...] = total
    carry_ref[...] = carry


def line_state(where, pieces, rates):
    return pl.pallas_call(
        line_kernel,
        out_shape=[STATE] * 2,
        in_specs=[SMEM_SPEC] + vspecs(5),
        out_specs=vspecs(2),
        compiler_params=params(),
        name="line_state",
    )(where, *pieces, rates)


def li_inner_kernel(z_ref, toep_ref, conv_ref):
    for block in range(WIDTH // LANES):
        cols = slice(block * LANES, (block + 1) * LANES)
        first = z_ref[0:LANES, cols]
        second = z_ref[LANES:ROWS, cols]
        top, low = filtered(toep_ref, block, jnp.zeros_like(first), first, second)
        conv_ref[0:LANES, cols] = top
        conv_ref[LANES:ROWS, cols] = low


def li_inner(z, toep):
    return pl.pallas_call(
        li_inner_kernel,
        out_shape=jax.ShapeDtypeStruct((ROWS, WIDTH), F32),
        in_specs=vspecs(2),
        out_specs=pl.BlockSpec(memory_space=pltpu.VMEM),
        compiler_params=params(),
        name="li_inner",
    )(z, toep)


def li_outer_kernel(
    where_ref, conv_ref, q_ref, feat_ref, leave_ref, rates_ref,
    carry_ref, other_ref, y1_ref, y2_ref, y3_ref, w_ref,
    y_ref, o0, o1, o2, o3, qx, wbuf, sems,
):
    copies = share_loads(where_ref, w_ref, wbuf, sems, 1)
    y, zl, k = where_ref[2], where_ref[3], where_ref[4]
    rates = rates_ref[...]
    above = jnp.where(y >= 1, y1_ref[...], 0.0)
    above = above + jnp.where(y >= 2, jnp.exp(-rates * (2.0 * ROWS * NZ)) * y2_ref[...], 0.0)
    above = above + jnp.where(y >= 3, jnp.exp(-rates * (4.0 * ROWS * NZ)) * y3_ref[...], 0.0)
    chip = carry_ref[...] + jnp.exp(-rates * (zl * (2 * ROWS)).astype(F32)) * above
    full = jnp.where(k == 0, chip, jnp.exp(-rates * (1.0 * ROWS)) * chip + other_ref[...])
    for block in range(WIDTH // LANES):
        cols = slice(block * LANES, (block + 1) * LANES)
        qx[...] = q_ref[:, cols].astype(F32)
        qf = feature(qx, 16, ROWS, feat_ref[0, :, cols])
        state = full[:, cols]
        spread = jnp.concatenate(
            [jnp.where(own_lanes(g), state, 0.0) for g in range(NG)], axis=0
        )
        outer = jnp.dot(
            leave_ref[:, cols], spread, preferred_element_type=F32, precision=lax.Precision.HIGHEST
        )
        y_ref[:, cols] = (qf * (conv_ref[:, cols] + outer)).astype(BF16)
    share_products(copies, y_ref, wbuf, (o0, o1, o2, o3))


def li_outer(where, conv, q, feat, leave, rates, carry, other, above, weight):
    return pl.pallas_call(
        li_outer_kernel,
        out_shape=[PIECE] * 5,
        in_specs=[SMEM_SPEC] + vspecs(10) + hspecs(1),
        out_specs=vspecs(5),
        scratch_shapes=[pltpu.VMEM((16 + ROWS, LANES), F32)] + SHARE_SCRATCH,
        compiler_params=params(48),
        name="li_outer",
    )(where, conv, q, feat, leave, rates, carry, other, *above, weight)


def ctx_of(y, zl, k):
    return (y * NZ + zl) * NC + k


def mp_of(x, zh):
    return x * NH + zh


def x_shift(by):
    return [(mp_of(x, h), mp_of((x + by) % NX, h)) for x in range(NX) for h in range(NH)]


H_SWAP = [(mp_of(x, h), mp_of(x, 1 - h)) for x in range(NX) for h in range(NH)]
CORE_SWAP = [(i, i ^ 1) for i in range(NY * NZ * NC)]


def z_shift(by):
    return [
        (ctx_of(y, z, k), ctx_of(y, (z + by) % NZ, k))
        for y in range(NY) for z in range(NZ) for k in range(NC)
    ]


def y_shift(by):
    return [
        (ctx_of(y, z, k), ctx_of((y + by) % NY, z, k))
        for y in range(NY) for z in range(NZ) for k in range(NC)
    ]


GATHER_RING = [
    (y, z) for z in range(NZ) for y in (range(1, NY) if z % 2 == 0 else range(NY - 1, 0, -1))
] + [(0, z) for z in range(NZ - 1, -1, -1)]
GATHER_ORDER = [ctx_of(y, z, k) for y, z in GATHER_RING for k in range(NC)]


def gathered_at(y, z, k):
    along = y - 1 if z % 2 == 0 else NY - 1 - y
    return jnp.where(y == 0, NZ * (NY - 1) + NZ - 1 - z, z * (NY - 1) + along) * NC + k


def weight_moves():
    moves = []
    for y in range(NY):
        for zl in range(NZ):
            for k in range(NC):
                for x in range(NX):
                    for h in range(NH):
                        x2, h2, y2 = y, zl // 2, (x + 2) % NY
                        l0 = zl % 2
                        odd = 1 - l0
                        outer = h ^ h2
                        high = odd if outer else 1 - odd
                        z2 = high * 2 + odd
                        src = ctx_of(y, zl, k) * (NX * NH) + mp_of(x, h)
                        dst = ctx_of(y2, z2, k) * (NX * NH) + mp_of(x2, h2)
                        moves.append((src, dst))
    return moves


def tied(*values):
    return lax.optimization_barrier(values)


def sum_shares(where, y, other, weight, own_extra):
    got = [lax.ppermute(other[d], "mp", x_shift(d)) for d in (1, 3, 2)]
    total_other = other[0].astype(F32)
    for piece in got:
        total_other = total_other + piece.astype(F32)
    total_other, *mine = tied(total_other.astype(BF16), *shares(where, y, weight, 0))
    crossed = lax.ppermute(total_other, "mp", H_SWAP)
    got_mine = [lax.ppermute(mine[d], "mp", x_shift(d)) for d in (1, 3, 2)]
    (total,) = tied(own_extra.astype(F32) + mine[0].astype(F32) + crossed.astype(F32))
    for piece in got_mine:
        total = total + piece.astype(F32)
    return total.astype(BF16)


def body(
    query_mr, key_mr, value_mr, featurizer_mr, mr_taps, out_mr,
    residual, in_weight, featurizer_li, li_rates, li_residues, out_li,
):
    ctx = lax.axis_index("ctx")
    mp = lax.axis_index("mp")
    x, zh = mp // NH, mp % NH
    y, zl, k = ctx // (NZ * NC), (ctx // NC) % NZ, ctx % NC
    where = jnp.stack([x, zh, y, zl, k]).astype(jnp.int32)

    forward = [(i, i + 1) for i in range(NY * NZ * NC - 1)]
    moved = lax.ppermute(in_weight, ("ctx", "mp"), weight_moves())
    rim, query_mr, key_mr, value_mr = rim_rows(query_mr, key_mr, value_mr)
    halo = lax.ppermute(rim, "ctx", forward)
    toep_mr = toeplitz(mr_taps)
    halo, moved, toep_mr = tied(halo, moved, toep_mr)
    weights = lax.all_gather(moved, "ctx", axis_index_groups=[GATHER_ORDER])
    gated_one, *other_one = mr_op(
        where, query_mr, key_mr, value_mr, halo, featurizer_mr, toep_mr, out_mr
    )
    hidden = sum_shares(where, gated_one, other_one, out_mr, residual)
    filters = prep(li_rates.T, li_residues.T)

    before_rows = lax.ppermute(hidden[ROWS - 16 :], "ctx", forward)
    extended = jnp.concatenate([before_rows, hidden], axis=0)
    crossed = lax.ppermute(extended, "mp", H_SWAP)
    own_pieces = [extended] + [lax.ppermute(extended, "mp", x_shift(d)) for d in (1, 2, 3)]
    crossed, *filters = tied(crossed, *filters)
    toep_li, leave, enter, lane_rates = filters
    far_pieces = [crossed] + [lax.ppermute(crossed, "mp", x_shift(d)) for d in (1, 2, 3)]
    pieces = packed(own_pieces + far_pieces)
    fresh_q, product, load = project(where, pieces, weights, featurizer_li, enter)
    other_load = lax.ppermute(load, "ctx", CORE_SWAP)
    chip = chip_state(where, load, other_load, lane_rates)
    before = [lax.ppermute(chip, "ctx", z_shift(s)) for s in (1, 2, 3)]
    conv = li_inner(product, toep_li)
    *before, conv = tied(*before, conv)
    line_total, line_carry = line_state(where, [chip] + before, lane_rates)
    above = [lax.ppermute(line_total, "ctx", y_shift(s)) for s in (1, 2, 3)]
    gated_two, *other_two = li_outer(
        where, conv, fresh_q, featurizer_li, leave, lane_rates,
        line_carry, other_load, above, out_li,
    )
    return sum_shares(where, gated_two, other_two, out_li, hidden)


def solution(mesh):
    return jax.shard_map(
        body,
        mesh=mesh,
        in_specs=(
            P("ctx", "mp"),
            P("ctx", "mp"),
            P("ctx", "mp"),
            P(None, None, "mp"),
            P(None, "mp"),
            P("mp", None),
            P("ctx", "mp"),
            P(None, "mp", "ctx"),
            P(None, None, "mp"),
            P("mp", None),
            P("mp", None),
            P("mp", None),
        ),
        out_specs=P("ctx", "mp"),
        check_vma=False,
    )
```

```python
import functools
import jax
import jax.numpy as jnp
from jax import lax
from jax.experimental import pallas as pl
from jax.experimental.pallas import tpu as pltpu
from jax.sharding import PartitionSpec as P

F32 = jnp.float32
BF16 = jnp.bfloat16
GS = 16
LANES = 128
NG = LANES // GS
ROWS = 256
WIDTH = 512
HALO = 144


def params(mib=16):
    return pltpu.CompilerParams(vmem_limit_bytes=mib * 1024 * 1024)


def vspecs(n):
    return [pl.BlockSpec(memory_space=pltpu.VMEM)] * n


def hspecs(n):
    return [pl.BlockSpec(memory_space=pltpu.HBM)] * n


SMEM_SPEC = pl.BlockSpec(memory_space=pltpu.SMEM)


def own_lanes(group):
    lane = lax.broadcasted_iota(jnp.int32, (1, LANES), 1)
    return (lane // GS) == group


NY, NZ, NC, NX, NH = 4, 4, 2, 4, 2

def rim_kernel(q_ref, k_ref, v_ref, out_ref, q_out, k_out, v_out, sems):
    parts = ((k_ref, HALO, 0), (v_ref, HALO, HALO), (q_ref, 16, 2 * HALO))
    copies = []
    for i, (ref, depth, at) in enumerate(parts):
        copy = pltpu.make_async_copy(
            ref.at[pl.ds(ROWS - depth, depth)], out_ref.at[pl.ds(at, depth)], sems.at[i]
        )
        copy.start()
        copies.append(copy)
    for i, (ref, out) in enumerate(((q_ref, q_out), (k_ref, k_out), (v_ref, v_out))):
        copy = pltpu.make_async_copy(ref, out, sems.at[3 + i])
        copy.start()
        copies.append(copy)
    for copy in copies:
        copy.wait()


def rim_rows(q, k, v):
    return pl.pallas_call(
        rim_kernel,
        out_shape=[jax.ShapeDtypeStruct((2 * HALO + 16, WIDTH), BF16)] + [PIECE] * 3,
        in_specs=hspecs(3),
        out_specs=vspecs(4),
        scratch_shapes=[pltpu.SemaphoreType.DMA((6,))],
        compiler_params=params(),
        name="rim_rows",
    )(q, k, v)


OVER_FIRST = (((0,), (0,)), ((), ()))


def exact(a, b):
    return lax.dot_general(a, b, OVER_FIRST, preferred_element_type=F32, precision=lax.Precision.HIGHEST)


def toeplitz_rows(near, far):
    row = lax.broadcasted_iota(jnp.int32, (LANES, LANES), 0)
    col = lax.broadcasted_iota(jnp.int32, (LANES, LANES), 1)
    near = pltpu.roll(jnp.broadcast_to(near, (LANES, LANES)), 0, 1, stride=1, stride_axis=0)
    upper = near
    if far is not None:
        far = pltpu.roll(jnp.broadcast_to(far, (LANES, LANES)), 0, 1, stride=1, stride_axis=0)
    else:
        far = 0.0
    upper = jnp.where(col > row, near, far).astype(BF16)
    lower = jnp.where(col <= row, near, 0.0).astype(BF16)
    return upper, lower


def toeplitz_kernel(taps_ref, out_ref, near):
    tap = lax.broadcasted_iota(jnp.int32, (LANES, LANES), 0)
    at = lax.broadcasted_iota(jnp.int32, (LANES, LANES), 1)
    near[...] = exact(taps_ref[...], jnp.where(tap == lax.rem(LANES - at, LANES), 1.0, 0.0))

    def one(g, carry):
        upper, lower = toeplitz_rows(near[pl.ds(g, 1), :], None)
        start = pl.multiple_of(g * LANES, LANES)
        out_ref[pl.ds(start, LANES), 0:LANES] = upper
        out_ref[pl.ds(start, LANES), LANES:] = lower
        return carry

    lax.fori_loop(0, near.shape[0], one, 0)


def toeplitz(taps):
    groups = taps.shape[1]
    return pl.pallas_call(
        toeplitz_kernel,
        out_shape=jax.ShapeDtypeStruct((groups * LANES, 2 * LANES), BF16),
        in_specs=vspecs(1),
        out_specs=pl.BlockSpec(memory_space=pltpu.VMEM),
        scratch_shapes=[pltpu.VMEM((groups, LANES), F32)],
        compiler_params=params(),
        name="toeplitz",
    )(taps)


def prep_kernel(rates_ref, res_ref, toep_ref, leave_ref, enter_ref, lane_ref, near, far):
    modes, groups = rates_ref.shape
    mode_r = lax.broadcasted_iota(jnp.int32, (modes, modes), 0)
    mode_c = lax.broadcasted_iota(jnp.int32, (modes, modes), 1)
    same = jnp.where(mode_r == mode_c, 1.0, 0.0)
    rates = exact(rates_ref[...], same)
    weights = exact(res_ref[...], same)
    back = lax.broadcasted_iota(jnp.int32, (groups, LANES), 1)
    back = jnp.where(back == 0, 0, LANES - back).astype(F32)
    near_sum = jnp.zeros((groups, LANES), F32)
    far_sum = jnp.zeros((groups, LANES), F32)
    for n in range(GS):
        rate = rates[:, n : n + 1]
        weight = weights[:, n : n + 1]
        near_sum = near_sum + weight * jnp.exp(-rate * back)
        far_sum = far_sum + weight * jnp.exp(-rate * (back + LANES))
    near[...] = near_sum
    far[...] = far_sum

    def one(g, carry):
        upper, lower = toeplitz_rows(near[pl.ds(g, 1), :], far[pl.ds(g, 1), :])
        start = pl.multiple_of(g * LANES, LANES)
        toep_ref[pl.ds(start, LANES), 0:LANES] = upper
        toep_ref[pl.ds(start, LANES), LANES:] = lower
        return carry

    lax.fori_loop(0, groups, one, 0)
    lane = lax.broadcasted_iota(jnp.int32, (groups, WIDTH), 1)
    member = lax.broadcasted_iota(jnp.int32, (groups, WIDTH), 0)
    pick = jnp.where(lane // GS == member, 1.0, 0.0)
    lane_rates = exact(rates, pick)
    lane_ref[...] = lane_rates
    lane = lax.broadcasted_iota(jnp.int32, (modes, WIDTH), 1)
    member = lax.broadcasted_iota(jnp.int32, (modes, WIDTH), 0)
    ours = lax.rem(lane, GS) == member
    rate_row = jnp.sum(jnp.where(ours, lane_rates, 0.0), axis=0, keepdims=True)
    weight_row = jnp.sum(jnp.where(ours, exact(weights, pick), 0.0), axis=0, keepdims=True)
    step = lax.broadcasted_iota(jnp.int32, (ROWS, LANES), 0).astype(F32)
    for block in range(WIDTH // LANES):
        cols = slice(block * LANES, (block + 1) * LANES)
        rate = rate_row[:, cols]
        leave_ref[:, cols] = weight_row[:, cols] * jnp.exp(-rate * step)
        enter_ref[:, cols] = jnp.exp(-rate * (ROWS - step))


def prep(rates, residues):
    groups = rates.shape[1]
    return pl.pallas_call(
        prep_kernel,
        out_shape=[
            jax.ShapeDtypeStruct((groups * LANES, 2 * LANES), BF16),
            jax.ShapeDtypeStruct((ROWS, WIDTH), F32),
            jax.ShapeDtypeStruct((ROWS, WIDTH), F32),
            jax.ShapeDtypeStruct((GS, WIDTH), F32),
        ],
        in_specs=vspecs(2),
        out_specs=vspecs(4),
        scratch_shapes=[pltpu.VMEM((groups, LANES), F32)] * 2,
        compiler_params=params(),
        name="prep",
    )(rates, residues)


def feature(ext_ref, base, rows, taps):
    total = taps[0:1] * ext_ref[pl.ds(base, rows), :]
    for k in range(1, 3):
        total = total + taps[k : k + 1] * ext_ref[pl.ds(base - k, rows), :]
    return total


def filtered(toep_ref, block, early, middle, late):
    rhs = jnp.concatenate(
        [
            jnp.concatenate([early, middle], axis=0),
            jnp.concatenate([middle, late], axis=0),
        ],
        axis=1,
    )
    top = jnp.zeros((LANES, LANES), F32)
    low = jnp.zeros((LANES, LANES), F32)
    for g in range(NG):
        start = (block * NG + g) * LANES
        prod = jnp.dot(toep_ref[start : start + LANES, :], rhs, preferred_element_type=F32)
        mine = own_lanes(g)
        top = jnp.where(mine, prod[:, :LANES], top)
        low = jnp.where(mine, prod[:, LANES:], low)
    return top, low


def share_loads(where_ref, w_ref, wbuf, sems, flip):
    x = where_ref[0]
    zh = where_ref[1]
    half = zh if flip == 0 else 1 - zh
    copies = []
    for d in range(4):
        block = lax.rem(x + d, 4) * 2 + half
        copy = pltpu.make_async_copy(
            w_ref.at[:, pl.ds(pl.multiple_of(block * WIDTH, WIDTH), WIDTH)], wbuf.at[d], sems.at[d]
        )
        copy.start()
        copies.append(copy)
    return copies


def share_products(copies, y_ref, wbuf, outs):
    for d in (1, 3, 2, 0):
        copies[d].wait()
        outs[d][...] = jnp.dot(y_ref[...], wbuf[d], preferred_element_type=F32).astype(BF16)


SHARE_SCRATCH = [pltpu.VMEM((4, WIDTH, WIDTH), BF16), pltpu.SemaphoreType.DMA((4,))]
PIECE = jax.ShapeDtypeStruct((ROWS, WIDTH), BF16)


def share_kernel(flip, where_ref, y_ref, w_ref, o0, o1, o2, o3, wbuf, sems):
    copies = share_loads(where_ref, w_ref, wbuf, sems, flip)
    share_products(copies, y_ref, wbuf, (o0, o1, o2, o3))


def shares(where, y, weight, flip):
    return pl.pallas_call(
        functools.partial(share_kernel, flip),
        out_shape=[PIECE] * 4,
        in_specs=[SMEM_SPEC] + vspecs(1) + hspecs(1),
        out_specs=vspecs(4),
        scratch_shapes=SHARE_SCRATCH,
        compiler_params=params(48),
        name="shares",
    )(where, y, weight)


def mr_kernel(
    where_ref, q_ref, k_ref, v_ref, halo_ref, feat_ref, toep_ref, w_ref,
    y_ref, o0, o1, o2, o3, kx, vx, qx, wbuf, sems,
):
    copies = share_loads(where_ref, w_ref, wbuf, sems, 1)
    for block in range(WIDTH // LANES):
        cols = slice(block * LANES, (block + 1) * LANES)
        kx[0:HALO, :] = halo_ref[0:HALO, cols].astype(F32)
        kx[HALO:, :] = k_ref[:, cols].astype(F32)
        vx[0:HALO, :] = halo_ref[HALO : 2 * HALO, cols].astype(F32)
        vx[HALO:, :] = v_ref[:, cols].astype(F32)
        qx[0:16, :] = halo_ref[2 * HALO : 2 * HALO + 16, cols].astype(F32)
        qx[16:, :] = q_ref[:, cols].astype(F32)
        zs = []
        for part in range(3):
            base = HALO - LANES + part * LANES
            kf = feature(kx, base, LANES, feat_ref[1, :, cols])
            vf = feature(vx, base, LANES, feat_ref[2, :, cols])
            zs.append((kf * vf).astype(BF16))
        top, low = filtered(toep_ref, block, *zs)
        for part, conv in ((0, top), (1, low)):
            qf = feature(qx, 16 + part * LANES, LANES, feat_ref[0, :, cols])
            y_ref[part * LANES : (part + 1) * LANES, cols] = (qf * conv).astype(BF16)
    share_products(copies, y_ref, wbuf, (o0, o1, o2, o3))


def mr_op(where, q, k, v, halo, feat, toep, weight):
    return pl.pallas_call(
        mr_kernel,
        out_shape=[PIECE] * 5,
        in_specs=[SMEM_SPEC] + vspecs(6) + hspecs(1),
        out_specs=vspecs(5),
        scratch_shapes=[
            pltpu.VMEM((HALO + ROWS, LANES), F32),
            pltpu.VMEM((HALO + ROWS, LANES), F32),
            pltpu.VMEM((16 + ROWS, LANES), F32),
        ] + SHARE_SCRATCH,
        compiler_params=params(48),
        name="mr_op",
    )(where, q, k, v, halo, feat, toep, weight)


EXT = 16 + ROWS
EXT_PIECE = jax.ShapeDtypeStruct((EXT, WIDTH), BF16)


def pack_kernel(*refs):
    for i in range(8):
        refs[8][i // 2, :, (i % 2) * WIDTH : (i % 2 + 1) * WIDTH] = refs[i][...]


def packed(pieces):
    return pl.pallas_call(
        pack_kernel,
        out_shape=jax.ShapeDtypeStruct((4, EXT, 2 * WIDTH), BF16),
        in_specs=vspecs(8),
        out_specs=pl.BlockSpec(memory_space=pltpu.VMEM),
        compiler_params=params(),
        name="packed",
    )(*pieces)


STATE = jax.ShapeDtypeStruct((GS, WIDTH), F32)
AHEAD = 4


def project_kernel(
    where_ref, hidden_ref, w_ref, feat_ref, enter_ref, q_ref, z_ref, load_ref, wbuf, kx, vx, wsem
):
    x = where_ref[0]

    def piece_copies(i):
        e, d = i // 4, i % 4
        src_y = lax.rem(x + 6 - d, 4)
        copies = []
        for b in range(4):
            odd = 1 - b // 2
            high = odd if e == 1 else 1 - odd
            copy = pltpu.make_async_copy(
                w_ref.at[gathered_at(src_y, high * 2 + odd, b % 2)],
                wbuf.at[i // 2, :, pl.ds((i % 2) * WIDTH, WIDTH), pl.ds(b * LANES, LANES)],
                wsem.at[i, b],
            )
            copy.start()
            copies.append(copy)
        return copies

    pending = [piece_copies(i) for i in range(AHEAD)]
    sums = [None] * 3
    for pair in range(4):
        for copy in pending[2 * pair] + pending[2 * pair + 1]:
            copy.wait()
        for i in range(2 * pair + AHEAD, min(8, 2 * pair + 2 + AHEAD)):
            pending.append(piece_copies(i))
        for j in range(3):
            prod = jnp.dot(hidden_ref[pair], wbuf[pair, j], preferred_element_type=F32)
            sums[j] = prod if pair == 0 else sums[j] + prod
    q_ref[...] = sums[0].astype(BF16)
    for block in range(WIDTH // LANES):
        cols = slice(block * LANES, (block + 1) * LANES)
        kx[...] = sums[1][:, cols].astype(BF16).astype(F32)
        vx[...] = sums[2][:, cols].astype(BF16).astype(F32)
        kf = feature(kx, 16, ROWS, feat_ref[1, :, cols])
        vf = feature(vx, 16, ROWS, feat_ref[2, :, cols])
        z = (kf * vf).astype(BF16)
        z_ref[:, cols] = z
        enter = enter_ref[:, cols]
        high = enter.astype(BF16)
        rest = (enter - high.astype(F32)).astype(BF16)
        prod = lax.dot_general(high, z, OVER_FIRST, preferred_element_type=F32)
        prod = prod + lax.dot_general(rest, z, OVER_FIRST, preferred_element_type=F32)
        load = jnp.zeros((GS, LANES), F32)
        for g in range(NG):
            load = jnp.where(own_lanes(g), prod[g * GS : (g + 1) * GS, :], load)
        load_ref[:, cols] = load


def project(where, pieces, weights, feat, enter):
    return pl.pallas_call(
        project_kernel,
        out_shape=[EXT_PIECE, PIECE, STATE],
        in_specs=[SMEM_SPEC] + vspecs(1) + hspecs(1) + vspecs(2),
        out_specs=vspecs(3),
        scratch_shapes=[
            pltpu.VMEM((4, 3, 2 * WIDTH, WIDTH), BF16),
            pltpu.VMEM((EXT, LANES), F32),
            pltpu.VMEM((EXT, LANES), F32),
            pltpu.SemaphoreType.DMA((8, 4)),
        ],
        compiler_params=params(48),
        name="project",
    )(where, pieces, weights, feat, enter)


def chip_kernel(where_ref, load_ref, other_ref, rates_ref, chip_ref):
    k = where_ref[4]
    load, other = load_ref[...], other_ref[...]
    fade = jnp.exp(-rates_ref[...] * (1.0 * ROWS))
    chip_ref[...] = jnp.where(k == 0, load * fade + other, other * fade + load)


def chip_state(where, load, other, rates):
    return pl.pallas_call(
        chip_kernel,
        out_shape=STATE,
        in_specs=[SMEM_SPEC] + vspecs(3),
        out_specs=pl.BlockSpec(memory_space=pltpu.VMEM),
        compiler_params=params(),
        name="chip_state",
    )(where, load, other, rates)


def line_kernel(where_ref, c0, c1, c2, c3, rates_ref, total_ref, carry_ref):
    zl = where_ref[3]
    rates = rates_ref[...]
    total = jnp.zeros(rates.shape, F32)
    carry = jnp.zeros(rates.shape, F32)
    for s, ref in enumerate((c0, c1, c2, c3)):
        piece = ref[...]
        src = lax.rem(zl + NZ - s, NZ)
        gap = ((NZ - 1 - src) * (2 * ROWS)).astype(F32)
        total = total + jnp.exp(-rates * gap) * piece
        if s > 0:
            part = jnp.exp(-rates * (2.0 * ROWS * (s - 1))) * piece
            carry = carry + jnp.where(zl >= s, part, 0.0)
    total_ref[...] = total
    carry_ref[...] = carry


def line_state(where, pieces, rates):
    return pl.pallas_call(
        line_kernel,
        out_shape=[STATE] * 2,
        in_specs=[SMEM_SPEC] + vspecs(5),
        out_specs=vspecs(2),
        compiler_params=params(),
        name="line_state",
    )(where, *pieces, rates)


def li_inner_kernel(z_ref, toep_ref, conv_ref):
    for block in range(WIDTH // LANES):
        cols = slice(block * LANES, (block + 1) * LANES)
        first = z_ref[0:LANES, cols]
        second = z_ref[LANES:ROWS, cols]
        top, low = filtered(toep_ref, block, jnp.zeros_like(first), first, second)
        conv_ref[0:LANES, cols] = top
        conv_ref[LANES:ROWS, cols] = low


def li_inner(z, toep):
    return pl.pallas_call(
        li_inner_kernel,
        out_shape=jax.ShapeDtypeStruct((ROWS, WIDTH), F32),
        in_specs=vspecs(2),
        out_specs=pl.BlockSpec(memory_space=pltpu.VMEM),
        compiler_params=params(),
        name="li_inner",
    )(z, toep)


def li_outer_kernel(
    where_ref, conv_ref, q_ref, feat_ref, leave_ref, rates_ref,
    carry_ref, other_ref, y1_ref, y2_ref, y3_ref, w_ref,
    y_ref, o0, o1, o2, o3, qx, wbuf, sems,
):
    copies = share_loads(where_ref, w_ref, wbuf, sems, 1)
    y, zl, k = where_ref[2], where_ref[3], where_ref[4]
    rates = rates_ref[...]
    above = jnp.where(y >= 1, y1_ref[...], 0.0)
    above = above + jnp.where(y >= 2, jnp.exp(-rates * (2.0 * ROWS * NZ)) * y2_ref[...], 0.0)
    above = above + jnp.where(y >= 3, jnp.exp(-rates * (4.0 * ROWS * NZ)) * y3_ref[...], 0.0)
    chip = carry_ref[...] + jnp.exp(-rates * (zl * (2 * ROWS)).astype(F32)) * above
    full = jnp.where(k == 0, chip, jnp.exp(-rates * (1.0 * ROWS)) * chip + other_ref[...])
    for block in range(WIDTH // LANES):
        cols = slice(block * LANES, (block + 1) * LANES)
        qx[...] = q_ref[:, cols].astype(F32)
        qf = feature(qx, 16, ROWS, feat_ref[0, :, cols])
        state = full[:, cols]
        spread = jnp.concatenate(
            [jnp.where(own_lanes(g), state, 0.0) for g in range(NG)], axis=0
        )
        outer = jnp.dot(
            leave_ref[:, cols], spread, preferred_element_type=F32, precision=lax.Precision.HIGHEST
        )
        y_ref[:, cols] = (qf * (conv_ref[:, cols] + outer)).astype(BF16)
    share_products(copies, y_ref, wbuf, (o0, o1, o2, o3))


def li_outer(where, conv, q, feat, leave, rates, carry, other, above, weight):
    return pl.pallas_call(
        li_outer_kernel,
        out_shape=[PIECE] * 5,
        in_specs=[SMEM_SPEC] + vspecs(10) + hspecs(1),
        out_specs=vspecs(5),
        scratch_shapes=[pltpu.VMEM((16 + ROWS, LANES), F32)] + SHARE_SCRATCH,
        compiler_params=params(48),
        name="li_outer",
    )(where, conv, q, feat, leave, rates, carry, other, *above, weight)


def ctx_of(y, zl, k):
    return (y * NZ + zl) * NC + k


def mp_of(x, zh):
    return x * NH + zh


def x_shift(by):
    return [(mp_of(x, h), mp_of((x + by) % NX, h)) for x in range(NX) for h in range(NH)]


H_SWAP = [(mp_of(x, h), mp_of(x, 1 - h)) for x in range(NX) for h in range(NH)]
CORE_SWAP = [(i, i ^ 1) for i in range(NY * NZ * NC)]


def z_shift(by):
    return [
        (ctx_of(y, z, k), ctx_of(y, (z + by) % NZ, k))
        for y in range(NY) for z in range(NZ) for k in range(NC)
    ]


def y_shift(by):
    return [
        (ctx_of(y, z, k), ctx_of((y + by) % NY, z, k))
        for y in range(NY) for z in range(NZ) for k in range(NC)
    ]


GATHER_RING = [
    (y, z) for z in range(NZ) for y in (range(1, NY) if z % 2 == 0 else range(NY - 1, 0, -1))
] + [(0, z) for z in range(NZ - 1, -1, -1)]
GATHER_ORDER = [ctx_of(y, z, k) for y, z in GATHER_RING for k in range(NC)]


def gathered_at(y, z, k):
    along = y - 1 if z % 2 == 0 else NY - 1 - y
    return jnp.where(y == 0, NZ * (NY - 1) + NZ - 1 - z, z * (NY - 1) + along) * NC + k


def weight_moves():
    moves = []
    for y in range(NY):
        for zl in range(NZ):
            for k in range(NC):
                for x in range(NX):
                    for h in range(NH):
                        x2, h2, y2 = y, zl // 2, (x + 2) % NY
                        l0 = zl % 2
                        odd = 1 - l0
                        outer = h ^ h2
                        high = odd if outer else 1 - odd
                        z2 = high * 2 + odd
                        src = ctx_of(y, zl, k) * (NX * NH) + mp_of(x, h)
                        dst = ctx_of(y2, z2, k) * (NX * NH) + mp_of(x2, h2)
                        moves.append((src, dst))
    return moves


def tied(*values):
    return lax.optimization_barrier(values)


def sum_shares(where, y, other, weight, own_extra):
    got = [lax.ppermute(other[d], "mp", x_shift(d)) for d in (1, 3, 2)]
    total_other = other[0].astype(F32)
    for piece in got:
        total_other = total_other + piece.astype(F32)
    total_other, *mine = tied(total_other.astype(BF16), *shares(where, y, weight, 0))
    crossed = lax.ppermute(total_other, "mp", H_SWAP)
    got_mine = [lax.ppermute(mine[d], "mp", x_shift(d)) for d in (1, 3, 2)]
    (total,) = tied(own_extra.astype(F32) + mine[0].astype(F32) + crossed.astype(F32))
    for piece in got_mine:
        total = total + piece.astype(F32)
    return total.astype(BF16)


def body(
    query_mr, key_mr, value_mr, featurizer_mr, mr_taps, out_mr,
    residual, in_weight, featurizer_li, li_rates, li_residues, out_li,
):
    ctx = lax.axis_index("ctx")
    mp = lax.axis_index("mp")
    x, zh = mp // NH, mp % NH
    y, zl, k = ctx // (NZ * NC), (ctx // NC) % NZ, ctx % NC
    where = jnp.stack([x, zh, y, zl, k]).astype(jnp.int32)

    forward = [(i, i + 1) for i in range(NY * NZ * NC - 1)]
    moved = lax.ppermute(in_weight, ("ctx", "mp"), weight_moves())
    rim, query_mr, key_mr, value_mr = rim_rows(query_mr, key_mr, value_mr)
    halo = lax.ppermute(rim, "ctx", forward)
    toep_mr = toeplitz(mr_taps)
    halo, moved, toep_mr = tied(halo, moved, toep_mr)
    weights = lax.all_gather(moved, "ctx", axis_index_groups=[GATHER_ORDER])
    gated_one, *other_one = mr_op(
        where, query_mr, key_mr, value_mr, halo, featurizer_mr, toep_mr, out_mr
    )
    hidden = sum_shares(where, gated_one, other_one, out_mr, residual)
    filters = prep(li_rates.T, li_residues.T)

    before_rows = lax.ppermute(hidden[ROWS - 16 :], "ctx", forward)
    extended = jnp.concatenate([before_rows, hidden], axis=0)
    crossed = lax.ppermute(extended, "mp", H_SWAP)
    own_pieces = [extended] + [lax.ppermute(extended, "mp", x_shift(d)) for d in (1, 2, 3)]
    crossed, *filters = tied(crossed, *filters)
    toep_li, leave, enter, lane_rates = filters
    far_pieces = [crossed] + [lax.ppermute(crossed, "mp", x_shift(d)) for d in (1, 2, 3)]
    pieces = packed(own_pieces + far_pieces)
    fresh_q, product, load = project(where, pieces, weights, featurizer_li, enter)
    other_load = lax.ppermute(load, "ctx", CORE_SWAP)
    chip = chip_state(where, load, other_load, lane_rates)
    before = [lax.ppermute(chip, "ctx", z_shift(s)) for s in (1, 2, 3)]
    conv = li_inner(product, toep_li)
    *before, conv = tied(*before, conv)
    line_total, line_carry = line_state(where, [chip] + before, lane_rates)
    above = [lax.ppermute(line_total, "ctx", y_shift(s)) for s in (1, 2, 3)]
    gated_two, *other_two = li_outer(
        where, conv, fresh_q, featurizer_li, leave, lane_rates,
        line_carry, other_load, above, out_li,
    )
    return sum_shares(where, gated_two, other_two, out_li, hidden)


def solution(mesh):
    return jax.shard_map(
        body,
        mesh=mesh,
        in_specs=(
            P("ctx", "mp"),
            P("ctx", "mp"),
            P("ctx", "mp"),
            P(None, None, "mp"),
            P(None, "mp"),
            P("mp", None),
            P("ctx", "mp"),
            P(None, "mp", "ctx"),
            P(None, None, "mp"),
            P("mp", None),
            P("mp", None),
            P("mp", None),
        ),
        out_specs=P("ctx", "mp"),
        check_vma=False,
    )
```
